32 devices in a mesh: wide: 8 (over y, x, core), narrow: 4 (over z).
Axes of the slice: x: 2, y: 2, z: 4, core: 2. Of those that a mesh axis runs over, the one named last changes fastest.
Arguments:
- tokens: bfloat16 [10240, 1120], P(('wide', 'narrow')), may hold values from -6 to 6
- lengths: int32 [32], P(('wide', 'narrow')), may hold values from 1 to 320
- norm1_gain: bfloat16 [1120], P('narrow'), may hold values from 0.099609375 to 1.8984375
- norm1_bias: bfloat16 [1120], P('narrow'), may hold values from -3 to 3
- qkv_weight: bfloat16 [1120, 3360], P('narrow'), may hold values from -0.1875 to 0.1875
- query_bias: bfloat16 [1120], P('narrow'), may hold values from -3 to 3
- value_bias: bfloat16 [1120], P('narrow'), may hold values from -3 to 3
- out_weight: bfloat16 [1120, 1120], P('narrow'), may hold values from -1.5 to 1.5
- out_bias: bfloat16 [1120], P('narrow'), may hold values from -3 to 3
- norm2_gain: bfloat16 [1120], P('narrow'), may hold values from 0.099609375 to 1.8984375
- norm2_bias: bfloat16 [1120], P('narrow'), may hold values from -3 to 3
- up_weight: bfloat16 [1120, 4480], P('narrow'), may hold values from -0.1875 to 0.1875
- up_bias: bfloat16 [4480], P('narrow'), may hold values from -3 to 3
- down_weight: bfloat16 [4480, 1120], P('narrow'), may hold values from -0.09375 to 0.09375
- down_bias: bfloat16 [1120], P('narrow'), may hold values from -3 to 3
- cotangent: bfloat16 [10240, 1120], P(('wide', 'narrow')), may hold values from -6 to 6
Outputs:
- block_out: bfloat16 [10240, 1120], P(('wide', 'narrow'))
- input_grad: float32 [10240, 1120], P(('wide', 'narrow'))
- norm1_gain_grad: float32 [1120], P('narrow')
- norm1_bias_grad: float32 [1120], P('narrow')
- qkv_weight_grad: float32 [1120, 3360], P('narrow', 'wide')
- query_bias_grad: float32 [1120], P('narrow')
- value_bias_grad: float32 [1120], P('narrow')
- out_weight_grad: float32 [1120, 1120], P('narrow', 'wide')
- out_bias_grad: float32 [1120], P('narrow')
- norm2_gain_grad: float32 [1120], P('narrow')
- norm2_bias_grad: float32 [1120], P('narrow')
- up_weight_grad: float32 [1120, 4480], P('narrow', 'wide')
- up_bias_grad: float32 [4480], P('narrow')
- down_weight_grad: float32 [4480, 1120], P('narrow', 'wide')
- down_bias_grad: float32 [1120], P('narrow')
The draws below stay inside these ranges and needn't reach their ends.
All inputs are finite; a program needn't handle non-finite values.
Results may differ from the reference program's by a relative error of at most 0.012.
Values may be sent and summed in bfloat16 or wider, within the bound.
No kernel may reach another device: no remote copies, remote signals or barrier semaphores. Data moves between devices by JAX's collectives and lax.ppermute only.
A program may use at most 256 MiB of HBM per device.

```python
import jax
import jax.numpy as jnp
from jax import lax

D = 1120
HEADS = 20
HEAD = 56
FF = 4480
LEN = 320
CELLS = 32
TOKENS = 10240


def set_ends(entries, stream_key, least, largest):
    longest = entries.shape.index(max(entries.shape))
    spots = []
    for shift in (0, 1):
        where = [jax.random.randint(jax.random.fold_in(stream_key, axis), (), 0, length) for axis, length in enumerate(entries.shape)]
        where[longest] = (where[longest] + shift) % entries.shape[longest]
        spots.append(tuple(where))
    return entries.at[spots[0]].set(least).at[spots[1]].set(largest)


def steps_of(own_key, extent, pieces, low, high):
    def one(axis_at, shards_of):
        heights = jax.random.uniform(jax.random.fold_in(jax.random.fold_in(own_key, 6), axis_at), (shards_of,), jnp.float32, low / len(pieces), high / len(pieces))
        return jnp.repeat(jnp.exp(heights), extent[axis_at] // shards_of).reshape((-1,) + (1,) * (len(extent) - axis_at - 1))

    loudness = one(*pieces[0])
    for cut in pieces[1:]:
        loudness = loudness * one(*cut)
    return loudness


def bell_draw(rng, extent, scale, limit, split=(), dtype=jnp.bfloat16):
    values = jax.random.normal(rng, extent, jnp.float32) * scale
    if len(split) > 0:
        values = steps_of(rng, extent, split, -0.22, 0.18) * values
    return jnp.clip(values, min=-limit, max=limit).astype(dtype)


def setup_inputs(seed: int = 0) -> dict:
    arg_keys = jax.random.split(jax.random.key(seed), 17)
    tokens = bell_draw(arg_keys[0], (TOKENS, D), 1.0, 6.0, ((0, 32),))
    lengths = set_ends(jax.random.randint(arg_keys[1], (CELLS,), 1, LEN + 1), jax.random.fold_in(arg_keys[1], 1), 1, LEN).astype(jnp.int32)
    norm1_gain = jnp.clip(1.0 + 0.18 * jax.random.normal(arg_keys[2], (D,), jnp.float32), 0.099609375, 1.8984375).astype(jnp.bfloat16)
    norm1_bias = bell_draw(arg_keys[3], (D,), 0.5, 3.0, ((0, 4),))
    qkv_weight = bell_draw(arg_keys[4], (D, 3 * D), D ** -0.5, 0.1875, ((0, 4),))
    query_bias = bell_draw(arg_keys[5], (D,), 0.5, 3.0, ((0, 4),))
    value_bias = bell_draw(arg_keys[6], (D,), 0.5, 3.0, ((0, 4),))
    out_weight = bell_draw(arg_keys[7], (D, D), (D // 64) ** -0.5, 1.5, ((0, 4),))
    out_bias = bell_draw(arg_keys[8], (D,), 0.5, 3.0, ((0, 4),))
    norm2_gain = jnp.clip(1.0 + 0.18 * jax.random.normal(arg_keys[9], (D,), jnp.float32), 0.099609375, 1.8984375).astype(jnp.bfloat16)
    norm2_bias = bell_draw(arg_keys[10], (D,), 0.5, 3.0, ((0, 4),))
    up_weight = bell_draw(arg_keys[11], (D, FF), D ** -0.5, 0.1875, ((0, 4),))
    up_bias = bell_draw(arg_keys[12], (FF,), 0.5, 3.0, ((0, 4),))
    down_weight = bell_draw(arg_keys[13], (FF, D), FF ** -0.5, 0.09375, ((0, 4),))
    down_bias = bell_draw(arg_keys[14], (D,), 0.5, 3.0, ((0, 4),))
    cotangent = bell_draw(arg_keys[15], (TOKENS, D), 1.0, 6.0, ((0, 32),))
    return {"tokens": tokens, "lengths": lengths, "norm1_gain": norm1_gain, "norm1_bias": norm1_bias, "qkv_weight": qkv_weight, "query_bias": query_bias, "value_bias": value_bias, "out_weight": out_weight, "out_bias": out_bias, "norm2_gain": norm2_gain, "norm2_bias": norm2_bias, "up_weight": up_weight, "up_bias": up_bias, "down_weight": down_weight, "down_bias": down_bias, "cotangent": cotangent}


EPSILON = 1e-05
FILL = -1000000000.0

@jax.custom_vjp
def low(v):
    return lax.optimization_barrier(v.astype(jnp.bfloat16)).astype(jnp.float32)

@jax.custom_vjp
def low_back(v):
    return v

def low_keep(v):
    return (low(v), None)

def low_pass(kept, grad):
    return (grad,)

def back_keep(v):
    return (v, None)

def back_low(kept, grad):
    return (low(grad),)
low.defvjp(low_keep, low_pass)
low_back.defvjp(back_keep, back_low)

def wide_product(first, second):
    return jnp.dot(first, second, precision=lax.Precision.HIGHEST)

def layer_norm(values, gain, shift):
    center = values - lax.optimization_barrier(jnp.mean(values, axis=-1, keepdims=True))
    spread = lax.optimization_barrier(jnp.mean(center * center, axis=-1, keepdims=True))
    return center * lax.rsqrt(spread + EPSILON) * gain + shift

def cell_forward(params, inputs, length):
    gain_one, shift_one, qkv_full, query_shift, value_shift, out_full, out_shift, gain_two, shift_two, up_full, up_shift, down_full, down_shift = params
    positions = jnp.arange(LEN)
    normed_one = low(layer_norm(inputs, gain_one, shift_one))
    joined = wide_product(normed_one, qkv_full)
    queries = low_back(low(joined[:, :D] + query_shift)).reshape(LEN, HEADS, HEAD)
    keys_all = low_back(low(joined[:, D:2 * D])).reshape(LEN, HEADS, HEAD)
    values_all = low_back(low(joined[:, 2 * D:] + value_shift)).reshape(LEN, HEADS, HEAD)
    scores = jnp.einsum('qhd,khd->hqk', queries, keys_all, precision=lax.Precision.HIGHEST) * HEAD ** (-0.5)
    allowed = (positions[None, :] <= positions[:, None]) & (positions[None, :] < length)
    scores = low_back(jnp.where(allowed[None], scores, FILL))
    attn_probs = low(jax.nn.softmax(scores, axis=-1))
    context = jnp.einsum('hqk,khd->qhd', attn_probs, values_all, precision=lax.Precision.HIGHEST).reshape(LEN, D)
    context = low_back(low(context))
    attended = low_back(wide_product(context, out_full) + out_shift)
    middle = inputs + attended
    normed_two = low(layer_norm(middle, gain_two, shift_two))
    hidden_pre = low_back(wide_product(normed_two, up_full) + up_shift)
    activated = low(jax.nn.gelu(hidden_pre, approximate=True))
    mlp_out = low_back(wide_product(activated, down_full) + down_shift)
    keep_rows = (positions < length).astype(jnp.float32)[:, None]
    return keep_rows * (middle + mlp_out)

def reference(tokens, lengths, norm1_gain, norm1_bias, qkv_weight, query_bias, value_bias, out_weight, out_bias, norm2_gain, norm2_bias, up_weight, up_bias, down_weight, down_bias, cotangent):
    params = (norm1_gain.astype(jnp.float32), norm1_bias.astype(jnp.float32), qkv_weight.astype(jnp.float32), query_bias.astype(jnp.float32), value_bias.astype(jnp.float32), out_weight.astype(jnp.float32), out_bias.astype(jnp.float32), norm2_gain.astype(jnp.float32), norm2_bias.astype(jnp.float32), up_weight.astype(jnp.float32), up_bias.astype(jnp.float32), down_weight.astype(jnp.float32), down_bias.astype(jnp.float32))
    inputs = tokens.astype(jnp.float32).reshape(CELLS, LEN, D)
    upstream = cotangent.astype(jnp.float32).reshape(CELLS, LEN, D)
    starting = tuple((jnp.zeros_like(element) for element in params))

    def one_cell(running, element):
        cell_in, length, cell_grad = element
        result, pull = jax.vjp(lambda weights, values: cell_forward(weights, values, length), params, cell_in)
        param_grads, input_part = pull(cell_grad)
        running = tuple((summed + addend for summed, addend in zip(running, param_grads)))
        return (running, (result, input_part))
    totals, (results, input_parts) = lax.scan(one_cell, starting, (inputs, lengths, upstream))
    return (results.reshape(TOKENS, D).astype(jnp.bfloat16), input_parts.reshape(TOKENS, D), totals[0], totals[1], totals[2], totals[3], totals[4], totals[5], totals[6], totals[7], totals[8], totals[9], totals[10], totals[11], totals[12])
```

```python
import jax
import jax.numpy as jnp
from jax import lax
from jax.sharding import Mesh, PartitionSpec as P

HEADS = 20
EPSILON = 1e-05
FILL = -1000000000.0
BF = jnp.bfloat16
F32 = jnp.float32
AXES = ("o", "y", "x", "c", "z")
WIDE = ("o", "y", "x", "c")
SWAP = [(0, 1), (1, 0)]
GROUP = 4


def swap(value, axis):
    return lax.ppermute(value, axis, SWAP)


def dot(first, second):
    return jnp.dot(first, second, preferred_element_type=F32)


def dot_left(first, second):
    return lax.dot_general(first, second, (((0,), (0,)), ((), ())), preferred_element_type=F32)


def dot_right(first, second):
    return lax.dot_general(first, second, (((1,), (1,)), ((), ())), preferred_element_type=F32)


def pick(blocks, index):
    return lax.dynamic_index_in_dim(blocks, index, 0, keepdims=False)


def choose(flag, first, second):
    return jnp.where(flag == 0, first, second)


def group_gather(value):
    over_core = swap(value, "c")
    over_x = swap(value, "x")
    return [value, over_core, over_x, swap(over_x, "c")]


def group_scatter(parts):
    sent = swap(jnp.stack([parts[1], parts[3]]).astype(BF), "c")
    ours = parts[0] + sent[0].astype(F32)
    theirs = (parts[2] + sent[1].astype(F32)).astype(BF)
    return ours + swap(theirs, "x").astype(F32)


def group_exchange(parts):
    far = swap(jnp.stack([parts[2], parts[3]]), "x")
    near = swap(jnp.stack([parts[1], far[1]]), "c")
    return [parts[0], near[0], far[0], near[1]]


def depth_shift(value, shift, count):
    return lax.ppermute(value, "z", [(i, (i + shift) % count) for i in range(count)])


def depth_place(blocks, here, count):
    return jnp.stack([pick(blocks, (here - z) % count) for z in range(count)])


def depth_scatter(parts, here, count):
    total = pick(parts, here).astype(F32)
    for shift in range(1, count):
        total = total + depth_shift(pick(parts, (here + shift) % count), shift, count).astype(F32)
    return total


def normal(values):
    center = values - jnp.mean(values, axis=-1, keepdims=True)
    spread = jnp.mean(center * center, axis=-1, keepdims=True)
    inverse = lax.rsqrt(spread + EPSILON)
    return center * inverse, inverse


def normal_back(grad, unit, inverse):
    return (
        grad
        - jnp.mean(grad, axis=-1, keepdims=True)
        - unit * jnp.mean(grad * unit, axis=-1, keepdims=True)
    ) * inverse


def gelu_tanh(values):
    return jax.nn.gelu(values, approximate=True)


def build(outer, depth):
    def shards(
        tokens, lengths, norm1_gain, norm1_bias, qkv_weight, query_bias, value_bias, out_weight,
        out_bias, norm2_gain, norm2_bias, up_weight, up_bias, down_weight, down_bias, cotangent,
    ):
        rows, width = tokens.shape
        cells = lengths.shape[0]
        slots = rows // cells
        hidden = up_weight.shape[1]
        heads = HEADS // GROUP
        head = width // HEADS
        part = width // GROUP
        part_depth = width // depth
        hidden_depth = hidden // depth
        block = hidden_depth // GROUP
        mine = depth * block
        wide = outer * 2 * GROUP
        scale = head ** (-0.5)
        y, x, c, z = (lax.axis_index(name) for name in ("y", "x", "c", "z"))
        member = 2 * x + c
        row = outer * 2

        vectors = jnp.concatenate(
            [norm1_gain, norm1_bias, query_bias, value_bias, out_bias, norm2_gain, norm2_bias, down_bias, up_bias]
        ).reshape(12, part_depth)
        vectors = depth_place(
            jnp.stack([vectors] + [depth_shift(vectors, r, depth) for r in range(1, depth)]), z, depth
        ).astype(F32)
        whole = jnp.transpose(vectors[:, :8], (1, 0, 2)).reshape(8, width)
        gain_one, shift_one, query_shift, value_shift, out_shift, gain_two, shift_two, down_shift = whole
        query_shift = pick(query_shift.reshape(GROUP, part), member)
        value_shift = pick(value_shift.reshape(GROUP, part), member)
        up_shift = lax.dynamic_slice_in_dim(
            vectors[:, 8:].reshape(depth, hidden_depth), member * block, block, 1
        ).reshape(mine)

        half = (part_depth // 2 + 7) // 8 * 8
        start = part_depth - half
        qkv_own = lax.dynamic_slice_in_dim(
            qkv_weight.reshape(part_depth, 3, width), member * part, part, 2
        ).reshape(part_depth, 3 * part)
        qkv_half = choose(y, qkv_own[:half], qkv_own[start:])
        near = jnp.stack([depth_shift(qkv_half, r, depth) for r in range(1, depth)])
        far = swap(near, "y")
        qkv_rest = jnp.concatenate(
            [choose(y, near, far), choose(y, far, near)[:, 2 * half - part_depth :]], axis=1
        )
        qkv_full = depth_place(jnp.concatenate([qkv_own[None], qkv_rest]), z, depth).reshape(width, 3 * part)

        inputs = tokens.astype(F32)
        unit_one, inverse_one = normal(inputs)
        normed_one = (unit_one * gain_one + shift_one).astype(BF)
        normed_one_all = jnp.concatenate(group_gather(normed_one))
        lengths_all = jnp.concatenate(group_gather(lengths))

        up_own = lax.dynamic_slice_in_dim(
            up_weight.reshape(part_depth, depth, hidden_depth), member * block, block, 2
        ).reshape(part_depth, mine)
        down_own = lax.dynamic_slice_in_dim(down_weight, member * block, block, 0)

        pieces = 2 * GROUP
        height = (part_depth // pieces + 7) // 8 * 8
        starts = [(p * (part_depth - height) // (pieces - 1)) // 8 * 8 for p in range(pieces - 1)] + [part_depth - height]
        ends = starts[1:] + [part_depth]
        place = 4 * y + member
        out_piece = lax.dynamic_slice_in_dim(out_weight, jnp.array(starts)[place], height, 0)
        got = jnp.stack([depth_shift(out_piece, r, depth) for r in range(1, depth)])[:, None]
        for axis, flag in (("c", c), ("x", x), ("y", y)):
            other = swap(got, axis)
            got = jnp.concatenate([choose(flag, got, other), choose(flag, other, got)], axis=1)
        out_rest = jnp.concatenate([got[:, p, : ends[p] - starts[p]] for p in range(pieces)], axis=1)
        out_full = depth_place(jnp.concatenate([out_weight[None], out_rest]), z, depth).reshape(width, width)

        turn = choose(y, up_own, down_own) if part_depth == block and mine == width else None
        if turn is None:
            up_rest = jnp.stack([depth_shift(up_own, r, depth) for r in range(1, depth)])
            down_rest = jnp.stack([depth_shift(down_own, r, depth) for r in range(1, depth)])
        else:
            near = jnp.stack([depth_shift(turn, r, depth) for r in range(1, depth)])
            far = swap(near, "y")
            up_rest, down_rest = choose(y, near, far), choose(y, far, near)
        up_full = depth_place(jnp.concatenate([up_own[None], up_rest]), z, depth).reshape(width, mine)
        down_full = depth_place(jnp.concatenate([down_own[None], down_rest]), z, depth).reshape(mine, width)

        positions = jnp.arange(slots)
        keep = (positions[None, :] < lengths[:, None]).astype(F32).reshape(rows, 1)
        grad_rows = cotangent.astype(F32) * keep
        grad_all = jnp.concatenate(group_gather(grad_rows.astype(BF)))

        joined = dot(normed_one_all, qkv_full)
        shape = (GROUP * cells, slots, heads, head)
        queries = (joined[:, :part] + query_shift).astype(BF).reshape(shape)
        keys = joined[:, part : 2 * part].astype(BF).reshape(shape)
        values = (joined[:, 2 * part :] + value_shift).astype(BF).reshape(shape)
        allowed = (positions[None, None, :] <= positions[None, :, None]) & (
            positions[None, None, :] < lengths_all[:, None, None]
        )
        scores = jnp.einsum("cqhd,ckhd->chqk", queries, keys, preferred_element_type=F32) * scale
        probs = jax.nn.softmax(jnp.where(allowed[:, None], scores, FILL), axis=-1)
        probs_low = probs.astype(BF)
        context = jnp.einsum("chqk,ckhd->cqhd", probs_low, values, preferred_element_type=F32)
        context = context.astype(BF).reshape(GROUP, rows, part)
        context = jnp.stack(group_exchange([context[k] for k in range(GROUP)]))
        context = jnp.concatenate([pick(context, member ^ k) for k in range(GROUP)], axis=1)

        middle = inputs + (dot(context, out_full) + out_shift)
        unit_two, inverse_two = normal(middle)
        normed_two = (unit_two * gain_two + shift_two).astype(BF)
        normed_two_all = jnp.concatenate(group_gather(normed_two))

        pre = dot(normed_two_all, up_full) + up_shift
        activated, gelu_pull = jax.vjp(gelu_tanh, pre)
        activated = activated.astype(BF)
        pre_grad = gelu_pull(dot_right(grad_all, down_full))[0].astype(BF)
        two_parts = dot_right(pre_grad, up_full).reshape(GROUP, rows, width)
        two_grad = group_scatter([two_parts[k] for k in range(GROUP)])
        mlp_parts = dot(activated, down_full).reshape(GROUP, rows, width)
        mlp_out = group_scatter([mlp_parts[k] for k in range(GROUP)]) + down_shift
        block_out = (keep * (middle + mlp_out)).astype(BF)

        middle_grad = grad_rows + normal_back(two_grad * gain_two, unit_two, inverse_two)
        middle_low = middle_grad.astype(BF)
        context_grad = dot_right(middle_low, out_full).astype(BF)
        context_grad = jnp.transpose(context_grad.reshape(rows, GROUP, part), (1, 0, 2))
        context_grad = group_exchange([pick(context_grad, member ^ k) for k in range(GROUP)])
        context_grad = jnp.stack(context_grad).reshape(shape)

        probs_grad = jnp.einsum("cqhd,ckhd->chqk", context_grad, values, preferred_element_type=F32)
        value_grad = jnp.einsum("chqk,cqhd->ckhd", probs_low, context_grad, preferred_element_type=F32)
        score_grad = probs * (probs_grad - jnp.sum(probs * probs_grad, axis=-1, keepdims=True))
        score_grad = score_grad.astype(BF)
        query_grad = jnp.einsum("chqk,ckhd->cqhd", score_grad, keys, preferred_element_type=F32) * scale
        key_grad = jnp.einsum("chqk,cqhd->ckhd", score_grad, queries, preferred_element_type=F32) * scale
        total = GROUP * rows
        joined_grad = jnp.concatenate(
            [query_grad.reshape(total, part), key_grad.reshape(total, part), value_grad.reshape(total, part)], axis=1
        ).astype(BF)
        one_parts = dot_right(joined_grad, qkv_full).reshape(GROUP, rows, width)
        one_grad = group_scatter([one_parts[k] for k in range(GROUP)])
        input_grad = middle_grad + normal_back(one_grad * gain_one, unit_one, inverse_one)

        each = mine // row
        side = width // row

        def columns(array, count, index):
            array = array.reshape(array.shape[0], outer, 2, count)
            return lax.dynamic_index_in_dim(array, index, 2, keepdims=False).reshape(array.shape[0], outer * count)

        def both(left, right, count):
            sent = swap(dot_left(left, columns(right, count, 1 - y)).astype(BF), "y")
            return (dot_left(left, columns(right, count, y)) + sent.astype(F32)).astype(BF)

        def over_outer(piece, count):
            piece = piece.reshape(piece.shape[0], outer, count)
            if outer == 1:
                return piece[:, 0]
            return lax.psum_scatter(piece, "o", scatter_dimension=1, tiled=False)

        down_piece = over_outer(
            depth_scatter(both(activated, grad_all, side).reshape(depth, block, outer * side), z, depth), side
        ).astype(BF)
        up_piece = over_outer(
            depth_scatter(both(normed_two_all, pre_grad, each).reshape(depth, part_depth, outer * each), z, depth), each
        ).astype(BF)
        down_all = jnp.stack(group_gather(down_piece))
        up_all = jnp.stack(group_gather(up_piece))
        down_all = jnp.stack([pick(down_all, member ^ k) for k in range(GROUP)])
        down_weight_grad = lax.dynamic_index_in_dim(
            down_all.reshape(hidden_depth, GROUP, side // GROUP), member, 1, keepdims=False
        ).astype(F32)
        up_all = up_all.reshape(GROUP, part_depth, each // block, block)
        ratio = wide // depth
        fold = GROUP // ratio
        up_pieces = []
        for k in range(fold):
            source = (member % ratio) * fold + k if fold > 1 else member
            chunk = pick(up_all, member ^ source)
            up_pieces.append(lax.dynamic_index_in_dim(chunk, member // ratio, 1, keepdims=False))
        up_weight_grad = jnp.concatenate(up_pieces, axis=1).astype(F32)

        out_parts = dot_left(middle_low, context).astype(BF).reshape(outer, 2, 2, 2, width // wide, width)
        for axis, flag in ((3, c), (2, x), (1, y)):
            sent = swap(lax.dynamic_index_in_dim(out_parts, 1 - flag, axis, keepdims=False), AXES[axis])
            out_parts = lax.dynamic_index_in_dim(out_parts, flag, axis, keepdims=False).astype(F32) + sent.astype(F32)
            out_parts = out_parts.astype(BF)
        out_parts = jnp.transpose(out_parts.reshape(outer, width // wide, depth, part_depth), (2, 0, 1, 3))
        out_piece = depth_scatter(out_parts, z, depth)
        out_piece = out_piece[0] if outer == 1 else lax.psum_scatter(out_piece, "o", scatter_dimension=0, tiled=False)
        out_weight_grad = out_piece.T

        qkv_parts = dot_left(normed_one_all, joined_grad).reshape(depth, part_depth, 3 * part)
        top, bottom = qkv_parts[:, :half], qkv_parts[:, start:]
        sent = swap(choose(y, bottom, top).astype(BF), "y")
        qkv_parts = (choose(y, top, bottom) + sent.astype(F32)).astype(BF)
        qkv_piece = depth_scatter(qkv_parts, z, depth).astype(BF)
        qkv_all = jnp.stack(group_gather(qkv_piece))
        qkv_all = jnp.stack([pick(qkv_all, member ^ k) for k in range(GROUP)]).reshape(GROUP, half, 3, part)
        qkv_all = jnp.transpose(qkv_all, (1, 2, 0, 3)).reshape(half, outer, 2, GROUP, 3 * width // wide)
        qkv_all = lax.dynamic_index_in_dim(qkv_all, member, 3, keepdims=False)
        if outer > 1:
            qkv_all = lax.psum_scatter(qkv_all, "o", scatter_dimension=1, tiled=True)
        qkv_all = qkv_all[:, 0]
        sent = swap(lax.dynamic_index_in_dim(qkv_all, 1 - y, 1, keepdims=False), "y")
        kept = lax.dynamic_index_in_dim(qkv_all, y, 1, keepdims=False)
        qkv_weight_grad = jnp.concatenate(
            [choose(y, kept, sent), choose(y, sent, kept)[2 * half - part_depth :]]
        ).astype(F32)

        def spread_out(vector):
            zero = jnp.zeros((GROUP,) + vector.shape, F32)
            return lax.dynamic_update_index_in_dim(zero, vector, member, 0)

        joined_sums = jnp.sum(joined_grad.astype(F32), axis=0)
        sums = [
            jnp.sum(one_grad * unit_one, axis=0),
            jnp.sum(one_grad, axis=0),
            spread_out(joined_sums[:part]).reshape(width),
            spread_out(joined_sums[2 * part :]).reshape(width),
            jnp.sum(middle_low.astype(F32), axis=0),
            jnp.sum(two_grad * unit_two, axis=0),
            jnp.sum(two_grad, axis=0),
            jnp.sum(grad_rows, axis=0),
        ]
        up_sums = spread_out(jnp.sum(pre_grad.astype(F32), axis=0).reshape(depth, block))
        up_sums = jnp.transpose(up_sums, (1, 0, 2)).reshape(depth, hidden_depth)
        packed = jnp.concatenate([total_of.reshape(depth, part_depth) for total_of in sums] + [up_sums], axis=1)
        packed = depth_scatter(packed, z, depth)
        for axis in ("c", "x", "y"):
            packed = packed + swap(packed, axis)
        if outer > 1:
            packed = lax.psum(packed, "o")
        vector = [packed[k * part_depth : (k + 1) * part_depth] for k in range(8)]
        return (
            block_out, input_grad, vector[0], vector[1], qkv_weight_grad, vector[2], vector[3], out_weight_grad,
            vector[4], vector[5], vector[6], up_weight_grad, packed[8 * part_depth :], down_weight_grad, vector[7],
        )

    return shards


def solution(mesh):
    wide, depth = mesh.shape["wide"], mesh.shape["narrow"]
    outer = wide // 8
    fine = Mesh(mesh.devices.reshape(outer, 2, 2, 2, depth), AXES)
    rows, vec, mat = P(AXES, None), P("z"), P("z", None)
    placed = (
        rows, P(AXES), vec, vec, mat, vec, vec, mat, vec, vec, vec, mat, vec, mat, vec, rows,
    )
    grad = P("z", WIDE)
    return jax.shard_map(
        build(outer, depth),
        mesh=fine,
        in_specs=placed,
        out_specs=(rows, rows, vec, vec, grad, vec, vec, grad, vec, vec, vec, grad, vec, grad, vec),
        check_vma=False,
    )
```

```python
import functools

import jax
import jax.numpy as jnp
from jax import lax
from jax.experimental import pallas as pl
from jax.experimental.pallas import tpu as pltpu
from jax.sharding import Mesh, PartitionSpec as P

HEADS = 20
EPSILON = 1e-05
FILL = -1000000000.0
BF = jnp.bfloat16
F32 = jnp.float32
AXES = ("o", "y", "x", "c", "z")
WIDE = ("o", "y", "x", "c")
SWAP = [(0, 1), (1, 0)]
GROUP = 4
MIB = 1024 * 1024


def swap(value, axis):
    return lax.ppermute(value, axis, SWAP)


def dot(first, second):
    return jnp.dot(first, second, preferred_element_type=F32)


def dot_left(first, second):
    return lax.dot_general(first, second, (((0,), (0,)), ((), ())), preferred_element_type=F32)


def dot_right(first, second):
    return lax.dot_general(first, second, (((1,), (1,)), ((), ())), preferred_element_type=F32)


def shape_of(dims, dtype):
    return jax.ShapeDtypeStruct(dims, dtype)


class Order:
    def __init__(self):
        self.token = None

    def __call__(self, body, outs, scalars, arrays, after=(), scratch=(), flops=0, mib=28, name=None):
        after = list(after) + ([] if self.token is None else [self.token])
        n_scalar, n_array, n_out = len(scalars), len(arrays), len(outs)

        def run(*refs):
            token = refs[n_scalar + n_array + len(after) + n_out]
            values = tuple(ref[0] for ref in refs[:n_scalar])
            rest = refs[n_scalar + n_array + len(after) :]
            token[...] = jnp.zeros(token.shape, F32)
            body(values, *refs[n_scalar : n_scalar + n_array], *rest[:n_out], *rest[n_out + 1 :])

        moved = sum(a.size * a.dtype.itemsize for a in arrays) + sum(a.size * a.dtype.itemsize for a in outs)
        *given, self.token = pl.pallas_call(
            run,
            out_shape=(*outs, shape_of((8, 128), F32)),
            in_specs=[pl.BlockSpec(memory_space=pltpu.SMEM)] * n_scalar
            + [pl.BlockSpec(memory_space=pltpu.VMEM)] * n_array
            + [pl.BlockSpec(memory_space=pl.ANY)] * len(after),
            out_specs=(pl.BlockSpec(memory_space=pltpu.VMEM),) * (n_out + 1),
            scratch_shapes=list(scratch),
            compiler_params=pltpu.CompilerParams(vmem_limit_bytes=mib * MIB),
            cost_estimate=pl.CostEstimate(flops=int(flops), bytes_accessed=int(moved), transcendentals=0),
            name=name,
        )(*scalars, *arrays, *after)
        return given


def group_gather(value):
    over_x = swap(value, "x")
    over_core = swap(value, "c")
    return [value, over_core, over_x, swap(over_x, "c")]


def depth_shift(value, shift, count):
    return lax.ppermute(value, "z", [(i, (i + shift) % count) for i in range(count)])


def depth_exchange(parts):
    return lax.all_to_all(parts, "z", 0, 0)


def depth_line(value, count):
    up, down = [], []
    for s in range(count - 1):
        up.append(lax.ppermute(up[-1] if s else value, "z", [(i, i + 1) for i in range(s, count - 1)]))
        down.append(lax.ppermute(down[-1] if s else value, "z", [(i, i - 1) for i in range(1, count - s)]))
    return up, down


def normal(values):
    center = values - jnp.mean(values, axis=-1, keepdims=True)
    spread = jnp.mean(center * center, axis=-1, keepdims=True)
    inverse = lax.rsqrt(spread + EPSILON)
    return center * inverse, inverse


def normal_back(grad, unit, inverse):
    return (
        grad
        - jnp.mean(grad, axis=-1, keepdims=True)
        - unit * jnp.mean(grad * unit, axis=-1, keepdims=True)
    ) * inverse


def when_each(index, count, step):
    for k in range(count):
        pl.when(index == k)(functools.partial(step, k))


def next_block(z, step, count):
    return z + 1 + step if step < count - 1 - z else count - 2 - step


def line_ref(z, other, up, down):
    return up[z - 1 - other] if other < z else down[other - z - 1]


def allowed_of(rows, length):
    query = lax.broadcasted_iota(jnp.int32, (rows, rows), 0)
    key = lax.broadcasted_iota(jnp.int32, (rows, rows), 1)
    return (key <= query) & (key < length)


def head_probs(query, key, allowed, scale):
    scores = jnp.where(allowed, dot_right(query, key) * scale, FILL)
    weights = jnp.exp(scores - jnp.max(scores, axis=1, keepdims=True))
    return weights * (1.0 / jnp.sum(weights, axis=1, keepdims=True))


def attend(heads, lengths, normed, full, query_shift, value_shift, joined, contexts):
    rows, part = normed[0].shape[0], full.shape[1] // 3
    head = part // heads
    scale = head ** (-0.5)
    for n, x in enumerate(normed):
        sums = dot(x[...], full[...])
        query = (sums[:, :part] + query_shift[...]).astype(BF)
        key = sums[:, part : 2 * part].astype(BF)
        value = (sums[:, 2 * part :] + value_shift[...]).astype(BF)
        joined[n, :, :part] = query
        joined[n, :, part : 2 * part] = key
        joined[n, :, 2 * part :] = value
        allowed = allowed_of(rows, lengths[n])
        out = []
        for h in range(heads):
            cut = slice(h * head, (h + 1) * head)
            probs = head_probs(query[:, cut], key[:, cut], allowed, scale).astype(BF)
            out.append(dot(probs, value[:, cut]))
        contexts[n][...] = jnp.concatenate(out, axis=1).astype(BF)


def attend_back(heads, lengths, joined, grad, out):
    rows, part = joined.shape[1], joined.shape[2] // 3
    head = part // heads
    scale = head ** (-0.5)
    for n in range(joined.shape[0]):
        query, key, value = (joined[n, :, p * part : (p + 1) * part] for p in range(3))
        above = grad[n][...]
        allowed = allowed_of(rows, lengths[n])
        found = ([], [], [])
        for h in range(heads):
            cut = slice(h * head, (h + 1) * head)
            q, k, v, g = query[:, cut], key[:, cut], value[:, cut], above[:, cut]
            probs = head_probs(q, k, allowed, scale)
            probs_grad = dot_right(g, v)
            found[2].append(dot_left(probs.astype(BF), g))
            score = probs * (probs_grad - jnp.sum(probs * probs_grad, axis=1, keepdims=True))
            score = score.astype(BF)
            found[0].append(dot(score, k) * scale)
            found[1].append(dot_left(score, q) * scale)
        out[n] = jnp.concatenate(found[0] + found[1] + found[2], axis=1).astype(BF)


def gelu_both(values):
    root = (2.0 / jnp.pi) ** 0.5
    square = values * values
    bend = jnp.tanh(root * (values + 0.044715 * (square * values)))
    half = 0.5 * (1.0 + bend)
    slope = half + 0.5 * values * (1.0 - bend * bend) * (root * (1.0 + 3.0 * 0.044715 * square))
    return values * half, slope


def column_sum(values):
    return jnp.sum(values, axis=0, keepdims=True)


def build(outer, depth):
    def shards(
        tokens, lengths, norm1_gain, norm1_bias, qkv_weight, query_bias, value_bias, out_weight,
        out_bias, norm2_gain, norm2_bias, up_weight, up_bias, down_weight, down_bias, cotangent,
    ):
        rows, width = tokens.shape
        heads = HEADS // GROUP
        part = width // GROUP
        part_depth = width // depth
        hidden_depth = up_weight.shape[1] // depth
        block = hidden_depth // GROUP
        mine = depth * block
        wide = outer * 2 * GROUP
        sides = outer * 2
        y, x, c, z = (lax.axis_index(name).astype(jnp.int32).reshape(1) for name in ("y", "x", "c", "z"))
        member = 2 * x + c
        others = range(1, depth)
        step = Order()

        row_low, row_full = shape_of((rows, width), BF), shape_of((rows, width), F32)
        row_pair = shape_of((2, rows, width), BF)
        row_sum = shape_of((1, width), F32)
        cell, pair = shape_of((rows, part), BF), shape_of((2, rows, part), BF)

        half = (part_depth // 2 + 15) // 16 * 16
        rest = part_depth - half
        half_shape = shape_of((half, 3 * part), BF)

        def take_qkv(s, weight, own, send):
            def columns(k):
                for p in range(3):
                    at = (p * GROUP + k) * part
                    own[:, p * part : (p + 1) * part] = weight[:, at : at + part]

            when_each(s[0], GROUP, columns)

            @pl.when(s[1] == 0)
            def _():
                send[...] = own[:half]

            @pl.when(s[1] == 1)
            def _():
                send[:rest] = own[half:]
                send[rest:] = jnp.zeros((half - rest, 3 * part), BF)

        qkv_own, qkv_half = step(
            take_qkv, [shape_of((part_depth, 3 * part), BF), half_shape], [member, y], [qkv_weight], name="take_qkv"
        )
        qkv_up, qkv_down = depth_line(qkv_half, depth)

        vectors = jnp.concatenate(
            [
                jnp.stack([norm1_gain, norm1_bias, query_bias, value_bias, out_bias, norm2_gain, norm2_bias, down_bias]),
                up_bias.reshape(GROUP, block),
            ]
        )
        vectors = [vectors] + [depth_shift(vectors, r, depth) for r in others]

        def norm_one(s, values, *refs):
            blocks, (normed, whole, up_shift, query_shift, value_shift) = refs[:depth], refs[depth:]

            def put(k):
                for r in range(depth):
                    at = (k - r) % depth * part_depth
                    whole[:, at : at + part_depth] = blocks[r][:8].astype(F32)

                    def of_member(m, r=r):
                        to = (k - r) % depth * block
                        up_shift[:, to : to + block] = blocks[r][8 + m : 9 + m].astype(F32)

                    when_each(s[1], GROUP, of_member)

            when_each(s[0], depth, put)

            def of_member(m):
                query_shift[...] = whole[2:3, m * part : (m + 1) * part]
                value_shift[...] = whole[3:4, m * part : (m + 1) * part]

            when_each(s[1], GROUP, of_member)
            normed[...] = (normal(values[...].astype(F32))[0] * whole[0:1] + whole[1:2]).astype(BF)

        normed_one, whole, up_shift, query_shift, value_shift = step(
            norm_one,
            [row_low, shape_of((8, width), F32), shape_of((1, mine), F32), shape_of((1, part), F32), shape_of((1, part), F32)],
            [z, member],
            [tokens, *vectors],
            name="norm_one",
        )
        normed_one_all = group_gather(normed_one)
        lengths_all = group_gather(lengths)

        def hand_on(up, down, like):
            came = []
            for s_at in others:

                def choose_block(s, *refs, at=s_at - 1):
                    ups, downs, out = refs[: at + 1], refs[at + 1 : -1], refs[-1]

                    def copy(k):
                        out[...] = line_ref(k, next_block(k, at, depth), ups, downs)[...]

                    when_each(s[0], depth, copy)

                (block_now,) = step(choose_block, [like], [z], [*up[:s_at], *down[:s_at]], name="hand_on")
                came.append(swap(block_now, "y"))
                yield came

        qkv_far = list(hand_on(qkv_up, qkv_down, half_shape))[-1]

        pieces = 2 * GROUP
        height = (part_depth // pieces + 7) // 8 * 8
        starts = [(p * (part_depth - height) // (pieces - 1)) // 8 * 8 for p in range(pieces - 1)] + [part_depth - height]
        ends = starts[1:] + [part_depth]

        turn_shape = shape_of((part_depth, mine), BF)

        def take_mlp(s, up, down, out, up_own, turn, piece):
            def part_of(k):
                for n in range(depth):
                    at = n * hidden_depth + k * block
                    up_own[:, n * block : (n + 1) * block] = up[:, at : at + block]

                @pl.when(s[1] == 1)
                def _():
                    turn[...] = down[k * block : (k + 1) * block]

                def piece_of(p):
                    piece[...] = out[starts[p] : starts[p] + height]

                when_each(s[0] + GROUP * s[1], pieces, piece_of)

            when_each(s[0], GROUP, part_of)

            @pl.when(s[1] == 0)
            def _():
                turn[...] = up_own[...]

        up_own, turn, out_piece = step(
            take_mlp,
            [turn_shape, turn_shape, shape_of((height, width), BF)],
            [member, y],
            [up_weight, down_weight, out_weight],
            name="take_mlp",
        )
        out_pieces = [depth_shift(out_piece, r, depth) for r in others]
        mlp_up, mlp_down = depth_line(turn, depth)
        mlp_far_steps = hand_on(mlp_up, mlp_down, turn_shape)

        def live(s, values, grads, low, sums):
            keep = (lax.broadcasted_iota(jnp.int32, (rows, 1), 0) < s[0]).astype(F32)
            kept = values[...].astype(F32) * keep
            grads[...] = kept
            low[...] = kept.astype(BF)
            sums[...] = column_sum(kept)

        grad_rows, grad_low, down_sum = step(
            live, [row_full, row_low, row_sum], [lengths], [cotangent], after=[normed_one_all[2]], name="live"
        )
        grad_all = group_gather(grad_low)

        attend_flops = 2 * rows * width * 3 * part * 2 + 2 * heads * 4 * rows * rows * 128
        lines = depth - 1

        def attend_far(s, own, *refs):
            ups, downs, handed = refs[:lines], refs[lines : 2 * lines], refs[2 * lines : 3 * lines]
            first, second, shift_q, shift_v, full, joined, context = refs[3 * lines :]

            def put(k):
                full[k * part_depth : (k + 1) * part_depth] = own[...]
                for at in range(lines):
                    other = next_block(k, at, depth)
                    low = other * part_depth

                    def both(side, low=low, at=at, other=other):
                        ours = line_ref(k, other, ups, downs)
                        top, bottom = (ours, handed[at]) if side == 0 else (handed[at], ours)
                        full[low : low + half] = top[...]
                        full[low + half : low + part_depth] = bottom[:rest]

                    when_each(s[1], 2, both)

            when_each(s[0], depth, put)
            attend(heads, s[2:], (first, second), full, shift_q, shift_v, joined, (context.at[0], context.at[1]))

        joined_shape = shape_of((2, rows, 3 * part), BF)
        qkv_full, joined_far, context_far = step(
            attend_far,
            [shape_of((width, 3 * part), BF), joined_shape, pair],
            [z, y, lengths_all[2], lengths_all[3]],
            [qkv_own, *qkv_up, *qkv_down, *qkv_far, normed_one_all[2], normed_one_all[3], query_shift, value_shift],
            flops=attend_flops,
            name="attend_far",
        )
        came_far = swap(context_far, "x")
        next(mlp_far_steps)

        def attend_near(s, full, first, second, shift_q, shift_v, joined, ours, theirs):
            attend(heads, s, (first, second), full, shift_q, shift_v, joined, (ours, theirs))

        joined_near, context_own, context_core = step(
            attend_near,
            [joined_shape, cell, cell],
            [lengths_all[0], lengths_all[1]],
            [qkv_full, normed_one_all[0], normed_one_all[1], query_shift, value_shift],
            flops=attend_flops,
            name="attend_near",
        )
        came_core = swap(context_core, "c")
        came_last = swap(came_far[1], "c")

        got = jnp.stack(out_pieces)
        spread = [got]
        for axis in ("c", "x", "y"):
            spread = spread + [swap(v, axis) for v in spread]

        def out_whole(s, own, *refs):
            blocks, full = refs[:-1], refs[-1]

            def put(k):
                full[k * part_depth : (k + 1) * part_depth] = own[...]

                def of_place(p):
                    for other in range(pieces):
                        q = p ^ other
                        for r in others:
                            at = (k - r) % depth * part_depth + starts[q]
                            full[at : at + ends[q] - starts[q]] = blocks[other][r - 1, : ends[q] - starts[q]]

                when_each(s[1] + GROUP * s[2], pieces, of_place)

            when_each(s[0], depth, put)

        (out_full,) = step(
            out_whole, [shape_of((width, width), BF)], [z, member, y], [out_weight, *spread], name="out_whole"
        )
        next(mlp_far_steps)

        def project(s, own, core, far_pair, last, full, values, vector, context, middle, normed):
            def put(k):
                for other, ref in enumerate((own, core, None, last)):
                    at = (k ^ other) * part
                    context[:, at : at + part] = far_pair[0] if ref is None else ref[...]

            when_each(s[0], GROUP, put)
            total = values[...].astype(F32) + (dot(context[...], full[...]) + vector[4:5])
            middle[...] = total
            normed[...] = (normal(total)[0] * vector[5:6] + vector[6:7]).astype(BF)

        context, middle, normed_two = step(
            project,
            [row_low, row_full, row_low],
            [member],
            [context_own, came_core, came_far, came_last, out_full, tokens, whole],
            flops=2 * rows * width * width,
            name="project",
        )
        normed_two_all = group_gather(normed_two)
        mlp_far = list(mlp_far_steps)[-1]

        def feed(s, up_ref, down_ref, *refs):
            ups, downs, handed = refs[:lines], refs[lines : 2 * lines], refs[2 * lines : 3 * lines]
            refs = refs[3 * lines :]
            normed, grads, shift = refs[:4], refs[4:8], refs[8]
            active, before, sums, down_full, two_own, two_core, two_far, up_full = refs[9:]

            def put(k):
                up_full[k * part_depth : (k + 1) * part_depth] = up_ref[...]

                def of_member(m):
                    down_full[k * block : (k + 1) * block] = down_ref[m * block : (m + 1) * block]

                when_each(s[2], GROUP, of_member)
                for at in range(lines):
                    other = next_block(k, at, depth)

                    def both(side, at=at, other=other):
                        ours = line_ref(k, other, ups, downs)
                        up_from, down_from = (ours, handed[at]) if side == 0 else (handed[at], ours)
                        up_full[other * part_depth : (other + 1) * part_depth] = up_from[...]
                        down_full[other * block : (other + 1) * block] = down_from[...]

                    when_each(s[1], 2, both)

            when_each(s[0], depth, put)
            total = jnp.zeros((1, mine), F32)
            for k in (3, 2, 1, 0):
                at = slice(k * rows, (k + 1) * rows)
                value, slope = gelu_both(dot(normed[k][...], up_full[...]) + shift[...])
                active[at] = value.astype(BF)
                grad = (dot_right(grads[k][...], down_full[...]) * slope).astype(BF)
                before[at] = grad
                total = total + column_sum(grad.astype(F32))
                two = dot_right(grad, up_full[...])
                if k == 0:
                    two_own[...] = two
                elif k == 2:
                    two_far[...] = two
                else:
                    two_core[k // 2] = two.astype(BF)
            sums[...] = total

        hidden_rows = shape_of((GROUP * rows, mine), BF)
        active, before, up_sums, down_full, two_own, two_core, two_far = step(
            feed,
            [hidden_rows, hidden_rows, shape_of((1, mine), F32), shape_of((mine, width), BF), row_full, row_pair, row_full],
            [z, y, member],
            [up_own, down_weight, *mlp_up, *mlp_down, *mlp_far, *normed_two_all, *grad_all, up_shift],
            scratch=[pltpu.VMEM((width, mine), BF)],
            flops=3 * 2 * GROUP * rows * width * mine,
            mib=52,
            name="feed",
        )
        two_came = swap(two_core, "c")

        each, side = mine // sides, width // sides

        def columns_for(value, count, index):
            cut = [value[:, (2 * o + index) * count : (2 * o + index + 1) * count] for o in range(outer)]
            return cut[0] if outer == 1 else jnp.concatenate(cut, axis=1)

        def weight_grad(left, right, count, came, name):
            n_left, n_right = len(left), len(right)
            out = shape_of((depth, left[0].shape[1] // depth, outer * count), BF)

            def body(s, *refs):
                lefts, rights = refs[:n_left], refs[n_left : n_left + n_right]
                refs = refs[n_left + n_right :]
                came_ref, (out_ref, *packed) = (None, refs) if came is None else (refs[0], refs[1:])
                left_all = lefts[0] if n_left == 1 else packed[0]
                right_all = packed[-1]
                for k in range(n_left if n_left > 1 else 0):
                    left_all[k * rows : (k + 1) * rows] = lefts[k][...]

                def pack(index):
                    for k, ref in enumerate(rights):
                        tall = ref.shape[0]
                        right_all[k * tall : (k + 1) * tall] = columns_for(ref, count, index)

                when_each(s[0], 2, lambda k: pack(1 - k if came is None else k))
                total = dot_left(left_all[...], right_all[...])
                tall = total.shape[0] // depth
                for n in range(depth):
                    piece = total[n * tall : (n + 1) * tall]
                    if came is not None:
                        piece = piece + came_ref[n].astype(F32)
                    out_ref[n] = piece.astype(BF)

            scratch = [pltpu.VMEM((GROUP * rows, outer * count), BF)]
            if n_left > 1:
                scratch = [pltpu.VMEM((GROUP * rows, left[0].shape[1]), BF)] + scratch
            (result,) = step(
                body, [out], [y], [*left, *right, *([] if came is None else [came])],
                scratch=scratch, flops=2 * GROUP * rows * left[0].shape[1] * outer * count, mib=32, name=name,
            )
            return result

        down_came = swap(weight_grad([active], grad_all, side, None, "down_send"), "y")

        def add_far(s, far, came, out):
            out[...] = (far[...] + came[1].astype(F32)).astype(BF)

        (two_sent,) = step(add_far, [row_low], [], [two_far, two_came], name="add_two")
        two_last = swap(two_sent, "x")
        up_came = swap(weight_grad(normed_two_all, [before], each, None, "up_send"), "y")

        def feed_out(s, active_ref, full, own, core, far_out):
            for k in range(GROUP):
                value = dot(active_ref[k * rows : (k + 1) * rows], full[...])
                if k == 0:
                    own[...] = value
                elif k == 2:
                    far_out[...] = value
                else:
                    core[k // 2] = value.astype(BF)

        mlp_own, mlp_core, mlp_away = step(
            feed_out, [row_full, row_pair, row_full], [], [active, down_full],
            flops=2 * GROUP * rows * width * mine, name="feed_out",
        )
        mlp_came = swap(mlp_core, "c")

        def turn_back(
            s, own, came, last, values, grads, vector, full,
            middle_grad, low, ours, core, far_pair, gain_sum, shift_sum, out_sum,
        ):
            two = own[...] + came[0].astype(F32) + last[...].astype(F32)
            unit, inverse = normal(values[...])
            gain_sum[...] = column_sum(two * unit)
            shift_sum[...] = column_sum(two)
            total = grads[...] + normal_back(two * vector[5:6], unit, inverse)
            middle_grad[...] = total
            low[...] = total.astype(BF)
            out_sum[...] = column_sum(total.astype(BF).astype(F32))
            grad = dot_right(low[...], full[...]).astype(BF)

            def split(k):
                for other in range(GROUP):
                    at = (k ^ other) * part
                    piece = grad[:, at : at + part]
                    if other == 0:
                        ours[...] = piece
                    elif other == 1:
                        core[...] = piece
                    else:
                        far_pair[other - 2] = piece

            when_each(s[0], GROUP, split)

        middle_grad, middle_low, grad_own, grad_core, grad_far, gain_two_sum, shift_two_sum, out_sum = step(
            turn_back,
            [row_full, row_low, cell, cell, pair, row_sum, row_sum, row_sum],
            [member],
            [two_own, two_came, two_last, middle, grad_rows, whole, out_full],
            flops=2 * rows * width * width,
            name="turn_back",
        )
        back_far = swap(grad_far, "x")
        back_core = swap(grad_core, "c")
        back_last = swap(back_far[1], "c")

        strip = width // wide

        def out_grad(s, low, values, send, keep):
            total = dot_left(low[...], values[...])

            def split(k):
                for q in range(wide // 2):
                    for core in range(2):
                        target = keep if core == k else send
                        at = (2 * q + core) * strip
                        target[q] = total[at : at + strip].astype(BF)

            when_each(s[0], 2, split)

        out_shape = shape_of((wide // 2, strip, width), BF)
        out_send, out_keep = step(
            out_grad, [out_shape, out_shape], [c], [middle_low, context], flops=2 * rows * width * width, name="out_grad"
        )
        out_came = swap(out_send, "c")

        def out_fold(flag, keep, came, span):
            count = keep.shape[0] // 2

            def body(s, kept, arrived, send, keep_out):
                def split(k):
                    for q in range(count):
                        at = q // span * 2 * span + q % span
                        for bit in range(2):
                            target = keep_out if bit == k else send
                            source = at + bit * span
                            target[q] = (kept[source].astype(F32) + arrived[source].astype(F32)).astype(BF)

                when_each(s[0], 2, split)

            out = shape_of((count, strip, width), BF)
            return step(body, [out, out], [flag], [keep, came], name="out_fold")

        down_parts = depth_exchange(weight_grad([active], grad_all, side, down_came, "down_keep"))
        out_send, out_keep = out_fold(x, out_keep, out_came, 1)
        out_came = swap(out_send, "x")
        (mlp_sent,) = step(add_far, [row_low], [], [mlp_away, mlp_came], name="add_mlp")
        mlp_last = swap(mlp_sent, "x")

        def attend_back_near(s, joined, first, second, out):
            attend_back(heads, s, joined, (first, second), out)

        def attend_back_far(s, joined, first, second, out):
            attend_back(heads, s, joined, (first.at[0], second), out)

        back_flops = 2 * heads * 2 * rows * rows * 5 * 128 * 2
        (joined_grad_near,) = step(
            attend_back_near, [joined_shape], [lengths_all[0], lengths_all[1]], [joined_near, grad_own, back_core],
            flops=back_flops, name="attend_back_near",
        )
        up_parts = depth_exchange(weight_grad(normed_two_all, [before], each, up_came, "up_keep"))
        out_send, out_keep = out_fold(y, out_keep, out_came, 1)
        out_came = swap(out_send, "y")
        (joined_grad_far,) = step(
            attend_back_far, [joined_shape], [lengths_all[2], lengths_all[3]], [joined_far, back_far, back_last],
            flops=back_flops, name="attend_back_far",
        )

        def qkv_grad(s, first, second, third, fourth, near_ref, far_ref, send, keep, sums, left_all, right_all):
            for k, ref in enumerate((first, second, third, fourth)):
                left_all[k * rows : (k + 1) * rows] = ref[...]
                right_all[k * rows : (k + 1) * rows] = (near_ref, far_ref)[k // 2][k % 2]
            sums[...] = column_sum(right_all[...].astype(F32))
            total = dot_left(left_all[...], right_all[...])

            def split(k):
                first_half, second_half = (keep, send) if k == 0 else (send, keep)
                for n in range(depth):
                    at = n * part_depth
                    first_half[n] = total[at : at + half].astype(BF)
                    second_half[n, :rest] = total[at + half : at + part_depth].astype(BF)
                    second_half[n, rest:] = jnp.zeros((half - rest, 3 * part), BF)

            when_each(s[0], 2, split)

        halves = shape_of((depth, half, 3 * part), BF)
        qkv_send, qkv_keep, joined_sums = step(
            qkv_grad,
            [halves, halves, shape_of((1, 3 * part), F32)],
            [y],
            [*normed_one_all, joined_grad_near, joined_grad_far],
            scratch=[pltpu.VMEM((GROUP * rows, width), BF), pltpu.VMEM((GROUP * rows, 3 * part), BF)],
            flops=2 * GROUP * rows * width * 3 * part,
            mib=32,
            name="qkv_grad",
        )
        qkv_came = swap(qkv_send, "y")

        def one_back(s, near_ref, far_ref, full, own, core, far_out):
            own[...] = dot_right(near_ref[0], full[...])
            core[0] = dot_right(near_ref[1], full[...]).astype(BF)
            far_out[...] = dot_right(far_ref[0], full[...])
            core[1] = dot_right(far_ref[1], full[...]).astype(BF)

        one_own, one_core, one_far = step(
            one_back, [row_full, row_pair, row_full], [], [joined_grad_near, joined_grad_far, qkv_full],
            flops=2 * GROUP * rows * width * 3 * part, name="one_back",
        )
        one_came = swap(one_core, "c")

        def leave(s, own, came, last, values, vector, out):
            keep = (lax.broadcasted_iota(jnp.int32, (rows, 1), 0) < s[0]).astype(F32)
            fed = own[...] + came[0].astype(F32) + last[...].astype(F32) + vector[7:8]
            out[...] = (keep * (values[...] + fed)).astype(BF)

        (block_out,) = step(
            leave, [row_low], [lengths], [mlp_own, mlp_came, mlp_last, middle, whole], name="leave"
        )
        (one_sent,) = step(add_far, [row_low], [], [one_far, one_came], name="add_one")
        one_last = swap(one_sent, "x")

        tall = max(block, part_depth)
        low_type = BF if outer == 1 else F32

        def feed_pieces(s, down_ref, up_ref, out):
            for at, ref in enumerate((down_ref, up_ref)):
                total = ref[0].astype(F32)
                for n in others:
                    total = total + ref[n].astype(F32)
                out[at] = total.astype(low_type)

        (feed_piece,) = step(
            feed_pieces, [shape_of((2, tall, outer * each), low_type)], [], [down_parts, up_parts], name="feed_pieces"
        )
        if outer > 1:
            feed_piece = feed_piece.reshape(2, tall, outer, each)
            feed_piece = lax.psum_scatter(feed_piece, "o", scatter_dimension=2, tiled=False).astype(BF)
        feed_all = group_gather(feed_piece)

        def qkv_fold(s, keep, came, out):
            for n in range(depth):
                out[n] = (keep[n].astype(F32) + came[n].astype(F32)).astype(BF)

        (qkv_parts,) = step(qkv_fold, [halves], [], [qkv_keep, qkv_came], name="qkv_fold")
        qkv_parts = depth_exchange(qkv_parts)

        def out_split(s, keep, came, out):
            for q in range(outer):
                total = keep[q].astype(F32) + came[q].astype(F32)
                for n in range(depth):
                    out[n, q] = total[:, n * part_depth : (n + 1) * part_depth].astype(BF)

        (out_parts,) = step(
            out_split, [shape_of((depth, outer, strip, part_depth), BF)], [], [out_keep, out_came], name="out_split"
        )
        out_parts = depth_exchange(out_parts)

        def finish(s, own, came, last, values, vector, middle_ref, out, gain_sum, shift_sum):
            one = own[...] + came[0].astype(F32) + last[...].astype(F32)
            unit, inverse = normal(values[...].astype(F32))
            gain_sum[...] = column_sum(one * unit)
            shift_sum[...] = column_sum(one)
            out[...] = middle_ref[...] + normal_back(one * vector[0:1], unit, inverse)

        input_grad, gain_one_sum, shift_one_sum = step(
            finish, [row_full, row_sum, row_sum], [],
            [one_own, one_came, one_last, tokens, whole, middle_grad], name="finish",
        )

        def vector_pack(s, gain_one, shift_one, joined, out_ref, gain_two, shift_two, down_ref, up_ref, packed, line):
            packed[...] = jnp.zeros(packed.shape, F32)
            line[...] = jnp.zeros(line.shape, F32)
            for k, ref in ((0, gain_one), (1, shift_one), (4, out_ref), (5, gain_two), (6, shift_two), (7, down_ref)):
                line[k : k + 1] = ref[...]

            def of_member(m):
                line[2:3, m * part : (m + 1) * part] = joined[:, :part]
                line[3:4, m * part : (m + 1) * part] = joined[:, 2 * part :]
                for n in range(depth):
                    packed[n, 8 + m : 9 + m] = up_ref[:, n * block : (n + 1) * block]

            when_each(s[0], GROUP, of_member)
            for n in range(depth):
                packed[n, :8] = line[:, n * part_depth : (n + 1) * part_depth]

        (packed,) = step(
            vector_pack,
            [shape_of((depth, 8 + GROUP, part_depth), F32)],
            [member],
            [gain_one_sum, shift_one_sum, joined_sums, out_sum, gain_two_sum, shift_two_sum, down_sum, up_sums],
            scratch=[pltpu.VMEM((8, width), F32)],
            name="vector_pack",
        )
        packed = jnp.sum(depth_exchange(packed), axis=0)
        for axis in ("c", "x", "y"):
            packed = packed + swap(packed, axis)
        if outer > 1:
            packed = lax.psum(packed, "o")

        ratio = wide // depth
        fold = GROUP // ratio

        def feed_grads(s, *refs):
            blocks, (down_out, up_out) = refs[:4], refs[4:]

            def of_member(k):
                for m in range(GROUP):
                    cut = blocks[k ^ m][0, :, k * (side // GROUP) : (k + 1) * (side // GROUP)]
                    down_out[m * block : (m + 1) * block] = cut.astype(F32)
                for f in range(fold):
                    source = k % ratio * fold + f
                    at = k // ratio * block
                    up_out[:, f * block : (f + 1) * block] = blocks[k ^ source][1, :, at : at + block].astype(F32)

            when_each(s[0], GROUP, of_member)

        down_weight_grad, up_weight_grad = step(
            feed_grads,
            [shape_of((hidden_depth, side // GROUP), F32), shape_of((part_depth, fold * block), F32)],
            [member],
            feed_all,
            name="feed_grads",
        )

        def qkv_sum(s, parts, out):
            total = parts[0].astype(F32)
            for n in others:
                total = total + parts[n].astype(F32)
            out[...] = total.astype(BF)

        (qkv_piece,) = step(qkv_sum, [half_shape], [], [qkv_parts], name="qkv_sum")
        qkv_all = group_gather(qkv_piece)
        span = 3 * width // wide

        def qkv_columns(s, *refs):
            blocks, (keep, send) = refs[:4], refs[4:]

            def of_member(k):
                for o in range(outer):
                    for side_at in range(2):
                        cut, at = [], ((2 * o + side_at) * GROUP + k) * span
                        stop = at + span
                        while at < stop:
                            to = min(stop, (at // part + 1) * part)
                            p, m = divmod(at // part, GROUP)
                            low = p * part + at % part
                            cut.append(blocks[k ^ m][:, low : low + to - at])
                            at = to
                        found = cut[0] if len(cut) == 1 else jnp.concatenate(cut, axis=1)

                        def put(here, found=found, side_at=side_at, o=o):
                            target = keep if here == side_at else send
                            target[o] = found

                        when_each(s[1], 2, put)

            when_each(s[0], GROUP, of_member)

        span_shape = shape_of((outer, half, span), BF)
        qkv_keep, qkv_send = step(
            qkv_columns, [span_shape, span_shape], [member, y], qkv_all, name="qkv_columns"
        )
        if outer > 1:
            qkv_keep, qkv_send = (
                lax.psum_scatter(v.astype(F32), "o", scatter_dimension=0, tiled=True).astype(BF)
                for v in (qkv_keep, qkv_send)
            )
        qkv_came = swap(qkv_send, "y")

        def out_last(s, parts, out):
            total = parts[0].astype(F32)
            for n in others:
                total = total + parts[n].astype(F32)
            out[...] = total

        (out_sums,) = step(out_last, [shape_of((outer, strip, part_depth), F32)], [], [out_parts], name="out_last")
        out_sums = out_sums[0] if outer == 1 else lax.psum_scatter(out_sums, "o", scatter_dimension=0, tiled=False)
        out_weight_grad = out_sums.T

        def qkv_rows(s, keep, came, out):
            def put(k):
                top, bottom = (keep, came) if k == 0 else (came, keep)
                out[:half] = top[0].astype(F32)
                out[half:] = bottom[0, :rest].astype(F32)

            when_each(s[0], 2, put)

        (qkv_weight_grad,) = step(
            qkv_rows, [shape_of((part_depth, span), F32)], [y], [qkv_keep, qkv_came], name="qkv_rows"
        )
        return (
            block_out, input_grad, packed[0], packed[1], qkv_weight_grad, packed[2], packed[3], out_weight_grad,
            packed[4], packed[5], packed[6], up_weight_grad, packed[8:].reshape(hidden_depth), down_weight_grad, packed[7],
        )

    return shards


def solution(mesh):
    wide, depth = mesh.shape["wide"], mesh.shape["narrow"]
    outer = wide // 8
    fine = Mesh(mesh.devices.reshape(outer, 2, 2, 2, depth), AXES)
    rows, vec, mat = P(AXES, None), P("z"), P("z", None)
    placed = (
        rows, P(AXES), vec, vec, mat, vec, vec, mat, vec, vec, vec, mat, vec, mat, vec, rows,
    )
    grad = P("z", WIDE)
    return jax.shard_map(
        build(outer, depth),
        mesh=fine,
        in_specs=placed,
        out_specs=(rows, rows, vec, vec, grad, vec, vec, grad, vec, vec, vec, grad, vec, grad, vec),
        check_vma=False,
    )
```

```python
import functools

import jax
import jax.numpy as jnp
from jax import lax
from jax.experimental import pallas as pl
from jax.experimental.pallas import tpu as pltpu
from jax.sharding import Mesh, PartitionSpec as P

HEADS = 20
EPSILON = 1e-05
FILL = -1000000000.0
BF = jnp.bfloat16
F32 = jnp.float32
AXES = ("o", "y", "x", "c", "z")
WIDE = ("o", "y", "x", "c")
SWAP = [(0, 1), (1, 0)]
GROUP = 4
MIB = 1024 * 1024
PER_MICRO = 0.55e6


def swap(value, axis):
    return lax.ppermute(value, axis, SWAP)


def dot(first, second):
    return jnp.dot(first, second, preferred_element_type=F32)


def dot_left(first, second):
    return lax.dot_general(first, second, (((0,), (0,)), ((), ())), preferred_element_type=F32)


def dot_right(first, second):
    return lax.dot_general(first, second, (((1,), (1,)), ((), ())), preferred_element_type=F32)


def shape_of(dims, dtype):
    return jax.ShapeDtypeStruct(dims, dtype)


class Order:
    def __init__(self):
        self.token = None

    def __call__(self, body, outs, scalars, arrays, far=(), after=(), scratch=(), mib=28, micros=1.0, name=None):
        after = list(after) + ([] if self.token is None else [self.token])
        n_scalar, n_array, n_out = len(scalars), len(arrays) + len(far), len(outs)

        def run(*refs):
            token = refs[n_scalar + n_array + len(after) + n_out]
            values = tuple(ref[0] for ref in refs[:n_scalar])
            rest = refs[n_scalar + n_array + len(after) :]
            token[...] = jnp.zeros(token.shape, F32)
            body(values, *refs[n_scalar : n_scalar + n_array], *rest[:n_out], *rest[n_out + 1 :])

        *given, self.token = pl.pallas_call(
            run,
            out_shape=(*outs, shape_of((8, 128), F32)),
            in_specs=[pl.BlockSpec(memory_space=pltpu.SMEM)] * n_scalar
            + [pl.BlockSpec(memory_space=pltpu.VMEM)] * len(arrays)
            + [pl.BlockSpec(memory_space=pltpu.HBM)] * len(far)
            + [pl.BlockSpec(memory_space=pl.ANY)] * len(after),
            out_specs=(pl.BlockSpec(memory_space=pltpu.VMEM),) * (n_out + 1),
            scratch_shapes=list(scratch),
            compiler_params=pltpu.CompilerParams(vmem_limit_bytes=mib * MIB),
            cost_estimate=pl.CostEstimate(flops=0, bytes_accessed=int(micros * PER_MICRO), transcendentals=0),
            name=name,
        )(*scalars, *arrays, *far, *after)
        return given


def group_gather(value):
    over_x = swap(value, "x")
    over_core = swap(value, "c")
    return [value, over_core, over_x, swap(over_x, "c")]


def depth_shift(value, shift, count):
    return lax.ppermute(value, "z", [(i, (i + shift) % count) for i in range(count)])


def depth_line(value, count):
    up, down = [], []
    for s in range(count - 1):
        up.append(lax.ppermute(up[-1] if s else value, "z", [(i, i + 1) for i in range(s, count - 1)]))
        down.append(lax.ppermute(down[-1] if s else value, "z", [(i, i - 1) for i in range(1, count - s)]))
    return up, down


def next_block(z, step, count):
    return z + 1 + step if step < count - 1 - z else count - 2 - step


def line_ref(z, other, up, down):
    return up[z - 1 - other] if other < z else down[other - z - 1]


def depth_exchange(parts):
    return lax.all_to_all(parts, "z", 0, 0)


def sum_of(refs):
    total = refs[0].astype(F32)
    for k in range(1, refs.shape[0]):
        total = total + refs[k].astype(F32)
    return total


def normal(values):
    center = values - jnp.mean(values, axis=-1, keepdims=True)
    spread = jnp.mean(center * center, axis=-1, keepdims=True)
    inverse = lax.rsqrt(spread + EPSILON)
    return center * inverse, inverse


def normal_back(grad, unit, inverse):
    return (
        grad
        - jnp.mean(grad, axis=-1, keepdims=True)
        - unit * jnp.mean(grad * unit, axis=-1, keepdims=True)
    ) * inverse


def when_each(index, count, step):
    for k in range(count):
        pl.when(index == k)(functools.partial(step, k))


def allowed_of(rows, length):
    query = lax.broadcasted_iota(jnp.int32, (rows, rows), 0)
    key = lax.broadcasted_iota(jnp.int32, (rows, rows), 1)
    return (key <= query) & (key < length)


def length_of(payload, rows):
    high = payload[rows : rows + 1, 0:1].astype(F32)
    low = payload[rows : rows + 1, 128:129].astype(F32)
    return (high * 16.0 + low).astype(jnp.int32)


def head_probs(query, key, allowed, scale):
    scores = jnp.where(allowed, dot_right(query, key) * scale, FILL)
    weights = jnp.exp(scores - jnp.max(scores, axis=1, keepdims=True))
    return weights * (1.0 / jnp.sum(weights, axis=1, keepdims=True))


def attend(heads, tokens, full, vectors, query_shift, value_shift, normed, joined, contexts):
    rows, part = normed.shape[1], full.shape[1] // 3
    head = part // heads
    scale = head ** (-0.5)
    for n, x in enumerate(tokens):
        normed[n] = (normal(x[:rows].astype(F32))[0] * vectors[0:1] + vectors[1:2]).astype(BF)
        sums = dot(normed[n], full[...])
        query = (sums[:, :part] + query_shift[...]).astype(BF)
        key = sums[:, part : 2 * part].astype(BF)
        value = (sums[:, 2 * part :] + value_shift[...]).astype(BF)
        joined[n, :, :part] = query
        joined[n, :, part : 2 * part] = key
        joined[n, :, 2 * part :] = value
        allowed = allowed_of(rows, length_of(x, rows))
        out = []
        for h in range(heads):
            cut = slice(h * head, (h + 1) * head)
            probs = head_probs(query[:, cut], key[:, cut], allowed, scale).astype(BF)
            out.append(dot(probs, value[:, cut]))
        contexts[n][...] = jnp.concatenate(out, axis=1).astype(BF)


def attend_back(chosen, head, length, joined, above, out):
    rows, part = above.shape
    scale = head ** (-0.5)
    allowed = allowed_of(rows, length)
    found = ([], [], [])
    for h in chosen:
        q, k, v = (joined[:, p * part + h * head : p * part + (h + 1) * head] for p in range(3))
        g = above[:, h * head : (h + 1) * head]
        probs = head_probs(q, k, allowed, scale)
        probs_grad = dot_right(g, v)
        found[2].append(dot_left(probs.astype(BF), g))
        score = probs * (probs_grad - jnp.sum(probs * probs_grad, axis=1, keepdims=True))
        score = score.astype(BF)
        found[0].append(dot(score, k) * scale)
        found[1].append(dot_left(score, q) * scale)
    out[...] = jnp.concatenate(found[0] + found[1] + found[2], axis=1).astype(BF)


def gelu_both(values):
    root = (2.0 / jnp.pi) ** 0.5
    square = values * values
    bend = jnp.tanh(root * (values + 0.044715 * (square * values)))
    half = 0.5 * (1.0 + bend)
    slope = half + 0.5 * values * (1.0 - bend * bend) * (root * (1.0 + 3.0 * 0.044715 * square))
    return values * half, slope


def column_sum(values):
    return jnp.sum(values, axis=0, keepdims=True)


def build(outer, depth):
    def shards(
        tokens, lengths, norm1_gain, norm1_bias, qkv_weight, query_bias, value_bias, out_weight,
        out_bias, norm2_gain, norm2_bias, up_weight, up_bias, down_weight, down_bias, cotangent,
    ):
        rows, width = tokens.shape
        heads = HEADS // GROUP
        part = width // GROUP
        part_depth = width // depth
        hidden_depth = up_weight.shape[1] // depth
        block = hidden_depth // GROUP
        mine = depth * block
        wide = outer * 2 * GROUP
        sides = outer * 2
        y, x, c, z = (lax.axis_index(name).astype(jnp.int32).reshape(1) for name in ("y", "x", "c", "z"))
        member = 2 * x + c
        others = range(1, depth)
        step = Order()

        row_low, row_full = shape_of((rows, width), BF), shape_of((rows, width), F32)
        row_pair = shape_of((2, rows, width), BF)
        row_sum = shape_of((1, width), F32)
        cell, pair = shape_of((rows, part), BF), shape_of((2, rows, part), BF)

        def take_rows(s, values, out):
            out[:rows] = values[...]
            lane = lax.broadcasted_iota(jnp.int32, (16, width), 1)
            out[rows:] = jnp.where(lane < 128, s[0] // 16, s[0] % 16).astype(F32).astype(BF)

        (tokens_low,) = step(
            take_rows, [shape_of((rows + 16, width), BF)], [lengths], [tokens], micros=0.8, mib=10, name="take_rows"
        )
        tokens_all = group_gather(tokens_low)

        half = (part_depth // 2 + 15) // 16 * 16
        rest = part_depth - half
        quad_shape, half_shape = shape_of((part_depth, 4 * part), BF), shape_of((half, 4 * part), BF)
        biases = (norm1_gain, norm1_bias, query_bias, value_bias, out_bias, norm2_gain, norm2_bias, down_bias, up_bias)

        def take_quad(s, qkv, out, own, send):
            def columns(k):
                for p in range(3):
                    at = (p * GROUP + k) * part
                    own[:, p * part : (p + 1) * part] = qkv[:, at : at + part]
                own[:, 3 * part :] = out[:, k * part : (k + 1) * part]

            when_each(s[0], GROUP, columns)

            @pl.when(s[1] == 0)
            def _():
                send[...] = own[:half]

            @pl.when(s[1] == 1)
            def _():
                send[:rest] = own[half:]
                send[rest:] = jnp.zeros((half - rest, 4 * part), BF)

        quad_own, quad_half = step(
            take_quad, [quad_shape, half_shape], [member, y], [qkv_weight, out_weight], micros=0.5, mib=12, name="take_quad"
        )
        quad_up, quad_down = depth_line(quad_half, depth)

        def take_vectors(s, *refs):
            found = [ref[...].astype(F32).reshape(1, part_depth) for ref in refs[:8]]
            more = [refs[8][k * block : (k + 1) * block].astype(F32).reshape(1, block) for k in range(GROUP)]
            refs[9][...] = jnp.zeros(refs[9].shape, F32)
            refs[9][:8, :part_depth] = jnp.concatenate(found, axis=0)
            refs[9][:GROUP, part_depth : 2 * part_depth] = jnp.concatenate(more, axis=0)

        (lines_own,) = step(
            take_vectors, [shape_of((8, 2 * part_depth), F32)], [], biases, micros=0.5, mib=8, name="take_vectors"
        )
        lines_all = [lines_own] + [depth_shift(lines_own, r, depth) for r in others]

        def live(s, values, low, sums):
            keep = (lax.broadcasted_iota(jnp.int32, (rows, 1), 0) < s[0]).astype(F32)
            kept = values[...].astype(F32) * keep
            low[...] = kept.astype(BF)
            sums[...] = column_sum(kept)

        grad_low, down_sum = step(live, [row_low, row_sum], [lengths], [cotangent], micros=0.5, mib=10, name="live")
        grad_all = group_gather(grad_low)

        def hand_on(up, down, like, after=False):
            came = []
            for s_at in others:

                def choose_block(s, *refs, at=s_at - 1):
                    ups, downs, out = refs[: at + 1], refs[at + 1 : -1], refs[-1]

                    def copy(k):
                        out[...] = line_ref(k, next_block(k, at, depth), ups, downs)[...]

                    when_each(s[0], depth, copy)

                (block_now,) = step(
                    choose_block, [like], [z], [*up[:s_at], *down[:s_at]], after=came[-1:] if after else (), micros=1.5, mib=8, name="hand_on"
                )
                came.append(swap(block_now, "y"))
                yield came

        quad_far = list(hand_on(quad_up, quad_down, half_shape))[-1]

        turn_shape = shape_of((part_depth, mine), BF)

        def take_mlp(s, up, down, up_own, turn):
            def part_of(k):
                for n in range(depth):
                    at = n * hidden_depth + k * block
                    up_own[:, n * block : (n + 1) * block] = up[:, at : at + block]

                @pl.when(s[1] == 1)
                def _():
                    turn[...] = down[k * block : (k + 1) * block]

            when_each(s[0], GROUP, part_of)

            @pl.when(s[1] == 0)
            def _():
                turn[...] = up_own[...]

        up_own, turn = step(
            take_mlp, [turn_shape, turn_shape], [member, y], [up_weight, down_weight], after=[quad_up[-1], quad_down[-1]], micros=1.2, mib=20,
            name="take_mlp",
        )
        mlp_up, mlp_down = depth_line(turn, depth)
        mlp_far_steps = hand_on(mlp_up, mlp_down, turn_shape, True)

        lines = depth - 1

        def assemble(s, own, *refs):
            blocks, refs = refs[:depth], refs[depth:]
            ups, downs, handed = refs[:lines], refs[lines : 2 * lines], refs[2 * lines : 3 * lines]
            full, out_cols, whole, query_shift, value_shift, up_shift = refs[3 * lines :]

            def put_vectors(at, values):
                whole[:, at * part_depth : (at + 1) * part_depth] = values[:, :part_depth]

                def of_member(m):
                    up_shift[:, at * block : (at + 1) * block] = values[m : m + 1, part_depth : 2 * part_depth]

                when_each(s[2], GROUP, of_member)

            def put(k):
                full[k * part_depth : (k + 1) * part_depth] = own[:, : 3 * part]
                out_cols[:, k * part : (k + 1) * part] = own[:, 3 * part :]
                for r in range(depth):
                    put_vectors((k - r) % depth, blocks[r][...])
                for at in range(lines):
                    other = next_block(k, at, depth)
                    low, cols = other * part_depth, slice(other * part, (other + 1) * part)

                    def both(side, at=at, low=low, cols=cols, other=other):
                        ours = line_ref(k, other, ups, downs)
                        top, bottom = (ours, handed[at]) if side == 0 else (handed[at], ours)
                        full[low : low + half] = top[:, : 3 * part]
                        full[low + half : low + part_depth] = bottom[:rest, : 3 * part]
                        out_cols[:half, cols] = top[:, 3 * part :]
                        out_cols[half:, cols] = bottom[:rest, 3 * part :]

                    when_each(s[1], 2, both)

            when_each(s[0], depth, put)

            def of_member(m):
                query_shift[...] = whole[2:3, m * part : (m + 1) * part]
                value_shift[...] = whole[3:4, m * part : (m + 1) * part]

            when_each(s[2], GROUP, of_member)

        shift_shape = shape_of((1, part), F32)
        qkv_full, out_part, whole, query_shift, value_shift, up_shift = step(
            assemble,
            [shape_of((width, 3 * part), BF), shape_of((part_depth, depth * part), BF), shape_of((8, width), F32), shift_shape,
             shift_shape, shape_of((1, mine), F32)],
            [z, y, member],
            [quad_own, *lines_all, *quad_up, *quad_down, *quad_far],
            after=[grad_all[2]],
            micros=1.3, mib=16, name="assemble",
        )
        out_all = group_gather(out_part)
        next(mlp_far_steps)


        def attend_far(s, full, vector, first, second, shift_q, shift_v, normed, joined, context):
            attend(heads, (first, second), full, vector, shift_q, shift_v, normed, joined,
                   (context.at[0], context.at[1]))

        joined_shape = shape_of((2, rows, 3 * part), BF)
        normed_far, joined_far, context_far = step(
            attend_far,
            [row_pair, joined_shape, pair],
            [],
            [qkv_full, whole, tokens_all[2], tokens_all[3], query_shift, value_shift],
            micros=9, mib=20, name="attend_far",
        )
        came_far = swap(context_far, "x")
        next(mlp_far_steps)

        def attend_near(s, full, vector, first, second, shift_q, shift_v, normed, joined, ours, theirs):
            attend(heads, (first, second), full, vector, shift_q, shift_v, normed, joined,
                   (ours, theirs))

        normed_near, joined_near, context_own, context_core = step(
            attend_near,
            [row_pair, joined_shape, cell, cell],
            [],
            [qkv_full, whole, tokens_all[0], tokens_all[1], query_shift, value_shift],
            micros=9, mib=20, name="attend_near",
        )
        came_core = swap(context_core, "c")
        came_last = swap(came_far[1], "c")

        mlp_far = list(mlp_far_steps)[-1]

        def out_whole(s, *refs):
            blocks, full = refs[:-1], refs[-1]

            def put(k):
                for other in range(GROUP):
                    at = (k ^ other) * part
                    for n in range(depth):
                        rows_of = slice(n * part_depth, (n + 1) * part_depth)
                        full[rows_of, at : at + part] = blocks[other][:, n * part : (n + 1) * part]

            when_each(s[0], GROUP, put)

        (out_full,) = step(out_whole, [shape_of((width, width), BF)], [member], out_all, micros=1, mib=12, name="out_whole")

        def project(s, own, core, far_pair, last, full, values, vector, context, middle, normed):
            def put(k):
                for other, ref in enumerate((own, core, None, last)):
                    at = (k ^ other) * part
                    context[:, at : at + part] = far_pair[0] if ref is None else ref[...]

            when_each(s[0], GROUP, put)
            total = values[...].astype(F32) + (dot(context[...], full[...]) + vector[4:5])
            middle[...] = total
            normed[...] = (normal(total)[0] * vector[5:6] + vector[6:7]).astype(BF)

        context, middle, normed_two = step(
            project,
            [row_low, row_full, row_low],
            [member],
            [context_own, came_core, came_far, came_last, out_full, tokens, whole],
            micros=3.6, mib=20, name="project",
        )
        normed_two_all = group_gather(normed_two)

        def feed(s, up_ref, down_ref, *refs):
            ups, downs, handed = refs[:lines], refs[lines : 2 * lines], refs[2 * lines : 3 * lines]
            refs = refs[3 * lines :]
            normed, grads, shift = refs[:4], refs[4:8], refs[8]
            active, before, sums, down_full, two_own, two_core, two_far, up_full = refs[9:]

            def put(k):
                up_full[k * part_depth : (k + 1) * part_depth] = up_ref[...]

                def of_member(m):
                    down_full[k * block : (k + 1) * block] = down_ref[m * block : (m + 1) * block]

                when_each(s[2], GROUP, of_member)
                for at in range(lines):
                    other = next_block(k, at, depth)

                    def both(side, at=at, other=other):
                        ours = line_ref(k, other, ups, downs)
                        up_from, down_from = (ours, handed[at]) if side == 0 else (handed[at], ours)
                        up_full[other * part_depth : (other + 1) * part_depth] = up_from[...]
                        down_full[other * block : (other + 1) * block] = down_from[...]

                    when_each(s[1], 2, both)

            when_each(s[0], depth, put)
            total = jnp.zeros((1, mine), F32)
            for k in (3, 2, 1, 0):
                at = slice(k * rows, (k + 1) * rows)
                value, slope = gelu_both(dot(normed[k][...], up_full[...]) + shift[...])
                active[at] = value.astype(BF)
                grad = (dot_right(grads[k][...], down_full[...]) * slope).astype(BF)
                before[at] = grad
                total = total + column_sum(grad.astype(F32))
                two = dot_right(grad, up_full[...])
                if k == 0:
                    two_own[...] = two
                elif k == 2:
                    two_far[...] = two
                else:
                    two_core[k // 2] = two.astype(BF)
            sums[...] = total

        hidden_rows = shape_of((GROUP * rows, mine), BF)
        active, before, up_sums, down_full, two_own, two_core, two_far = step(
            feed,
            [hidden_rows, hidden_rows, shape_of((1, mine), F32), shape_of((mine, width), BF), row_full, row_pair, row_full],
            [z, y, member],
            [up_own, down_weight, *mlp_up, *mlp_down, *mlp_far, *normed_two_all, *grad_all, up_shift],
            scratch=[pltpu.VMEM((width, mine), BF)],
            mib=52,
            micros=22.6, name="feed",
        )
        two_came = swap(two_core, "c")

        each, side = mine // sides, width // sides

        def columns_for(value, count, index):
            cut = [value[:, (2 * o + index) * count : (2 * o + index + 1) * count] for o in range(outer)]
            return cut[0] if outer == 1 else jnp.concatenate(cut, axis=1)

        tall = max(block, part_depth)
        fold_rows = (tall // 2 + 15) // 16 * 16
        fold_rest = tall - fold_rows
        pack_shape = shape_of((depth, fold_rows, 2 * outer * each), BF)
        feed_scratch = [pltpu.VMEM((GROUP * rows, width), BF), pltpu.VMEM((GROUP * rows, outer * each), BF)]

        def store_rows(total, came, out):
            cut = total.shape[1]
            for n in range(depth):
                top = total[n * tall : n * tall + fold_rows]
                low = total[n * tall + fold_rows : (n + 1) * tall]
                if came is not None:
                    top = top + came[n, :, :cut].astype(F32)
                    low = low + came[n, :fold_rest, cut:].astype(F32)
                out[n, :, :cut] = top.astype(BF)
                out[n, :fold_rest, cut:] = low.astype(BF)
                out[n, fold_rest:, cut:] = jnp.zeros((fold_rows - fold_rest, cut), BF)

        def down_product(grads, right_all, index):
            for k, ref in enumerate(grads):
                right_all[k * rows : (k + 1) * rows] = columns_for(ref[...], side, index)

        def up_product(before_ref, right_all, index):
            right_all[...] = columns_for(before_ref[...], each, index)

        def feed_part(product, arrays, scratch, came, name, after=()):
            n_array, n_came = len(arrays), len(came)

            def body(s, *refs):
                inputs, came_refs, (out, *left_refs, right_all) = (
                    refs[:n_array], refs[n_array : n_array + n_came], refs[n_array + n_came :]
                )
                when_each(s[0], 2, lambda k: product(inputs, right_all, k if n_came else 1 - k))
                if left_refs:
                    for k in range(GROUP):
                        left_refs[0][k * rows : (k + 1) * rows] = inputs[1 + k][...]
                left = left_refs[0] if left_refs else inputs[0]
                store_rows(dot_left(left[...], right_all[...]), came_refs[0] if n_came else None, out)

            return step(
                body, [pack_shape], [y], [*arrays, *came], after=after, scratch=scratch, mib=32, micros=4, name=name
            )[0]

        def down_part(came, name, after=()):
            return feed_part(
                lambda refs, right, k: down_product(refs[1:], right, k),
                [active, *grad_all], feed_scratch[1:], came, name, after,
            )

        def up_part(came, name, after=()):
            return feed_part(
                lambda refs, right, k: up_product(refs[0], right, k),
                [before, *normed_two_all], feed_scratch, came, name, after,
            )

        down_came = swap(down_part([], "down_send"), "y")

        def add_far(s, far, came, out):
            out[...] = (far[...] + came[1].astype(F32)).astype(BF)

        (two_sent,) = step(add_far, [row_low], [], [two_far, two_came], micros=0.7, mib=10, name="add_two")
        two_last = swap(two_sent, "x")

        def feed_out(s, active_ref, full, own, core, far_out):
            for k in range(GROUP):
                value = dot(active_ref[k * rows : (k + 1) * rows], full[...])
                if k == 0:
                    own[...] = value
                elif k == 2:
                    far_out[...] = value
                else:
                    core[k // 2] = value.astype(BF)

        mlp_own, mlp_core, mlp_away = step(
            feed_out, [row_full, row_pair, row_full], [], [active, down_full],
        )
        mlp_came = swap(mlp_core, "c")

        def turn_back(
            s, own, came, last, values, grads, vector, full,
            middle_grad, low, ours, core, far_pair, gain_sum, shift_sum, out_sum,
        ):
            two = own[...] + came[0].astype(F32) + last[...].astype(F32)
            unit, inverse = normal(values[...])
            gain_sum[...] = column_sum(two * unit)
            shift_sum[...] = column_sum(two)
            total = grads[...].astype(F32) + normal_back(two * vector[5:6], unit, inverse)
            middle_grad[...] = total
            low[...] = total.astype(BF)
            out_sum[...] = column_sum(total.astype(BF).astype(F32))
            grad = dot_right(low[...], full[...]).astype(BF)

            def split(k):
                for other in range(GROUP):
                    at = (k ^ other) * part
                    piece = grad[:, at : at + part]
                    if other == 0:
                        ours[...] = piece
                    elif other == 1:
                        core[...] = piece
                    else:
                        far_pair[other - 2] = piece

            when_each(s[0], GROUP, split)

        middle_grad, middle_low, grad_own, grad_core, grad_far, gain_two_sum, shift_two_sum, out_sum = step(
            turn_back,
            [row_full, row_low, cell, cell, pair, row_sum, row_sum, row_sum],
            [member],
            [two_own, two_came, two_last, middle, grad_low, whole, out_full],
            micros=3.2, mib=24, name="turn_back",
        )
        back_far = swap(grad_far, "x")
        back_core = swap(grad_core, "c")
        back_last = swap(back_far[1], "c")

        strip = width // wide
        padded = (strip + 15) // 16 * 16

        def out_grad(s, low, values, send, keep):
            total = dot_left(low[...], values[...])

            def split(k):
                for q in range(wide // 2):
                    for core in range(2):
                        target = keep if core == k else send
                        at = (2 * q + core) * strip
                        target[q, :strip] = total[at : at + strip].astype(BF)
                        target[q, strip:] = jnp.zeros((padded - strip, width), BF)

            when_each(s[0], 2, split)

        out_shape = shape_of((wide // 2, padded, width), BF)
        out_send, out_keep = step(
            out_grad, [out_shape, out_shape], [c], [middle_low, context], micros=2, mib=20, name="out_grad"
        )
        out_came = swap(out_send, "c")

        def out_fold(flag, keep, came, span):
            count = keep.shape[0] // 2

            def body(s, kept, arrived, send, keep_out):
                def split(k):
                    for q in range(count):
                        at = q // span * 2 * span + q % span
                        for bit in range(2):
                            target = keep_out if bit == k else send
                            source = at + bit * span
                            target[q] = (kept[source].astype(F32) + arrived[source].astype(F32)).astype(BF)

                when_each(s[0], 2, split)

            out = shape_of((count, padded, width), BF)
            return step(body, [out, out], [flag], [keep, came], micros=1.4, mib=16, name="out_fold")

        head = part // heads

        def attend_back_pair(joined, first, second, lows, name):
            def body(s, source, one, two, low_one, low_two, out):
                for k, (above, low) in enumerate(((one.at[0] if len(one.shape) == 3 else one, low_one), (two, low_two))):
                    attend_back(range(heads), head, length_of(low, rows), source.at[k], above, out.at[k])

            return step(
                body, [joined_shape], [], [joined, first, second, *lows], micros=3.6 * heads / 2, name=name
            )[0]

        joined_grad_near = attend_back_pair(joined_near, grad_own, back_core, tokens_all[:2], "attend_back_near")
        (mlp_sent,) = step(add_far, [row_low], [], [mlp_away, mlp_came], micros=1, mib=10, name="add_mlp")
        mlp_last = swap(mlp_sent, "x")
        down_parts = depth_exchange(down_part([down_came], "down_keep", [back_far]))
        up_came = swap(up_part([], "up_send"), "y")
        joined_grad_far = attend_back_pair(joined_far, back_far, back_last, tokens_all[2:], "attend_back_far")
        out_send, out_keep = out_fold(x, out_keep, out_came, 1)
        out_came = swap(out_send, "x")

        def qkv_grad(s, near_ref, far_ref, grad_near, grad_far, send, keep, sums):
            tall = 2 * rows
            grads = [ref[...].reshape(tall, 3 * part) for ref in (grad_near, grad_far)]
            sums[...] = column_sum(grads[0].astype(F32)) + column_sum(grads[1].astype(F32))
            total = dot_left(near_ref[...].reshape(tall, width), grads[0])
            total = total + dot_left(far_ref[...].reshape(tall, width), grads[1])

            def split(k):
                first_half, second_half = (keep, send) if k == 0 else (send, keep)
                for n in range(depth):
                    at = n * part_depth
                    first_half[n] = total[at : at + half].astype(BF)
                    second_half[n, :rest] = total[at + half : at + part_depth].astype(BF)
                    second_half[n, rest:] = jnp.zeros((half - rest, 3 * part), BF)

            when_each(s[0], 2, split)

        halves = shape_of((depth, half, 3 * part), BF)
        qkv_send, qkv_keep, joined_sums = step(
            qkv_grad,
            [halves, halves, shape_of((1, 3 * part), F32)],
            [y],
            [normed_near, normed_far, joined_grad_near, joined_grad_far],
            mib=32,
            micros=4.5,
            name="qkv_grad",
        )
        qkv_came = swap(qkv_send, "y")

        def one_back(s, near_ref, far_ref, full, own, core, far_out):
            for k in range(GROUP):
                value = dot_right((near_ref, far_ref)[k // 2][k % 2], full[...])
                if k == 0:
                    own[...] = value
                elif k == 2:
                    far_out[...] = value
                else:
                    core[k // 2] = value.astype(BF)

        one_own, one_core, one_far = step(
            one_back, [row_full, row_pair, row_full], [], [joined_grad_near, joined_grad_far, qkv_full],
        )
        one_came = swap(one_core, "c")
        def leave(s, own, came, last, values, vector, out):
            keep = (lax.broadcasted_iota(jnp.int32, (rows, 1), 0) < s[0]).astype(F32)
            fed = own[...] + came[0].astype(F32) + last[...].astype(F32) + vector[7:8]
            out[...] = (keep * (values[...] + fed)).astype(BF)

        (block_out,) = step(
            leave, [row_low], [lengths], [mlp_own, mlp_came, mlp_last, middle, whole], micros=2.5, mib=14, name="leave"
        )

        up_parts = depth_exchange(up_part([up_came], "up_keep"))
        (one_sent,) = step(add_far, [row_low], [], [one_far, one_came], micros=0.7, mib=10, name="add_one")
        one_last = swap(one_sent, "x")

        out_send, out_keep = out_fold(y, out_keep, out_came, 1)
        out_came = swap(out_send, "y")

        def qkv_fold(s, keep, came, out):
            for n in range(depth):
                out[n] = (keep[n].astype(F32) + came[n].astype(F32)).astype(BF)

        (qkv_parts,) = step(qkv_fold, [halves], [], [qkv_keep, qkv_came], micros=1.2, mib=12, name="qkv_fold")
        qkv_parts = depth_exchange(qkv_parts)

        def finish(s, own, came, last, values, vector, middle_ref, out, gain_sum, shift_sum):
            one = own[...] + came[0].astype(F32) + last[...].astype(F32)
            unit, inverse = normal(values[...].astype(F32))
            gain_sum[...] = column_sum(one * unit)
            shift_sum[...] = column_sum(one)
            out[...] = middle_ref[...] + normal_back(one * vector[0:1], unit, inverse)

        input_grad, gain_one_sum, shift_one_sum = step(
            finish, [row_full, row_sum, row_sum], [],
            [one_own, one_came, one_last, tokens, whole, middle_grad], micros=3.6, mib=16, name="finish",
        )

        def vector_pack(s, gain_one, shift_one, out_ref, gain_two, shift_two, down_ref, up_ref, joined, packed, line):
            packed[...] = jnp.zeros(packed.shape, F32)
            line[...] = jnp.zeros(line.shape, F32)
            for k, ref in ((0, gain_one), (1, shift_one), (4, out_ref), (5, gain_two), (6, shift_two), (7, down_ref)):
                line[k : k + 1] = ref[...]

            def of_member(m):
                line[2:3, m * part : (m + 1) * part] = joined[:, :part]
                line[3:4, m * part : (m + 1) * part] = joined[:, 2 * part :]
                for n in range(depth):
                    packed[n, 8 + m : 9 + m] = up_ref[:, n * block : (n + 1) * block]

            when_each(s[0], GROUP, of_member)
            for n in range(depth):
                packed[n, :8] = line[:, n * part_depth : (n + 1) * part_depth]

        (packed,) = step(
            vector_pack,
            [shape_of((depth, 8 + GROUP, part_depth), F32)],
            [member],
            [gain_one_sum, shift_one_sum, out_sum, gain_two_sum, shift_two_sum, down_sum, up_sums, joined_sums],
            scratch=[pltpu.VMEM((8, width), F32)],
            micros=0.6, mib=8, name="vector_pack",
        )

        def vector_hops(packed):
            def add(s, one, two, out):
                out[...] = one[...] + two[...]

            spans = [1 << k for k in range(depth.bit_length() - 1)]
            hops = ["c", "x", "y", *spans]
            for k, hop in enumerate(hops):
                if isinstance(hop, str):
                    came = swap(packed, hop)
                else:
                    came = lax.ppermute(packed, "z", [(i, i ^ hop) for i in range(depth)])
                yield packed
                (packed,) = step(add, [shape_of(packed.shape, F32)], [], [packed, came], micros=0.5, mib=8, name="vector_add")
            yield packed

        hops = vector_hops(packed)
        next(hops)

        low_type = BF if outer == 1 else F32

        def feed_pieces(s, down_ref, up_ref, out):
            out[0] = sum_of(down_ref).astype(low_type)
            out[1] = sum_of(up_ref).astype(low_type)

        (feed_piece,) = step(
            feed_pieces, [shape_of((2, fold_rows, 2 * outer * each), low_type)], [], [down_parts, up_parts], micros=2.2,
            mib=16, name="feed_pieces",
        )
        if outer > 1:
            feed_piece = feed_piece.reshape(2, fold_rows, 2, outer, each)
            feed_piece = lax.psum_scatter(feed_piece, "o", scatter_dimension=3, tiled=False).astype(BF)
            feed_piece = feed_piece.reshape(2, fold_rows, 2 * each)
        feed_all = group_gather(feed_piece)
        next(hops)

        next(hops)

        ratio = wide // depth
        fold = GROUP // ratio

        def feed_grads(s, *refs):
            blocks, (down_out, up_out) = refs[:4], refs[4:]

            def of_member(k):
                for m in range(GROUP):
                    at, to = k * (side // GROUP), m * block
                    ref, span = blocks[k ^ m], side // GROUP
                    down_out[to : to + fold_rows] = ref[0, :, at : at + span].astype(F32)
                    down_out[to + fold_rows : to + block] = ref[0, :fold_rest, side + at : side + at + span].astype(F32)
                for f in range(fold):
                    source = k % ratio * fold + f
                    at = k // ratio * block
                    ref, to = blocks[k ^ source], slice(f * block, (f + 1) * block)
                    up_out[:fold_rows, to] = ref[1, :, at : at + block].astype(F32)
                    up_out[fold_rows:, to] = ref[1, :fold_rest, each + at : each + at + block].astype(F32)

            when_each(s[0], GROUP, of_member)

        down_weight_grad, up_weight_grad = step(
            feed_grads,
            [shape_of((hidden_depth, side // GROUP), F32), shape_of((part_depth, fold * block), F32)],
            [member],
            feed_all,
            micros=2.9, mib=12, name="feed_grads",
        )

        def out_split(s, keep, came, out):
            for q in range(outer):
                total = keep[q].astype(F32) + came[q].astype(F32)
                for n in range(depth):
                    out[n, q] = total[:, n * part_depth : (n + 1) * part_depth].astype(BF)

        (out_parts,) = step(
            out_split, [shape_of((depth, outer, padded, part_depth), BF)], [], [out_keep, out_came], micros=1, mib=8,
            name="out_split",
        )
        out_parts = depth_exchange(out_parts)
        next(hops)

        def qkv_sum(s, parts, out):
            out[...] = sum_of(parts).astype(BF)

        (qkv_piece,) = step(qkv_sum, [shape_of((half, 3 * part), BF)], [], [qkv_parts], micros=1, mib=8, name="qkv_sum")
        qkv_all = group_gather(qkv_piece)
        packed = list(hops)[-1]
        span = 3 * width // wide

        def qkv_columns(s, *refs):
            blocks, (keep, send) = refs[:4], refs[4:]

            def of_member(k):
                for o in range(outer):
                    for side_at in range(2):
                        cut, at = [], ((2 * o + side_at) * GROUP + k) * span
                        stop = at + span
                        while at < stop:
                            to = min(stop, (at // part + 1) * part)
                            p, m = divmod(at // part, GROUP)
                            low = p * part + at % part
                            cut.append(blocks[k ^ m][:, low : low + to - at])
                            at = to
                        found = cut[0] if len(cut) == 1 else jnp.concatenate(cut, axis=1)

                        def put(here, found=found, side_at=side_at, o=o):
                            target = keep if here == side_at else send
                            target[o] = found

                        when_each(s[1], 2, put)

            when_each(s[0], GROUP, of_member)

        span_shape = shape_of((outer, half, span), BF)
        qkv_keep, qkv_send = step(
            qkv_columns, [span_shape, span_shape], [member, y], qkv_all, micros=1, mib=8, name="qkv_columns"
        )
        if outer > 1:
            qkv_keep, qkv_send = (
                lax.psum_scatter(v.astype(F32), "o", scatter_dimension=0, tiled=True).astype(BF)
                for v in (qkv_keep, qkv_send)
            )
        qkv_came = swap(qkv_send, "y")

        def out_last(s, parts, out):
            out[...] = sum_of(parts)[:, :strip]

        (out_sums,) = step(out_last, [shape_of((outer, strip, part_depth), F32)], [], [out_parts], micros=0.7, mib=8, name="out_last")
        out_sums = out_sums[0] if outer == 1 else lax.psum_scatter(out_sums, "o", scatter_dimension=0, tiled=False)
        out_weight_grad = out_sums.T

        def qkv_rows(s, keep, came, out):
            def put(k):
                top, bottom = (keep, came) if k == 0 else (came, keep)
                out[:half] = top[0].astype(F32)
                out[half:] = bottom[0, :rest].astype(F32)

            when_each(s[0], 2, put)

        (qkv_weight_grad,) = step(
            qkv_rows, [shape_of((part_depth, span), F32)], [y], [qkv_keep, qkv_came], micros=0.8, mib=8, name="qkv_rows"
        )
        packed = lax.dynamic_index_in_dim(packed, z[0], 0, keepdims=False)
        if outer > 1:
            packed = lax.psum(packed, "o")
        return (
            block_out, input_grad, packed[0], packed[1], qkv_weight_grad, packed[2], packed[3], out_weight_grad,
            packed[4], packed[5], packed[6], up_weight_grad, packed[8:].reshape(hidden_depth), down_weight_grad, packed[7],
        )

    return shards


def solution(mesh):
    wide, depth = mesh.shape["wide"], mesh.shape["narrow"]
    outer = wide // 8
    fine = Mesh(mesh.devices.reshape(outer, 2, 2, 2, depth), AXES)
    rows, vec, mat = P(AXES, None), P("z"), P("z", None)
    placed = (
        rows, P(AXES), vec, vec, mat, vec, vec, mat, vec, vec, vec, mat, vec, mat, vec, rows,
    )
    grad = P("z", WIDE)
    return jax.shard_map(
        build(outer, depth),
        mesh=fine,
        in_specs=placed,
        out_specs=(rows, rows, vec, vec, grad, vec, vec, grad, vec, vec, vec, grad, vec, grad, vec),
        check_vma=False,
    )
```

```python
import functools

import jax
import jax.numpy as jnp
from jax import lax
from jax.experimental import pallas as pl
from jax.experimental.pallas import tpu as pltpu
from jax.sharding import Mesh, PartitionSpec as P

HEADS = 20
EPSILON = 1e-05
FILL = -1000000000.0
BF = jnp.bfloat16
F32 = jnp.float32
AXES = ("o", "y", "x", "c", "z")
WIDE = ("o", "y", "x", "c")
SWAP = [(0, 1), (1, 0)]
GROUP = 4
MIB = 1024 * 1024
PER_MICRO = 5e8
PLAN = (
    (1, 2, 0),
    (0, 0.4, 0),
    (2, 0.037, 0),
    (4, 1.5, 0),
    (3, 0.15, 0),
    (5, 0.45, 1),
    (6, 0.45, 0),
    (7, 0.36, 4),
    (8, 0.78, 1),
    (9, 0.45, 0),
    (10, 2.7, 0),
    (11, 4.5, 1),
    (12, 3, 0),
    (14, 0.188, 0),
    (13, 4, 1),
    (15, 5.4, 0),
    (16, 25, 0),
    (17, 21, 0),
    (20, 32, 0),
    (19, 0.525, 0),
    (18, 3, 0),
    (26, 12, 0),
    (21, 2, 0),
    (22, 0.25, 0),
    (23, 18, 0),
    (25, 0.05, 1),
    (24, 1, 0),
    (27, 9, 0),
    (31, 0.6, 0),
    (29, 32, 0),
    (30, 1.41, 0),
    (28, 1.68, 0),
    (32, 9.6, 0),
    (33, 4.8, 0),
    (34, 0.08, 0),
    (35, 32, 0),
    (36, 3.6, 0),
    (37, 0.6, 0),
    (38, 2.2, 0),
    (39, 2, 0),
    (40, 0.5, 0),
    (41, 2.9, 0),
    (42, 0.7, 0),
    (43, 0.35, 0),
    (44, 2.8, 0),
    (47, 0.7, 0),
    (45, 0.35, 0),
    (46, 0.1, 0),
    (48, 0.7, 0),
    (49, 16, 0),
)


class Later:
    def __init__(self, function, *values):
        self.function, self.values, self.found = function, values, None

    def get(self):
        if self.found is None:
            self.found = self.function(*(now(v) for v in self.values))
        return self.found

    def __getitem__(self, key):
        return Later(lambda v: v[key], self)


def now(value):
    return value.get() if isinstance(value, Later) else value


def send(value, axis, pairs):
    return Later(lambda v: lax.ppermute(v, axis, pairs), value)


def swap(value, axis):
    return send(value, axis, SWAP)


def dot(first, second):
    return jnp.dot(first, second, preferred_element_type=F32)


def dot_left(first, second):
    return lax.dot_general(first, second, (((0,), (0,)), ((), ())), preferred_element_type=F32)


def dot_right(first, second):
    return lax.dot_general(first, second, (((1,), (1,)), ((), ())), preferred_element_type=F32)


def shape_of(dims, dtype):
    return jax.ShapeDtypeStruct(dims, dtype)


class Order:
    def __init__(self):
        self.steps = []

    def __call__(self, body, outs, scalars, arrays, after=(), pins=-1, scratch=(), mib=28, micros=1.0, name=None):
        given = {}
        self.steps.append((body, outs, scalars, arrays, list(after), scratch, mib, micros, name, given, pins))
        return [Later(lambda k=k: given[k]) for k in range(len(outs))]

    def run(self, plan):
        if len(plan) != len(self.steps):
            plan = [(k, entry[7], entry[10]) for k, entry in enumerate(self.steps)]
        token = []
        for k, micros, pins in plan:
            body, outs, scalars, arrays, after, scratch, mib, _, name, given, _ = self.steps[k]
            after = [v for bit, v in enumerate(after) if pins >> bit & 1]
            *found, last = call_step(body, outs, scalars, arrays, after + token, scratch, mib, micros, name)
            token = [last]
            given.update(enumerate(found))


def call_step(body, outs, scalars, arrays, after, scratch, mib, micros, name):
    n_scalar, n_array, n_out = len(scalars), len(arrays), len(outs)

    def run(*refs):
        token = refs[n_scalar + n_array + len(after) + n_out]
        values = tuple(ref[0] for ref in refs[:n_scalar])
        rest = refs[n_scalar + n_array + len(after) :]
        token[...] = jnp.zeros(token.shape, F32)
        body(values, *refs[n_scalar : n_scalar + n_array], *rest[:n_out], *rest[n_out + 1 :])

    return pl.pallas_call(
        run,
        out_shape=(*outs, shape_of((8, 128), F32)),
        in_specs=[pl.BlockSpec(memory_space=pltpu.SMEM)] * n_scalar
        + [pl.BlockSpec(memory_space=pltpu.VMEM)] * n_array
        + [pl.BlockSpec(memory_space=pl.ANY)] * len(after),
        out_specs=(pl.BlockSpec(memory_space=pltpu.VMEM),) * (n_out + 1),
        scratch_shapes=list(scratch),
        compiler_params=pltpu.CompilerParams(vmem_limit_bytes=mib * MIB),
        cost_estimate=pl.CostEstimate(flops=int(micros * PER_MICRO), bytes_accessed=1024, transcendentals=0),
        name=name,
    )(*(now(v) for v in (*scalars, *arrays, *after)))


def group_gather(value):
    over_x = swap(value, "x")
    over_core = swap(value, "c")
    return [value, over_core, over_x, swap(over_x, "c")]


def depth_shift(value, shift, count):
    return send(value, "z", [(i, (i + shift) % count) for i in range(count)])


def depth_line(value, count):
    up, down = [], []
    for s in range(count - 1):
        up.append(send(up[-1] if s else value, "z", [(i, i + 1) for i in range(s, count - 1)]))
        down.append(send(down[-1] if s else value, "z", [(i, i - 1) for i in range(1, count - s)]))
    return up, down


def next_block(z, step, count):
    return z + 1 + step if step < count - 1 - z else count - 2 - step


def line_ref(z, other, up, down):
    return up[z - 1 - other] if other < z else down[other - z - 1]


def depth_exchange(parts):
    return Later(lambda v: lax.all_to_all(v, "z", 0, 0), parts)


def sum_of(refs):
    total = refs[0].astype(F32)
    for k in range(1, refs.shape[0]):
        total = total + refs[k].astype(F32)
    return total


def normal(values):
    center = values - jnp.mean(values, axis=-1, keepdims=True)
    spread = jnp.mean(center * center, axis=-1, keepdims=True)
    inverse = lax.rsqrt(spread + EPSILON)
    return center * inverse, inverse


def normal_back(grad, unit, inverse):
    return (
        grad
        - jnp.mean(grad, axis=-1, keepdims=True)
        - unit * jnp.mean(grad * unit, axis=-1, keepdims=True)
    ) * inverse


def when_each(index, count, step):
    for k in range(count):
        pl.when(index == k)(functools.partial(step, k))


def allowed_of(rows, length):
    query = lax.broadcasted_iota(jnp.int32, (rows, rows), 0)
    key = lax.broadcasted_iota(jnp.int32, (rows, rows), 1)
    return (key <= query) & (key < length)


def length_of(payload, rows):
    high = payload[rows : rows + 1, 0:1].astype(F32)
    low = payload[rows : rows + 1, 128:129].astype(F32)
    return (high * 16.0 + low).astype(jnp.int32)


def head_probs(query, key, allowed, scale):
    scores = jnp.where(allowed, dot_right(query, key) * scale, FILL)
    weights = jnp.exp(scores - jnp.max(scores, axis=1, keepdims=True))
    return weights * (1.0 / jnp.sum(weights, axis=1, keepdims=True))


def attend(heads, tokens, full, vectors, query_shift, value_shift, normed, joined, contexts):
    rows, part = normed.shape[1], full.shape[1] // 3
    head = part // heads
    scale = head ** (-0.5)
    for n, x in enumerate(tokens):
        normed[n] = (normal(x[:rows].astype(F32))[0] * vectors[0:1] + vectors[1:2]).astype(BF)
        sums = dot(normed[n], full[...])
        query = (sums[:, :part] + query_shift[...]).astype(BF)
        key = sums[:, part : 2 * part].astype(BF)
        value = (sums[:, 2 * part :] + value_shift[...]).astype(BF)
        joined[n, :, :part] = query
        joined[n, :, part : 2 * part] = key
        joined[n, :, 2 * part :] = value
        allowed = allowed_of(rows, length_of(x, rows))
        out = []
        for h in range(heads):
            cut = slice(h * head, (h + 1) * head)
            probs = head_probs(query[:, cut], key[:, cut], allowed, scale).astype(BF)
            out.append(dot(probs, value[:, cut]))
        contexts[n][...] = jnp.concatenate(out, axis=1).astype(BF)


def attend_back(chosen, head, length, joined, above, out):
    rows, part = above.shape
    scale = head ** (-0.5)
    allowed = allowed_of(rows, length)
    found = ([], [], [])
    for h in chosen:
        q, k, v = (joined[:, p * part + h * head : p * part + (h + 1) * head] for p in range(3))
        g = above[:, h * head : (h + 1) * head]
        probs = head_probs(q, k, allowed, scale)
        probs_grad = dot_right(g, v)
        found[2].append(dot_left(probs.astype(BF), g))
        score = probs * (probs_grad - jnp.sum(probs * probs_grad, axis=1, keepdims=True))
        score = score.astype(BF)
        found[0].append(dot(score, k) * scale)
        found[1].append(dot_left(score, q) * scale)
    out[...] = jnp.concatenate(found[0] + found[1] + found[2], axis=1).astype(BF)


def gelu_both(values):
    root = (2.0 / jnp.pi) ** 0.5
    square = values * values
    bend = jnp.tanh(root * (values + 0.044715 * (square * values)))
    half = 0.5 * (1.0 + bend)
    slope = half + 0.5 * values * (1.0 - bend * bend) * (root * (1.0 + 3.0 * 0.044715 * square))
    return values * half, slope


def column_sum(values):
    return jnp.sum(values, axis=0, keepdims=True)


def build(outer, depth):
    def shards(
        tokens, lengths, norm1_gain, norm1_bias, qkv_weight, query_bias, value_bias, out_weight,
        out_bias, norm2_gain, norm2_bias, up_weight, up_bias, down_weight, down_bias, cotangent,
    ):
        rows, width = tokens.shape
        heads = HEADS // GROUP
        part = width // GROUP
        part_depth = width // depth
        hidden_depth = up_weight.shape[1] // depth
        block = hidden_depth // GROUP
        mine = depth * block
        wide = outer * 2 * GROUP
        sides = outer * 2
        y, x, c, z = (lax.axis_index(name).astype(jnp.int32).reshape(1) for name in ("y", "x", "c", "z"))
        member = 2 * x + c
        others = range(1, depth)
        step = Order()

        row_low, row_full = shape_of((rows, width), BF), shape_of((rows, width), F32)
        row_pair = shape_of((2, rows, width), BF)
        row_sum = shape_of((1, width), F32)
        cell, pair = shape_of((rows, part), BF), shape_of((2, rows, part), BF)

        def take_rows(s, values, out):
            out[:rows] = values[...]
            lane = lax.broadcasted_iota(jnp.int32, (16, width), 1)
            out[rows:] = jnp.where(lane < 128, s[0] // 16, s[0] % 16).astype(F32).astype(BF)

        (tokens_low,) = step(
            take_rows, [shape_of((rows + 16, width), BF)], [lengths], [tokens], micros=0.8, mib=10, name="take_rows"
        )
        tokens_all = group_gather(tokens_low)

        half = (part_depth // 2 + 15) // 16 * 16
        rest = part_depth - half
        quad_shape, half_shape = shape_of((part_depth, 4 * part), BF), shape_of((half, 4 * part), BF)
        biases = (norm1_gain, norm1_bias, query_bias, value_bias, out_bias, norm2_gain, norm2_bias, down_bias, up_bias)

        def take_quad(s, qkv, out, own, send):
            def columns(k):
                for p in range(3):
                    at = (p * GROUP + k) * part
                    own[:, p * part : (p + 1) * part] = qkv[:, at : at + part]
                own[:, 3 * part :] = out[:, k * part : (k + 1) * part]

            when_each(s[0], GROUP, columns)

            @pl.when(s[1] == 0)
            def _():
                send[...] = own[:half]

            @pl.when(s[1] == 1)
            def _():
                send[:rest] = own[half:]
                send[rest:] = jnp.zeros((half - rest, 4 * part), BF)

        quad_own, quad_half = step(
            take_quad, [quad_shape, half_shape], [member, y], [qkv_weight, out_weight], micros=0.5, mib=12, name="take_quad"
        )
        quad_up, quad_down = depth_line(quad_half, depth)

        def take_vectors(s, *refs):
            found = [ref[...].astype(F32).reshape(1, part_depth) for ref in refs[:8]]
            more = [refs[8][k * block : (k + 1) * block].astype(F32).reshape(1, block) for k in range(GROUP)]
            refs[9][...] = jnp.zeros(refs[9].shape, F32)
            refs[9][:8, :part_depth] = jnp.concatenate(found, axis=0)
            refs[9][:GROUP, part_depth : 2 * part_depth] = jnp.concatenate(more, axis=0)

        (lines_own,) = step(
            take_vectors, [shape_of((8, 2 * part_depth), F32)], [], biases, micros=0.5, mib=8, name="take_vectors"
        )
        lines_all = [lines_own] + [depth_shift(lines_own, r, depth) for r in others]

        def live(s, values, low, sums):
            keep = (lax.broadcasted_iota(jnp.int32, (rows, 1), 0) < s[0]).astype(F32)
            kept = values[...].astype(F32) * keep
            low[...] = kept.astype(BF)
            sums[...] = column_sum(kept)

        grad_low, down_sum = step(live, [row_low, row_sum], [lengths], [cotangent], micros=0.5, mib=10, name="live")
        grad_all = group_gather(grad_low)

        def hand_on(up, down, like, after=False):
            came = []
            for s_at in others:

                def choose_block(s, *refs, at=s_at - 1):
                    ups, downs, out = refs[: at + 1], refs[at + 1 : -1], refs[-1]

                    def copy(k):
                        out[...] = line_ref(k, next_block(k, at, depth), ups, downs)[...]

                    when_each(s[0], depth, copy)

                (block_now,) = step(
                    choose_block, [like], [z], [*up[:s_at], *down[:s_at]], after=came[-1:], pins=int(after), micros=1.5, mib=8, name="hand_on"
                )
                came.append(swap(block_now, "y"))
                yield came

        quad_far = list(hand_on(quad_up, quad_down, half_shape))[-1]

        turn_shape = shape_of((part_depth, mine), BF)

        def take_mlp(s, up, down, up_own, turn):
            def part_of(k):
                for n in range(depth):
                    at = n * hidden_depth + k * block
                    up_own[:, n * block : (n + 1) * block] = up[:, at : at + block]

                @pl.when(s[1] == 1)
                def _():
                    turn[...] = down[k * block : (k + 1) * block]

            when_each(s[0], GROUP, part_of)

            @pl.when(s[1] == 0)
            def _():
                turn[...] = up_own[...]

        up_own, turn = step(
            take_mlp, [turn_shape, turn_shape], [member, y], [up_weight, down_weight], after=[quad_up[-1], quad_down[-1], *quad_far], pins=3, micros=1.2, mib=20,
            name="take_mlp",
        )
        mlp_up, mlp_down = depth_line(turn, depth)
        mlp_far_steps = hand_on(mlp_up, mlp_down, turn_shape, True)

        lines = depth - 1

        def assemble(s, own, *refs):
            blocks, refs = refs[:depth], refs[depth:]
            ups, downs, handed = refs[:lines], refs[lines : 2 * lines], refs[2 * lines : 3 * lines]
            full, out_cols, whole, query_shift, value_shift, up_shift = refs[3 * lines :]

            def put_vectors(at, values):
                whole[:, at * part_depth : (at + 1) * part_depth] = values[:, :part_depth]

                def of_member(m):
                    up_shift[:, at * block : (at + 1) * block] = values[m : m + 1, part_depth : 2 * part_depth]

                when_each(s[2], GROUP, of_member)

            def put(k):
                full[k * part_depth : (k + 1) * part_depth] = own[:, : 3 * part]
                out_cols[:, k * part : (k + 1) * part] = own[:, 3 * part :]
                for r in range(depth):
                    put_vectors((k - r) % depth, blocks[r][...])
                for at in range(lines):
                    other = next_block(k, at, depth)
                    low, cols = other * part_depth, slice(other * part, (other + 1) * part)

                    def both(side, at=at, low=low, cols=cols, other=other):
                        ours = line_ref(k, other, ups, downs)
                        top, bottom = (ours, handed[at]) if side == 0 else (handed[at], ours)
                        full[low : low + half] = top[:, : 3 * part]
                        full[low + half : low + part_depth] = bottom[:rest, : 3 * part]
                        out_cols[:half, cols] = top[:, 3 * part :]
                        out_cols[half:, cols] = bottom[:rest, 3 * part :]

                    when_each(s[1], 2, both)

            when_each(s[0], depth, put)

            def of_member(m):
                query_shift[...] = whole[2:3, m * part : (m + 1) * part]
                value_shift[...] = whole[3:4, m * part : (m + 1) * part]

            when_each(s[2], GROUP, of_member)

        shift_shape = shape_of((1, part), F32)
        qkv_full, out_part, whole, query_shift, value_shift, up_shift = step(
            assemble,
            [shape_of((width, 3 * part), BF), shape_of((part_depth, depth * part), BF), shape_of((8, width), F32), shift_shape,
             shift_shape, shape_of((1, mine), F32)],
            [z, y, member],
            [quad_own, *lines_all, *quad_up, *quad_down, *quad_far],
            after=[grad_all[2], grad_all[3], grad_all[1]],
            pins=1,
            micros=1.3, mib=16, name="assemble",
        )
        out_all = group_gather(out_part)
        next(mlp_far_steps)


        def attend_far(s, full, vector, first, second, shift_q, shift_v, normed, joined, context):
            attend(heads, (first, second), full, vector, shift_q, shift_v, normed, joined,
                   (context.at[0], context.at[1]))

        joined_shape = shape_of((2, rows, 3 * part), BF)
        normed_far, joined_far, context_far = step(
            attend_far,
            [row_pair, joined_shape, pair],
            [],
            [qkv_full, whole, tokens_all[2], tokens_all[3], query_shift, value_shift],
            micros=9, mib=20, name="attend_far",
        )
        came_far = swap(context_far, "x")
        next(mlp_far_steps)

        def attend_near(s, full, vector, first, second, shift_q, shift_v, normed, joined, ours, theirs):
            attend(heads, (first, second), full, vector, shift_q, shift_v, normed, joined,
                   (ours, theirs))

        normed_near, joined_near, context_own, context_core = step(
            attend_near,
            [row_pair, joined_shape, cell, cell],
            [],
            [qkv_full, whole, tokens_all[0], tokens_all[1], query_shift, value_shift],
            micros=9, mib=20, name="attend_near",
        )
        came_core = swap(context_core, "c")
        came_last = swap(came_far[1], "c")

        mlp_far = list(mlp_far_steps)[-1]

        def out_whole(s, *refs):
            blocks, full = refs[:-1], refs[-1]

            def put(k):
                for other in range(GROUP):
                    at = (k ^ other) * part
                    for n in range(depth):
                        rows_of = slice(n * part_depth, (n + 1) * part_depth)
                        full[rows_of, at : at + part] = blocks[other][:, n * part : (n + 1) * part]

            when_each(s[0], GROUP, put)

        (out_full,) = step(out_whole, [shape_of((width, width), BF)], [member], out_all, micros=1, mib=12, name="out_whole")

        def project(s, own, core, far_pair, last, full, values, vector, context, middle, normed):
            def put(k):
                for other, ref in enumerate((own, core, None, last)):
                    at = (k ^ other) * part
                    context[:, at : at + part] = far_pair[0] if ref is None else ref[...]

            when_each(s[0], GROUP, put)
            total = values[...].astype(F32) + (dot(context[...], full[...]) + vector[4:5])
            middle[...] = total
            normed[...] = (normal(total)[0] * vector[5:6] + vector[6:7]).astype(BF)

        context, middle, normed_two = step(
            project,
            [row_low, row_full, row_low],
            [member],
            [context_own, came_core, came_far, came_last, out_full, tokens, whole],
            micros=3.6, mib=20, name="project",
        )
        normed_two_all = group_gather(normed_two)

        def feed_cells(cells, normed, grads, up_full, down_full, shift, active, before, sums, two_low, two):
            total = jnp.zeros((1, mine), F32)
            for k in cells:
                at = slice(k * rows, (k + 1) * rows)
                value, slope = gelu_both(dot(normed[k][...], up_full[...]) + shift[...])
                active[at] = value.astype(BF)
                grad = (dot_right(grads[k][...], down_full[...]) * slope).astype(BF)
                before[at] = grad
                total = total + column_sum(grad.astype(F32))
                found = dot_right(grad, up_full[...])
                if k == 0:
                    two[...] = found
                else:
                    two_low[...] = found.astype(BF)
            sums[...] = total

        def feed_near(s, up_ref, down_ref, *refs):
            ups, downs, handed = refs[:lines], refs[lines : 2 * lines], refs[2 * lines : 3 * lines]
            refs = refs[3 * lines :]
            normed, grads, shift, (up_full, down_full, *outs) = refs[:2], refs[2:4], refs[4], refs[5:]

            def put(k):
                up_full[k * part_depth : (k + 1) * part_depth] = up_ref[...]

                def of_member(m):
                    down_full[k * block : (k + 1) * block] = down_ref[m * block : (m + 1) * block]

                when_each(s[2], GROUP, of_member)
                for at in range(lines):
                    other = next_block(k, at, depth)

                    def both(side, at=at, other=other):
                        ours = line_ref(k, other, ups, downs)
                        up_from, down_from = (ours, handed[at]) if side == 0 else (handed[at], ours)
                        up_full[other * part_depth : (other + 1) * part_depth] = up_from[...]
                        down_full[other * block : (other + 1) * block] = down_from[...]

                    when_each(s[1], 2, both)

            when_each(s[0], depth, put)
            feed_cells((1, 0), normed, grads, up_full, down_full, shift, *outs)

        hidden_rows, hidden_sum = shape_of((2 * rows, mine), BF), shape_of((1, mine), F32)
        up_full, down_full, active_near, before_near, up_sums_near, two_core, two_own = step(
            feed_near,
            [shape_of((width, mine), BF), shape_of((mine, width), BF), hidden_rows, hidden_rows, hidden_sum, row_low, row_full],
            [z, y, member],
            [up_own, down_weight, *mlp_up, *mlp_down, *mlp_far, *normed_two_all[:2], *grad_all[:2], up_shift],
            mib=40,
            micros=12.5, name="feed_near",
        )
        two_came = swap(two_core, "c")

        def feed_far(s, up_full, down_full, *refs):
            feed_cells((1, 0), refs[:2], refs[2:4], up_full, down_full, *refs[4:])

        active_far, before_far, up_sums_far, two_next, two_far = step(
            feed_far,
            [hidden_rows, hidden_rows, hidden_sum, row_low, row_full],
            [],
            [up_full, down_full, *normed_two_all[2:], *grad_all[2:], up_shift],
            mib=36,
            micros=10.5, name="feed_far",
        )
        next_came = swap(two_next, "c")
        active, before = [active_near, active_far], [before_near, before_far]

        each, side = mine // sides, width // sides

        def columns_for(value, count, index):
            cut = [value[:, (2 * o + index) * count : (2 * o + index + 1) * count] for o in range(outer)]
            return cut[0] if outer == 1 else jnp.concatenate(cut, axis=1)

        tall = max(block, part_depth)
        fold_rows = (tall // 2 + 15) // 16 * 16
        fold_rest = tall - fold_rows
        pack_shape = shape_of((depth, fold_rows, 2 * outer * each), BF)
        feed_scratch = [pltpu.VMEM((GROUP * rows, width), BF), pltpu.VMEM((GROUP * rows, outer * each), BF)]

        def store_rows(total, came, out):
            cut = total.shape[1]
            for n in range(depth):
                top = total[n * tall : n * tall + fold_rows]
                low = total[n * tall + fold_rows : (n + 1) * tall]
                if came is not None:
                    top = top + came[n, :, :cut].astype(F32)
                    low = low + came[n, :fold_rest, cut:].astype(F32)
                out[n, :, :cut] = top.astype(BF)
                out[n, :fold_rest, cut:] = low.astype(BF)
                out[n, fold_rest:, cut:] = jnp.zeros((fold_rows - fold_rest, cut), BF)

        def down_product(grads, right_all, index):
            for k, ref in enumerate(grads):
                right_all[k * rows : (k + 1) * rows] = columns_for(ref[...], side, index)

        def up_product(befores, right_all, index):
            for k, ref in enumerate(befores):
                right_all[2 * k * rows : 2 * (k + 1) * rows] = columns_for(ref[...], each, index)

        def feed_part(product, arrays, scratch, came, name, after=()):
            n_array, n_came = len(arrays), len(came)

            def body(s, *refs):
                inputs, came_refs, (out, *left_refs, right_all) = (
                    refs[:n_array], refs[n_array : n_array + n_came], refs[n_array + n_came :]
                )
                when_each(s[0], 2, lambda k: product(inputs, right_all, k if n_came else 1 - k))
                if left_refs:
                    for k in range(GROUP):
                        left_refs[0][k * rows : (k + 1) * rows] = inputs[2 + k][...]
                    total = dot_left(left_refs[0][...], right_all[...])
                else:
                    total = dot_left(inputs[0][...], right_all[: 2 * rows]) + dot_left(inputs[1][...], right_all[2 * rows :])
                store_rows(total, came_refs[0] if n_came else None, out)

            return step(
                body, [pack_shape], [y], [*arrays, *came], after=after, scratch=scratch, mib=32, micros=4, name=name
            )[0]

        def down_part(came, name, after=()):
            return feed_part(
                lambda refs, right, k: down_product(refs[2:], right, k),
                [*active, *grad_all], feed_scratch[1:], came, name, after,
            )

        def up_part(came, name, after=()):
            return feed_part(
                lambda refs, right, k: up_product(refs[:2], right, k),
                [*before, *normed_two_all], feed_scratch, came, name, after,
            )

        down_came = swap(down_part([], "down_send"), "y")

        def add_far(s, far, came, out):
            out[...] = (far[...] + came[1].astype(F32)).astype(BF)

        def add_two(s, far, came, out):
            out[...] = (far[...] + came[...].astype(F32)).astype(BF)

        (two_sent,) = step(add_two, [row_low], [], [two_far, next_came], micros=0.7, mib=10, name="add_two")
        two_last = swap(two_sent, "x")

        def feed_out(s, near_ref, far_ref, full, own, core, far_out):
            for k in range(GROUP):
                value = dot((near_ref, far_ref)[k // 2][k % 2 * rows : (k % 2 + 1) * rows], full[...])
                if k == 0:
                    own[...] = value
                elif k == 2:
                    far_out[...] = value
                else:
                    core[k // 2] = value.astype(BF)

        mlp_own, mlp_core, mlp_away = step(
            feed_out, [row_full, row_pair, row_full], [], [*active, down_full], micros=4.5, mib=24, name="feed_out",
        )
        mlp_came = swap(mlp_core, "c")

        def turn_back(
            s, own, came, last, values, grads, vector, full,
            middle_grad, low, ours, core, far_pair, gain_sum, shift_sum, out_sum,
        ):
            two = own[...] + came[...].astype(F32) + last[...].astype(F32)
            unit, inverse = normal(values[...])
            gain_sum[...] = column_sum(two * unit)
            shift_sum[...] = column_sum(two)
            total = grads[...].astype(F32) + normal_back(two * vector[5:6], unit, inverse)
            middle_grad[...] = total
            low[...] = total.astype(BF)
            out_sum[...] = column_sum(total.astype(BF).astype(F32))
            grad = dot_right(low[...], full[...]).astype(BF)

            def split(k):
                for other in range(GROUP):
                    at = (k ^ other) * part
                    piece = grad[:, at : at + part]
                    if other == 0:
                        ours[...] = piece
                    elif other == 1:
                        core[...] = piece
                    else:
                        far_pair[other - 2] = piece

            when_each(s[0], GROUP, split)

        middle_grad, middle_low, grad_own, grad_core, grad_far, gain_two_sum, shift_two_sum, out_sum = step(
            turn_back,
            [row_full, row_low, cell, cell, pair, row_sum, row_sum, row_sum],
            [member],
            [two_own, two_came, two_last, middle, grad_low, whole, out_full],
            micros=3.2, mib=24, name="turn_back",
        )
        back_far = swap(grad_far, "x")
        back_core = swap(grad_core, "c")
        back_last = swap(back_far[1], "c")

        strip = width // wide
        padded = (strip + 15) // 16 * 16

        def out_grad(s, low, values, send, keep):
            total = dot_left(low[...], values[...])

            def split(k):
                for q in range(wide // 2):
                    for core in range(2):
                        target = keep if core == k else send
                        at = (2 * q + core) * strip
                        target[q, :strip] = total[at : at + strip].astype(BF)
                        target[q, strip:] = jnp.zeros((padded - strip, width), BF)

            when_each(s[0], 2, split)

        out_shape = shape_of((wide // 2, padded, width), BF)
        out_send, out_keep = step(
            out_grad, [out_shape, out_shape], [c], [middle_low, context], micros=2, mib=20, name="out_grad"
        )
        out_came = swap(out_send, "c")

        def out_fold(flag, keep, came, count):
            span = 1

            def body(s, kept, arrived, send, keep_out):
                def split(k):
                    for q in range(count):
                        at = q // span * 2 * span + q % span
                        for bit in range(2):
                            target = keep_out if bit == k else send
                            source = at + bit * span
                            target[q] = (kept[source].astype(F32) + arrived[source].astype(F32)).astype(BF)

                when_each(s[0], 2, split)

            out = shape_of((count, padded, width), BF)
            return step(body, [out, out], [flag], [keep, came], micros=1.4, mib=16, name="out_fold")

        head = part // heads

        def attend_back_pair(joined, first, second, lows, name):
            def body(s, source, one, two, low_one, low_two, out):
                for k, (above, low) in enumerate(((one.at[0] if len(one.shape) == 3 else one, low_one), (two, low_two))):
                    attend_back(range(heads), head, length_of(low, rows), source.at[k], above, out.at[k])

            return step(
                body, [joined_shape], [], [joined, first, second, *lows], micros=3.6 * heads / 2, name=name
            )[0]

        joined_grad_near = attend_back_pair(joined_near, grad_own, back_core, tokens_all[:2], "attend_back_near")
        (mlp_sent,) = step(add_far, [row_low], [], [mlp_away, mlp_came], micros=1, mib=10, name="add_mlp")
        mlp_last = swap(mlp_sent, "x")
        down_parts = depth_exchange(down_part([down_came], "down_keep", [back_far]))
        up_came = swap(up_part([], "up_send"), "y")
        joined_grad_far = attend_back_pair(joined_far, back_far, back_last, tokens_all[2:], "attend_back_far")
        out_send, out_keep = out_fold(x, out_keep, out_came, wide // 4)
        out_came = swap(out_send, "x")

        def qkv_grad(s, near_ref, far_ref, grad_near, grad_far, send, keep, sums):
            tall = 2 * rows
            grads = [ref[...].reshape(tall, 3 * part) for ref in (grad_near, grad_far)]
            sums[...] = column_sum(grads[0].astype(F32)) + column_sum(grads[1].astype(F32))
            total = dot_left(near_ref[...].reshape(tall, width), grads[0])
            total = total + dot_left(far_ref[...].reshape(tall, width), grads[1])

            def split(k):
                first_half, second_half = (keep, send) if k == 0 else (send, keep)
                for n in range(depth):
                    at = n * part_depth
                    first_half[n] = total[at : at + half].astype(BF)
                    second_half[n, :rest] = total[at + half : at + part_depth].astype(BF)
                    second_half[n, rest:] = jnp.zeros((half - rest, 3 * part), BF)

            when_each(s[0], 2, split)

        halves = shape_of((depth, half, 3 * part), BF)
        qkv_send, qkv_keep, joined_sums = step(
            qkv_grad,
            [halves, halves, shape_of((1, 3 * part), F32)],
            [y],
            [normed_near, normed_far, joined_grad_near, joined_grad_far],
            mib=32,
            micros=4.5,
            name="qkv_grad",
        )
        qkv_came = swap(qkv_send, "y")

        def one_back(s, near_ref, far_ref, full, own, core, far_out):
            for k in range(GROUP):
                value = dot_right((near_ref, far_ref)[k // 2][k % 2], full[...])
                if k == 0:
                    own[...] = value
                elif k == 2:
                    far_out[...] = value
                else:
                    core[k // 2] = value.astype(BF)

        one_own, one_core, one_far = step(
            one_back, [row_full, row_pair, row_full], [], [joined_grad_near, joined_grad_far, qkv_full], micros=4.7, mib=24, name="one_back",
        )
        one_came = swap(one_core, "c")
        def leave(s, own, came, last, values, vector, out):
            keep = (lax.broadcasted_iota(jnp.int32, (rows, 1), 0) < s[0]).astype(F32)
            fed = own[...] + came[0].astype(F32) + last[...].astype(F32) + vector[7:8]
            out[...] = (keep * (values[...] + fed)).astype(BF)

        (block_out,) = step(
            leave, [row_low], [lengths], [mlp_own, mlp_came, mlp_last, middle, whole], micros=2.5, mib=14, name="leave"
        )

        up_parts = depth_exchange(up_part([up_came], "up_keep"))
        (one_sent,) = step(add_far, [row_low], [], [one_far, one_came], micros=0.7, mib=10, name="add_one")
        one_last = swap(one_sent, "x")

        out_send, out_keep = out_fold(y, out_keep, out_came, wide // 8)
        out_came = swap(out_send, "y")

        def qkv_fold(s, keep, came, out):
            for n in range(depth):
                out[n] = (keep[n].astype(F32) + came[n].astype(F32)).astype(BF)

        (qkv_parts,) = step(qkv_fold, [halves], [], [qkv_keep, qkv_came], micros=1.2, mib=12, name="qkv_fold")
        qkv_parts = depth_exchange(qkv_parts)

        def finish(s, own, came, last, values, vector, middle_ref, out, gain_sum, shift_sum):
            one = own[...] + came[0].astype(F32) + last[...].astype(F32)
            unit, inverse = normal(values[...].astype(F32))
            gain_sum[...] = column_sum(one * unit)
            shift_sum[...] = column_sum(one)
            out[...] = middle_ref[...] + normal_back(one * vector[0:1], unit, inverse)

        input_grad, gain_one_sum, shift_one_sum = step(
            finish, [row_full, row_sum, row_sum], [],
            [one_own, one_came, one_last, tokens, whole, middle_grad], micros=3.6, mib=16, name="finish",
        )

        def vector_pack(s, gain_one, shift_one, out_ref, gain_two, shift_two, down_ref, up_ref, up_more, joined, packed, line):
            packed[...] = jnp.zeros(packed.shape, F32)
            line[...] = jnp.zeros(line.shape, F32)
            for k, ref in ((0, gain_one), (1, shift_one), (4, out_ref), (5, gain_two), (6, shift_two), (7, down_ref)):
                line[k : k + 1] = ref[...]

            def of_member(m):
                line[2:3, m * part : (m + 1) * part] = joined[:, :part]
                line[3:4, m * part : (m + 1) * part] = joined[:, 2 * part :]
                for n in range(depth):
                    cols = slice(n * block, (n + 1) * block)
                    packed[n, 8 + m : 9 + m] = up_ref[:, cols] + up_more[:, cols]

            when_each(s[0], GROUP, of_member)
            for n in range(depth):
                packed[n, :8] = line[:, n * part_depth : (n + 1) * part_depth]

        packed_shape = shape_of((depth, 8 + GROUP, part_depth), F32)
        (packed,) = step(
            vector_pack,
            [packed_shape],
            [member],
            [gain_one_sum, shift_one_sum, out_sum, gain_two_sum, shift_two_sum, down_sum, up_sums_near, up_sums_far,
             joined_sums],
            scratch=[pltpu.VMEM((8, width), F32)],
            micros=0.6, mib=8, name="vector_pack",
        )

        def vector_hops(packed):
            def add(s, one, two, out):
                out[...] = one[...] + two[...]

            spans = [1 << k for k in range(depth.bit_length() - 1)]
            hops = ["c", "x", "y", *spans]
            for k, hop in enumerate(hops):
                if isinstance(hop, str):
                    came = swap(packed, hop)
                else:
                    came = send(packed, "z", [(i, i ^ hop) for i in range(depth)])
                yield packed
                (packed,) = step(add, [packed_shape], [], [packed, came], micros=0.5, mib=8, name="vector_add")
            yield packed

        hops = vector_hops(packed)
        next(hops)

        low_type = BF if outer == 1 else F32

        def feed_pieces(s, down_ref, up_ref, out):
            out[0] = sum_of(down_ref).astype(low_type)
            out[1] = sum_of(up_ref).astype(low_type)

        (feed_piece,) = step(
            feed_pieces, [shape_of((2, fold_rows, 2 * outer * each), low_type)], [], [down_parts, up_parts], micros=2.2,
            mib=16, name="feed_pieces",
        )
        if outer > 1:

            def over_outer(value):
                value = value.reshape(2, fold_rows, 2, outer, each)
                value = lax.psum_scatter(value, "o", scatter_dimension=3, tiled=False).astype(BF)
                return value.reshape(2, fold_rows, 2 * each)

            feed_piece = Later(over_outer, feed_piece)
        feed_all = group_gather(feed_piece)
        next(hops)

        next(hops)

        ratio = wide // depth
        fold = GROUP // ratio

        def feed_grads(s, *refs):
            blocks, (down_out, up_out) = refs[:4], refs[4:]

            def of_member(k):
                for m in range(GROUP):
                    at, to = k * (side // GROUP), m * block
                    ref, span = blocks[k ^ m], side // GROUP
                    down_out[to : to + fold_rows] = ref[0, :, at : at + span].astype(F32)
                    down_out[to + fold_rows : to + block] = ref[0, :fold_rest, side + at : side + at + span].astype(F32)
                for f in range(fold):
                    source = k % ratio * fold + f
                    at = k // ratio * block
                    ref, to = blocks[k ^ source], slice(f * block, (f + 1) * block)
                    up_out[:fold_rows, to] = ref[1, :, at : at + block].astype(F32)
                    up_out[fold_rows:, to] = ref[1, :fold_rest, each + at : each + at + block].astype(F32)

            when_each(s[0], GROUP, of_member)

        down_weight_grad, up_weight_grad = step(
            feed_grads,
            [shape_of((hidden_depth, side // GROUP), F32), shape_of((part_depth, fold * block), F32)],
            [member],
            feed_all,
            micros=2.9, mib=12, name="feed_grads",
        )

        def out_split(s, keep, came, out):
            for q in range(outer):
                total = keep[q].astype(F32) + came[q].astype(F32)
                for n in range(depth):
                    out[n, q] = total[:, n * part_depth : (n + 1) * part_depth].astype(BF)

        (out_parts,) = step(
            out_split, [shape_of((depth, outer, padded, part_depth), BF)], [], [out_keep, out_came], micros=1, mib=8,
            name="out_split",
        )
        out_parts = depth_exchange(out_parts)
        next(hops)

        def qkv_sum(s, parts, out):
            out[...] = sum_of(parts).astype(BF)

        (qkv_piece,) = step(qkv_sum, [shape_of((half, 3 * part), BF)], [], [qkv_parts], micros=1, mib=8, name="qkv_sum")
        qkv_all = group_gather(qkv_piece)
        packed = list(hops)[-1]
        span = 3 * width // wide

        def qkv_columns(s, *refs):
            blocks, (keep, send) = refs[:4], refs[4:]

            def of_member(k):
                for o in range(outer):
                    for side_at in range(2):
                        cut, at = [], ((2 * o + side_at) * GROUP + k) * span
                        stop = at + span
                        while at < stop:
                            to = min(stop, (at // part + 1) * part)
                            p, m = divmod(at // part, GROUP)
                            low = p * part + at % part
                            cut.append(blocks[k ^ m][:, low : low + to - at])
                            at = to
                        found = cut[0] if len(cut) == 1 else jnp.concatenate(cut, axis=1)

                        def put(here, found=found, side_at=side_at, o=o):
                            target = keep if here == side_at else send
                            target[o] = found

                        when_each(s[1], 2, put)

            when_each(s[0], GROUP, of_member)

        span_shape = shape_of((outer, half, span), BF)
        qkv_keep, qkv_send = step(
            qkv_columns, [span_shape, span_shape], [member, y], qkv_all, micros=1, mib=8, name="qkv_columns"
        )
        if outer > 1:
            qkv_keep, qkv_send = (
                Later(lambda v: lax.psum_scatter(v.astype(F32), "o", scatter_dimension=0, tiled=True).astype(BF), v)
                for v in (qkv_keep, qkv_send)
            )
        qkv_came = swap(qkv_send, "y")

        def out_last(s, parts, out):
            out[...] = sum_of(parts)[:, :strip]

        (out_sums,) = step(out_last, [shape_of((outer, strip, part_depth), F32)], [], [out_parts], micros=0.7, mib=8, name="out_last")

        def qkv_rows(s, keep, came, out):
            def put(k):
                top, bottom = (keep, came) if k == 0 else (came, keep)
                out[:half] = top[0].astype(F32)
                out[half:] = bottom[0, :rest].astype(F32)

            when_each(s[0], 2, put)

        (qkv_weight_grad,) = step(
            qkv_rows, [shape_of((part_depth, span), F32)], [y], [qkv_keep, qkv_came], micros=0.8, mib=8, name="qkv_rows"
        )
        step.run(PLAN)
        out_sums = out_sums.get()
        out_sums = out_sums[0] if outer == 1 else lax.psum_scatter(out_sums, "o", scatter_dimension=0, tiled=False)
        out_weight_grad = out_sums.T
        packed = lax.dynamic_index_in_dim(packed.get(), z[0], 0, keepdims=False)
        if outer > 1:
            packed = lax.psum(packed, "o")
        found = (
            block_out, input_grad, packed[0], packed[1], qkv_weight_grad, packed[2], packed[3], out_weight_grad,
            packed[4], packed[5], packed[6], up_weight_grad, packed[8:].reshape(hidden_depth), down_weight_grad, packed[7],
        )
        return tuple(now(v) for v in found)

    return shards


def solution(mesh):
    wide, depth = mesh.shape["wide"], mesh.shape["narrow"]
    outer = wide // 8
    fine = Mesh(mesh.devices.reshape(outer, 2, 2, 2, depth), AXES)
    rows, vec, mat = P(AXES, None), P("z"), P("z", None)
    placed = (
        rows, P(AXES), vec, vec, mat, vec, vec, mat, vec, vec, vec, mat, vec, mat, vec, rows,
    )
    grad = P("z", WIDE)
    return jax.shard_map(
        build(outer, depth),
        mesh=fine,
        in_specs=placed,
        out_specs=(rows, rows, vec, vec, grad, vec, vec, grad, vec, vec, vec, grad, vec, grad, vec),
        check_vma=False,
    )
```

```python
import functools

import jax
import jax.numpy as jnp
from jax import lax
from jax.experimental import pallas as pl
from jax.experimental.pallas import tpu as pltpu
from jax.sharding import Mesh, PartitionSpec as P

HEADS = 20
EPSILON = 1e-05
FILL = -1000000000.0
BF = jnp.bfloat16
F32 = jnp.float32
AXES = ("o", "y", "x", "c", "z")
WIDE = ("o", "y", "x", "c")
SWAP = [(0, 1), (1, 0)]
GROUP = 4
MIB = 1024 * 1024
PER_MICRO = 5e8
PLAN = (
    (1, 2, 0),
    (0, 0.4, 0),
    (2, 0.037, 0),
    (4, 1.5, 0),
    (3, 0.15, 0),
    (5, 0.315, 1),
    (6, 0.315, 0),
    (7, 0.36, 4),
    (8, 0.78, 5),
    (9, 0.45, 0),
    (10, 2.7, 0),
    (11, 4.5, 1),
    (12, 3, 0),
    (14, 0.1, 0),
    (13, 4, 1),
    (15, 5.4, 0),
    (16, 25, 0),
    (17, 32, 0),
    (20, 32, 0),
    (19, 0.525, 0),
    (18, 0.6, 0),
    (26, 4, 0),
    (21, 2, 0),
    (22, 0.25, 0),
    (23, 18, 0),
    (25, 0.3, 0),
    (24, 1, 0),
    (27, 9, 0),
    (29, 2, 0),
    (31, 0.02, 0),
    (30, 0.75, 0),
    (28, 2.52, 0),
    (32, 14.4, 0),
    (33, 7.2, 0),
    (34, 0.08, 0),
    (35, 32, 0),
    (36, 3.6, 0),
    (37, 0.6, 0),
    (39, 1, 0),
    (38, 2.2, 0),
    (40, 0.25, 0),
    (41, 2.9, 0),
    (42, 0.7, 0),
    (43, 0.35, 0),
    (44, 2.8, 0),
    (48, 32, 0),
    (47, 0.175, 0),
    (45, 0.35, 0),
    (46, 0.063, 0),
    (49, 10.08, 0),
)


class Later:
    def __init__(self, function, *values):
        self.function, self.values, self.found = function, values, None

    def get(self):
        if self.found is None:
            self.found = self.function(*(now(v) for v in self.values))
        return self.found

    def __getitem__(self, key):
        return Later(lambda v: v[key], self)


def now(value):
    return value.get() if isinstance(value, Later) else value


def send(value, axis, pairs):
    return Later(lambda v: lax.ppermute(v, axis, pairs), value)


def swap(value, axis):
    return send(value, axis, SWAP)


def dot(first, second):
    return jnp.dot(first, second, preferred_element_type=F32)


def dot_left(first, second):
    return lax.dot_general(first, second, (((0,), (0,)), ((), ())), preferred_element_type=F32)


def dot_right(first, second):
    return lax.dot_general(first, second, (((1,), (1,)), ((), ())), preferred_element_type=F32)


def shape_of(dims, dtype):
    return jax.ShapeDtypeStruct(dims, dtype)


class Order:
    def __init__(self):
        self.steps = []

    def __call__(self, body, outs, scalars, arrays, after=(), pins=-1, scratch=(), mib=28, micros=1.0, name=None):
        given = {}
        self.steps.append((body, outs, scalars, arrays, list(after), scratch, mib, micros, name, given, pins))
        return [Later(lambda k=k: given[k]) for k in range(len(outs))]

    def run(self, plan):
        if len(plan) != len(self.steps):
            plan = [(k, entry[7], entry[10]) for k, entry in enumerate(self.steps)]
        token = []
        for k, micros, pins in plan:
            body, outs, scalars, arrays, after, scratch, mib, _, name, given, _ = self.steps[k]
            after = [v for bit, v in enumerate(after) if pins >> bit & 1]
            *found, last = call_step(body, outs, scalars, arrays, after + token, scratch, mib, micros, name)
            token = [last]
            given.update(enumerate(found))


def call_step(body, outs, scalars, arrays, after, scratch, mib, micros, name):
    n_scalar, n_array, n_out = len(scalars), len(arrays), len(outs)

    def run(*refs):
        token = refs[n_scalar + n_array + len(after) + n_out]
        values = tuple(ref[0] for ref in refs[:n_scalar])
        rest = refs[n_scalar + n_array + len(after) :]
        token[...] = jnp.zeros(token.shape, F32)
        body(values, *refs[n_scalar : n_scalar + n_array], *rest[:n_out], *rest[n_out + 1 :])

    return pl.pallas_call(
        run,
        out_shape=(*outs, shape_of((8, 128), F32)),
        in_specs=[pl.BlockSpec(memory_space=pltpu.SMEM)] * n_scalar
        + [pl.BlockSpec(memory_space=pltpu.VMEM)] * n_array
        + [pl.BlockSpec(memory_space=pl.ANY)] * len(after),
        out_specs=(pl.BlockSpec(memory_space=pltpu.VMEM),) * (n_out + 1),
        scratch_shapes=list(scratch),
        compiler_params=pltpu.CompilerParams(vmem_limit_bytes=mib * MIB),
        cost_estimate=pl.CostEstimate(flops=int(micros * PER_MICRO), bytes_accessed=1024, transcendentals=0),
        name=name,
    )(*(now(v) for v in (*scalars, *arrays, *after)))


def group_gather(value):
    over_x = swap(value, "x")
    over_core = swap(value, "c")
    return [value, over_core, over_x, swap(over_x, "c")]


def depth_shift(value, shift, count):
    return send(value, "z", [(i, (i + shift) % count) for i in range(count)])


def depth_line(value, count):
    up, down = [], []
    for s in range(count - 1):
        up.append(send(up[-1] if s else value, "z", [(i, i + 1) for i in range(s, count - 1)]))
        down.append(send(down[-1] if s else value, "z", [(i, i - 1) for i in range(1, count - s)]))
    return up, down


def next_block(z, step, count):
    return z + 1 + step if step < count - 1 - z else count - 2 - step


def line_ref(z, other, up, down):
    return up[z - 1 - other] if other < z else down[other - z - 1]


def depth_exchange(parts):
    return Later(lambda v: lax.all_to_all(v, "z", 0, 0), parts)


def sum_of(refs):
    total = refs[0].astype(F32)
    for k in range(1, refs.shape[0]):
        total = total + refs[k].astype(F32)
    return total


def normal(values):
    center = values - jnp.mean(values, axis=-1, keepdims=True)
    spread = jnp.mean(center * center, axis=-1, keepdims=True)
    inverse = lax.rsqrt(spread + EPSILON)
    return center * inverse, inverse


def normal_back(grad, unit, inverse):
    return (
        grad
        - jnp.mean(grad, axis=-1, keepdims=True)
        - unit * jnp.mean(grad * unit, axis=-1, keepdims=True)
    ) * inverse


def when_each(index, count, step):
    for k in range(count):
        pl.when(index == k)(functools.partial(step, k))


def allowed_of(rows, length):
    query = lax.broadcasted_iota(jnp.int32, (rows, rows), 0)
    key = lax.broadcasted_iota(jnp.int32, (rows, rows), 1)
    return (key <= query) & (key < length)


def length_of(payload, rows):
    high = payload[rows : rows + 1, 0:1].astype(F32)
    low = payload[rows : rows + 1, 128:129].astype(F32)
    return (high * 16.0 + low).astype(jnp.int32)


def head_probs(query, key, allowed, scale):
    scores = jnp.where(allowed, dot_right(query, key) * scale, FILL)
    weights = jnp.exp(scores - jnp.max(scores, axis=1, keepdims=True))
    return weights * (1.0 / jnp.sum(weights, axis=1, keepdims=True))


def attend(heads, tokens, full, vectors, query_shift, value_shift, normed, joined, contexts):
    rows, part = normed.shape[1], full.shape[1] // 3
    head = part // heads
    scale = head ** (-0.5)
    for n, x in enumerate(tokens):
        normed[n] = (normal(x[:rows].astype(F32))[0] * vectors[0:1] + vectors[1:2]).astype(BF)
        sums = dot(normed[n], full[...])
        query = (sums[:, :part] + query_shift[...]).astype(BF)
        key = sums[:, part : 2 * part].astype(BF)
        value = (sums[:, 2 * part :] + value_shift[...]).astype(BF)
        joined[n, :, :part] = query
        joined[n, :, part : 2 * part] = key
        joined[n, :, 2 * part :] = value
        allowed = allowed_of(rows, length_of(x, rows))
        out = []
        for h in range(heads):
            cut = slice(h * head, (h + 1) * head)
            probs = head_probs(query[:, cut], key[:, cut], allowed, scale).astype(BF)
            out.append(dot(probs, value[:, cut]))
        contexts[n][...] = jnp.concatenate(out, axis=1).astype(BF)


def attend_back(chosen, head, length, joined, above, out):
    rows, part = above.shape
    scale = head ** (-0.5)
    allowed = allowed_of(rows, length)
    found = ([], [], [])
    for h in chosen:
        q, k, v = (joined[:, p * part + h * head : p * part + (h + 1) * head] for p in range(3))
        g = above[:, h * head : (h + 1) * head]
        probs = head_probs(q, k, allowed, scale)
        probs_grad = dot_right(g, v)
        found[2].append(dot_left(probs.astype(BF), g))
        score = probs * (probs_grad - jnp.sum(probs * probs_grad, axis=1, keepdims=True))
        score = score.astype(BF)
        found[0].append(dot(score, k) * scale)
        found[1].append(dot_left(score, q) * scale)
    out[...] = jnp.concatenate(found[0] + found[1] + found[2], axis=1).astype(BF)


def gelu_both(values):
    root = (2.0 / jnp.pi) ** 0.5
    square = values * values
    bend = jnp.tanh(root * (values + 0.044715 * (square * values)))
    half = 0.5 * (1.0 + bend)
    slope = half + 0.5 * values * (1.0 - bend * bend) * (root * (1.0 + 3.0 * 0.044715 * square))
    return values * half, slope


def column_sum(values):
    return jnp.sum(values, axis=0, keepdims=True)


def build(outer, depth):
    def shards(
        tokens, lengths, norm1_gain, norm1_bias, qkv_weight, query_bias, value_bias, out_weight,
        out_bias, norm2_gain, norm2_bias, up_weight, up_bias, down_weight, down_bias, cotangent,
    ):
        rows, width = tokens.shape
        heads = HEADS // GROUP
        part = width // GROUP
        part_depth = width // depth
        hidden_depth = up_weight.shape[1] // depth
        block = hidden_depth // GROUP
        mine = depth * block
        wide = outer * 2 * GROUP
        sides = outer * 2
        y, x, c, z = (lax.axis_index(name).astype(jnp.int32).reshape(1) for name in ("y", "x", "c", "z"))
        member = 2 * x + c
        others = range(1, depth)
        step = Order()

        row_low, row_full = shape_of((rows, width), BF), shape_of((rows, width), F32)
        row_pair = shape_of((2, rows, width), BF)
        row_sum = shape_of((1, width), F32)
        cell, pair = shape_of((rows, part), BF), shape_of((2, rows, part), BF)

        def take_rows(s, values, out):
            out[:rows] = values[...]
            lane = lax.broadcasted_iota(jnp.int32, (16, width), 1)
            out[rows:] = jnp.where(lane < 128, s[0] // 16, s[0] % 16).astype(F32).astype(BF)

        (tokens_low,) = step(
            take_rows, [shape_of((rows + 16, width), BF)], [lengths], [tokens], micros=0.8, mib=10, name="take_rows"
        )
        tokens_all = group_gather(tokens_low)

        half = (part_depth // 2 + 15) // 16 * 16
        rest = part_depth - half
        quad_shape, half_shape = shape_of((part_depth, 4 * part), BF), shape_of((half, 4 * part), BF)
        biases = (norm1_gain, norm1_bias, query_bias, value_bias, out_bias, norm2_gain, norm2_bias, down_bias, up_bias)

        def take_quad(s, qkv, out, own, send):
            def columns(k):
                for p in range(3):
                    at = (p * GROUP + k) * part
                    own[:, p * part : (p + 1) * part] = qkv[:, at : at + part]
                own[:, 3 * part :] = out[:, k * part : (k + 1) * part]

            when_each(s[0], GROUP, columns)

            @pl.when(s[1] == 0)
            def _():
                send[...] = own[:half]

            @pl.when(s[1] == 1)
            def _():
                send[:rest] = own[half:]
                send[rest:] = jnp.zeros((half - rest, 4 * part), BF)

        quad_own, quad_half = step(
            take_quad, [quad_shape, half_shape], [member, y], [qkv_weight, out_weight], micros=0.5, mib=12, name="take_quad"
        )
        quad_up, quad_down = depth_line(quad_half, depth)

        def take_vectors(s, *refs):
            found = [ref[...].astype(F32).reshape(1, part_depth) for ref in refs[:8]]
            more = [refs[8][k * block : (k + 1) * block].astype(F32).reshape(1, block) for k in range(GROUP)]
            refs[9][...] = jnp.zeros(refs[9].shape, F32)
            refs[9][:8, :part_depth] = jnp.concatenate(found, axis=0)
            refs[9][:GROUP, part_depth : 2 * part_depth] = jnp.concatenate(more, axis=0)

        (lines_own,) = step(
            take_vectors, [shape_of((8, 2 * part_depth), F32)], [], biases, micros=0.5, mib=8, name="take_vectors"
        )
        lines_all = [lines_own] + [depth_shift(lines_own, r, depth) for r in others]

        def live(s, values, low, sums):
            keep = (lax.broadcasted_iota(jnp.int32, (rows, 1), 0) < s[0]).astype(F32)
            kept = values[...].astype(F32) * keep
            low[...] = kept.astype(BF)
            sums[...] = column_sum(kept)

        grad_low, down_sum = step(live, [row_low, row_sum], [lengths], [cotangent], micros=0.5, mib=10, name="live")
        grad_all = group_gather(grad_low)

        def hand_on(up, down, like, after=False):
            came = []
            for s_at in others:

                def choose_block(s, *refs, at=s_at - 1):
                    ups, downs, out = refs[: at + 1], refs[at + 1 : -1], refs[-1]

                    def copy(k):
                        out[...] = line_ref(k, next_block(k, at, depth), ups, downs)[...]

                    when_each(s[0], depth, copy)

                (block_now,) = step(
                    choose_block, [like], [z], [*up[:s_at], *down[:s_at]], after=came[-1:], pins=int(after), micros=1.5, mib=8, name="hand_on"
                )
                came.append(swap(block_now, "y"))
                yield came

        quad_far = list(hand_on(quad_up, quad_down, half_shape))[-1]

        turn_shape = shape_of((part_depth, mine), BF)

        def take_mlp(s, up, down, up_own, turn):
            def part_of(k):
                for n in range(depth):
                    at = n * hidden_depth + k * block
                    up_own[:, n * block : (n + 1) * block] = up[:, at : at + block]

                @pl.when(s[1] == 1)
                def _():
                    turn[...] = down[k * block : (k + 1) * block]

            when_each(s[0], GROUP, part_of)

            @pl.when(s[1] == 0)
            def _():
                turn[...] = up_own[...]

        up_own, turn = step(
            take_mlp, [turn_shape, turn_shape], [member, y], [up_weight, down_weight], after=[quad_up[-1], quad_down[-1], *quad_far], pins=3, micros=1.2, mib=20,
            name="take_mlp",
        )
        mlp_up, mlp_down = depth_line(turn, depth)
        mlp_far_steps = hand_on(mlp_up, mlp_down, turn_shape, True)

        lines = depth - 1

        def assemble(s, own, *refs):
            blocks, refs = refs[:depth], refs[depth:]
            ups, downs, handed = refs[:lines], refs[lines : 2 * lines], refs[2 * lines : 3 * lines]
            full, out_cols, whole, query_shift, value_shift, up_shift = refs[3 * lines :]

            def put_vectors(at, values):
                whole[:, at * part_depth : (at + 1) * part_depth] = values[:, :part_depth]

                def of_member(m):
                    up_shift[:, at * block : (at + 1) * block] = values[m : m + 1, part_depth : 2 * part_depth]

                when_each(s[2], GROUP, of_member)

            def put(k):
                full[k * part_depth : (k + 1) * part_depth] = own[:, : 3 * part]
                out_cols[:, k * part : (k + 1) * part] = own[:, 3 * part :]
                for r in range(depth):
                    put_vectors((k - r) % depth, blocks[r][...])
                for at in range(lines):
                    other = next_block(k, at, depth)
                    low, cols = other * part_depth, slice(other * part, (other + 1) * part)

                    def both(side, at=at, low=low, cols=cols, other=other):
                        ours = line_ref(k, other, ups, downs)
                        top, bottom = (ours, handed[at]) if side == 0 else (handed[at], ours)
                        full[low : low + half] = top[:, : 3 * part]
                        full[low + half : low + part_depth] = bottom[:rest, : 3 * part]
                        out_cols[:half, cols] = top[:, 3 * part :]
                        out_cols[half:, cols] = bottom[:rest, 3 * part :]

                    when_each(s[1], 2, both)

            when_each(s[0], depth, put)

            def of_member(m):
                query_shift[...] = whole[2:3, m * part : (m + 1) * part]
                value_shift[...] = whole[3:4, m * part : (m + 1) * part]

            when_each(s[2], GROUP, of_member)

        shift_shape = shape_of((1, part), F32)
        qkv_full, out_part, whole, query_shift, value_shift, up_shift = step(
            assemble,
            [shape_of((width, 3 * part), BF), shape_of((part_depth, depth * part), BF), shape_of((8, width), F32), shift_shape,
             shift_shape, shape_of((1, mine), F32)],
            [z, y, member],
            [quad_own, *lines_all, *quad_up, *quad_down, *quad_far],
            after=[grad_all[2], grad_all[3], grad_all[1]],
            pins=1,
            micros=1.3, mib=16, name="assemble",
        )
        out_all = group_gather(out_part)
        next(mlp_far_steps)


        def attend_far(s, full, vector, first, second, shift_q, shift_v, normed, joined, context):
            attend(heads, (first, second), full, vector, shift_q, shift_v, normed, joined,
                   (context.at[0], context.at[1]))

        joined_shape = shape_of((2, rows, 3 * part), BF)
        normed_far, joined_far, context_far = step(
            attend_far,
            [row_pair, joined_shape, pair],
            [],
            [qkv_full, whole, tokens_all[2], tokens_all[3], query_shift, value_shift],
            micros=9, mib=20, name="attend_far",
        )
        came_far = swap(context_far, "x")
        next(mlp_far_steps)

        def attend_near(s, full, vector, first, second, shift_q, shift_v, normed, joined, ours, theirs):
            attend(heads, (first, second), full, vector, shift_q, shift_v, normed, joined,
                   (ours, theirs))

        normed_near, joined_near, context_own, context_core = step(
            attend_near,
            [row_pair, joined_shape, cell, cell],
            [],
            [qkv_full, whole, tokens_all[0], tokens_all[1], query_shift, value_shift],
            micros=9, mib=20, name="attend_near",
        )
        came_core = swap(context_core, "c")
        came_last = swap(came_far[1], "c")

        mlp_far = list(mlp_far_steps)[-1]

        def out_whole(s, *refs):
            blocks, full = refs[:-1], refs[-1]

            def put(k):
                for other in range(GROUP):
                    at = (k ^ other) * part
                    for n in range(depth):
                        rows_of = slice(n * part_depth, (n + 1) * part_depth)
                        full[rows_of, at : at + part] = blocks[other][:, n * part : (n + 1) * part]

            when_each(s[0], GROUP, put)

        (out_full,) = step(out_whole, [shape_of((width, width), BF)], [member], out_all, micros=1, mib=12, name="out_whole")

        def project(s, own, core, far_pair, last, full, values, vector, context, middle, normed):
            def put(k):
                for other, ref in enumerate((own, core, None, last)):
                    at = (k ^ other) * part
                    context[:, at : at + part] = far_pair[0] if ref is None else ref[...]

            when_each(s[0], GROUP, put)
            total = values[...].astype(F32) + (dot(context[...], full[...]) + vector[4:5])
            middle[...] = total
            normed[...] = (normal(total)[0] * vector[5:6] + vector[6:7]).astype(BF)

        context, middle, normed_two = step(
            project,
            [row_low, row_full, row_low],
            [member],
            [context_own, came_core, came_far, came_last, out_full, tokens, whole],
            micros=3.6, mib=20, name="project",
        )
        normed_two_all = group_gather(normed_two)

        def feed_cells(cells, normed, grads, up_full, down_full, shift, active, before, sums, two_low, two):
            total = jnp.zeros((1, mine), F32)
            for k in cells:
                at = slice(k * rows, (k + 1) * rows)
                value, slope = gelu_both(dot(normed[k][...], up_full[...]) + shift[...])
                active[at] = value.astype(BF)
                grad = (dot_right(grads[k][...], down_full[...]) * slope).astype(BF)
                before[at] = grad
                total = total + column_sum(grad.astype(F32))
                found = dot_right(grad, up_full[...])
                if k == 0:
                    two[...] = found
                else:
                    two_low[...] = found.astype(BF)
            sums[...] = total

        def feed_near(s, up_ref, down_ref, *refs):
            ups, downs, handed = refs[:lines], refs[lines : 2 * lines], refs[2 * lines : 3 * lines]
            refs = refs[3 * lines :]
            normed, grads, shift, (up_full, down_full, *outs) = refs[:2], refs[2:4], refs[4], refs[5:]

            def put(k):
                up_full[k * part_depth : (k + 1) * part_depth] = up_ref[...]

                def of_member(m):
                    down_full[k * block : (k + 1) * block] = down_ref[m * block : (m + 1) * block]

                when_each(s[2], GROUP, of_member)
                for at in range(lines):
                    other = next_block(k, at, depth)

                    def both(side, at=at, other=other):
                        ours = line_ref(k, other, ups, downs)
                        up_from, down_from = (ours, handed[at]) if side == 0 else (handed[at], ours)
                        up_full[other * part_depth : (other + 1) * part_depth] = up_from[...]
                        down_full[other * block : (other + 1) * block] = down_from[...]

                    when_each(s[1], 2, both)

            when_each(s[0], depth, put)
            feed_cells((1, 0), normed, grads, up_full, down_full, shift, *outs)

        hidden_rows, hidden_sum = shape_of((2 * rows, mine), BF), shape_of((1, mine), F32)
        up_full, down_full, active_near, before_near, up_sums_near, two_core, two_own = step(
            feed_near,
            [shape_of((width, mine), BF), shape_of((mine, width), BF), hidden_rows, hidden_rows, hidden_sum, row_low, row_full],
            [z, y, member],
            [up_own, down_weight, *mlp_up, *mlp_down, *mlp_far, *normed_two_all[:2], *grad_all[:2], up_shift],
            mib=40,
            micros=12.5, name="feed_near",
        )
        two_came = swap(two_core, "c")

        def feed_far(s, up_full, down_full, *refs):
            feed_cells((1, 0), refs[:2], refs[2:4], up_full, down_full, *refs[4:])

        active_far, before_far, up_sums_far, two_next, two_far = step(
            feed_far,
            [hidden_rows, hidden_rows, hidden_sum, row_low, row_full],
            [],
            [up_full, down_full, *normed_two_all[2:], *grad_all[2:], up_shift],
            mib=36,
            micros=10.5, name="feed_far",
        )
        next_came = swap(two_next, "c")
        active, before = [active_near, active_far], [before_near, before_far]

        each, side = mine // sides, width // sides

        def columns_for(value, count, index):
            cut = [value[:, (2 * o + index) * count : (2 * o + index + 1) * count] for o in range(outer)]
            return cut[0] if outer == 1 else jnp.concatenate(cut, axis=1)

        tall = max(block, part_depth)
        fold_rows = (tall // 2 + 15) // 16 * 16
        fold_rest = tall - fold_rows
        pack_shape = shape_of((depth, fold_rows, 2 * outer * each), BF)
        feed_scratch = [pltpu.VMEM((GROUP * rows, width), BF), pltpu.VMEM((GROUP * rows, outer * each), BF)]

        def store_rows(total, came, out):
            cut = total.shape[1]
            for n in range(depth):
                top = total[n * tall : n * tall + fold_rows]
                low = total[n * tall + fold_rows : (n + 1) * tall]
                if came is not None:
                    top = top + came[n, :, :cut].astype(F32)
                    low = low + came[n, :fold_rest, cut:].astype(F32)
                out[n, :, :cut] = top.astype(BF)
                out[n, :fold_rest, cut:] = low.astype(BF)
                out[n, fold_rest:, cut:] = jnp.zeros((fold_rows - fold_rest, cut), BF)

        def down_product(grads, right_all, index):
            for k, ref in enumerate(grads):
                right_all[k * rows : (k + 1) * rows] = columns_for(ref[...], side, index)

        def up_product(befores, right_all, index):
            for k, ref in enumerate(befores):
                right_all[2 * k * rows : 2 * (k + 1) * rows] = columns_for(ref[...], each, index)

        def feed_part(product, arrays, scratch, came, name, after=()):
            n_array, n_came = len(arrays), len(came)

            def body(s, *refs):
                inputs, came_refs, (out, *left_refs, right_all) = (
                    refs[:n_array], refs[n_array : n_array + n_came], refs[n_array + n_came :]
                )
                when_each(s[0], 2, lambda k: product(inputs, right_all, k if n_came else 1 - k))
                if left_refs:
                    for k in range(GROUP):
                        left_refs[0][k * rows : (k + 1) * rows] = inputs[2 + k][...]
                    total = dot_left(left_refs[0][...], right_all[...])
                else:
                    total = dot_left(inputs[0][...], right_all[: 2 * rows]) + dot_left(inputs[1][...], right_all[2 * rows :])
                store_rows(total, came_refs[0] if n_came else None, out)

            return step(
                body, [pack_shape], [y], [*arrays, *came], after=after, scratch=scratch, mib=32, micros=4, name=name
            )[0]

        def down_part(came, name, after=()):
            return feed_part(
                lambda refs, right, k: down_product(refs[2:], right, k),
                [*active, *grad_all], feed_scratch[1:], came, name, after,
            )

        def up_part(came, name, after=()):
            return feed_part(
                lambda refs, right, k: up_product(refs[:2], right, k),
                [*before, *normed_two_all], feed_scratch, came, name, after,
            )

        down_came = swap(down_part([], "down_send"), "y")

        def add_far(s, far, came, out):
            out[...] = (far[...] + came[1].astype(F32)).astype(BF)

        def add_two(s, far, came, out):
            out[...] = (far[...] + came[...].astype(F32)).astype(BF)

        (two_sent,) = step(add_two, [row_low], [], [two_far, next_came], micros=0.7, mib=10, name="add_two")
        two_last = swap(two_sent, "x")

        def feed_out(s, near_ref, far_ref, full, own, core, far_out):
            for k in range(GROUP):
                value = dot((near_ref, far_ref)[k // 2][k % 2 * rows : (k % 2 + 1) * rows], full[...])
                if k == 0:
                    own[...] = value
                elif k == 2:
                    far_out[...] = value
                else:
                    core[k // 2] = value.astype(BF)

        mlp_own, mlp_core, mlp_away = step(
            feed_out, [row_full, row_pair, row_full], [], [*active, down_full], micros=4.5, mib=24, name="feed_out",
        )
        mlp_came = swap(mlp_core, "c")

        def turn_back(
            s, own, came, last, values, grads, vector, full,
            middle_grad, low, ours, core, far_pair, gain_sum, shift_sum, out_sum,
        ):
            two = own[...] + came[...].astype(F32) + last[...].astype(F32)
            unit, inverse = normal(values[...])
            gain_sum[...] = column_sum(two * unit)
            shift_sum[...] = column_sum(two)
            total = grads[...].astype(F32) + normal_back(two * vector[5:6], unit, inverse)
            middle_grad[...] = total
            low[...] = total.astype(BF)
            out_sum[...] = column_sum(total.astype(BF).astype(F32))
            grad = dot_right(low[...], full[...]).astype(BF)

            def split(k):
                for other in range(GROUP):
                    at = (k ^ other) * part
                    piece = grad[:, at : at + part]
                    if other == 0:
                        ours[...] = piece
                    elif other == 1:
                        core[...] = piece
                    else:
                        far_pair[other - 2] = piece

            when_each(s[0], GROUP, split)

        middle_grad, middle_low, grad_own, grad_core, grad_far, gain_two_sum, shift_two_sum, out_sum = step(
            turn_back,
            [row_full, row_low, cell, cell, pair, row_sum, row_sum, row_sum],
            [member],
            [two_own, two_came, two_last, middle, grad_low, whole, out_full],
            micros=3.2, mib=24, name="turn_back",
        )
        back_far = swap(grad_far, "x")
        back_core = swap(grad_core, "c")
        back_last = swap(back_far[1], "c")

        strip = width // wide
        padded = (strip + 15) // 16 * 16

        def out_grad(s, low, values, send, keep):
            total = dot_left(low[...], values[...])

            def split(k):
                for q in range(wide // 2):
                    for core in range(2):
                        target = keep if core == k else send
                        at = (2 * q + core) * strip
                        target[q, :strip] = total[at : at + strip].astype(BF)
                        target[q, strip:] = jnp.zeros((padded - strip, width), BF)

            when_each(s[0], 2, split)

        out_shape = shape_of((wide // 2, padded, width), BF)
        out_send, out_keep = step(
            out_grad, [out_shape, out_shape], [c], [middle_low, context], micros=2, mib=20, name="out_grad"
        )
        out_came = swap(out_send, "c")

        def out_fold(flag, keep, came, count):
            span = 1

            def body(s, kept, arrived, send, keep_out):
                def split(k):
                    for q in range(count):
                        at = q // span * 2 * span + q % span
                        for bit in range(2):
                            target = keep_out if bit == k else send
                            source = at + bit * span
                            target[q] = (kept[source].astype(F32) + arrived[source].astype(F32)).astype(BF)

                when_each(s[0], 2, split)

            out = shape_of((count, padded, width), BF)
            return step(body, [out, out], [flag], [keep, came], micros=1.4, mib=16, name="out_fold")

        head = part // heads

        def attend_back_pair(joined, first, second, lows, name):
            def body(s, source, one, two, low_one, low_two, out):
                for k, (above, low) in enumerate(((one.at[0] if len(one.shape) == 3 else one, low_one), (two, low_two))):
                    attend_back(range(heads), head, length_of(low, rows), source.at[k], above, out.at[k])

            return step(
                body, [joined_shape], [], [joined, first, second, *lows], micros=3.6 * heads / 2, name=name
            )[0]

        joined_grad_near = attend_back_pair(joined_near, grad_own, back_core, tokens_all[:2], "attend_back_near")
        (mlp_sent,) = step(add_far, [row_low], [], [mlp_away, mlp_came], micros=1, mib=10, name="add_mlp")
        mlp_last = swap(mlp_sent, "x")
        down_parts = depth_exchange(down_part([down_came], "down_keep", [back_far]))
        up_came = swap(up_part([], "up_send"), "y")
        joined_grad_far = attend_back_pair(joined_far, back_far, back_last, tokens_all[2:], "attend_back_far")
        out_send, out_keep = out_fold(x, out_keep, out_came, wide // 4)
        out_came = swap(out_send, "x")

        def qkv_grad(s, near_ref, far_ref, grad_near, grad_far, send, keep, sums):
            tall = 2 * rows
            grads = [ref[...].reshape(tall, 3 * part) for ref in (grad_near, grad_far)]
            sums[...] = column_sum(grads[0].astype(F32)) + column_sum(grads[1].astype(F32))
            total = dot_left(near_ref[...].reshape(tall, width), grads[0])
            total = total + dot_left(far_ref[...].reshape(tall, width), grads[1])

            def split(k):
                first_half, second_half = (keep, send) if k == 0 else (send, keep)
                for n in range(depth):
                    at = n * part_depth
                    first_half[n] = total[at : at + half].astype(BF)
                    second_half[n, :rest] = total[at + half : at + part_depth].astype(BF)
                    second_half[n, rest:] = jnp.zeros((half - rest, 3 * part), BF)

            when_each(s[0], 2, split)

        halves = shape_of((depth, half, 3 * part), BF)
        qkv_send, qkv_keep, joined_sums = step(
            qkv_grad,
            [halves, halves, shape_of((1, 3 * part), F32)],
            [y],
            [normed_near, normed_far, joined_grad_near, joined_grad_far],
            mib=32,
            micros=4.5,
            name="qkv_grad",
        )
        qkv_came = swap(qkv_send, "y")

        def one_back(s, near_ref, far_ref, full, own, core, far_out):
            for k in range(GROUP):
                value = dot_right((near_ref, far_ref)[k // 2][k % 2], full[...])
                if k == 0:
                    own[...] = value
                elif k == 2:
                    far_out[...] = value
                else:
                    core[k // 2] = value.astype(BF)

        one_own, one_core, one_far = step(
            one_back, [row_full, row_pair, row_full], [], [joined_grad_near, joined_grad_far, qkv_full], micros=4.7, mib=24, name="one_back",
        )
        one_came = swap(one_core, "c")
        def leave(s, own, came, last, values, vector, out):
            keep = (lax.broadcasted_iota(jnp.int32, (rows, 1), 0) < s[0]).astype(F32)
            fed = own[...] + came[0].astype(F32) + last[...].astype(F32) + vector[7:8]
            out[...] = (keep * (values[...] + fed)).astype(BF)

        (block_out,) = step(
            leave, [row_low], [lengths], [mlp_own, mlp_came, mlp_last, middle, whole], micros=2.5, mib=14, name="leave"
        )

        up_parts = depth_exchange(up_part([up_came], "up_keep"))
        (one_sent,) = step(add_far, [row_low], [], [one_far, one_came], micros=0.7, mib=10, name="add_one")
        one_last = swap(one_sent, "x")

        out_send, out_keep = out_fold(y, out_keep, out_came, wide // 8)
        out_came = swap(out_send, "y")

        def qkv_fold(s, keep, came, out):
            for n in range(depth):
                out[n] = (keep[n].astype(F32) + came[n].astype(F32)).astype(BF)

        (qkv_parts,) = step(qkv_fold, [halves], [], [qkv_keep, qkv_came], micros=1.2, mib=12, name="qkv_fold")
        qkv_parts = depth_exchange(qkv_parts)

        def finish(s, own, came, last, values, vector, middle_ref, out, gain_sum, shift_sum):
            one = own[...] + came[0].astype(F32) + last[...].astype(F32)
            unit, inverse = normal(values[...].astype(F32))
            gain_sum[...] = column_sum(one * unit)
            shift_sum[...] = column_sum(one)
            out[...] = middle_ref[...] + normal_back(one * vector[0:1], unit, inverse)

        input_grad, gain_one_sum, shift_one_sum = step(
            finish, [row_full, row_sum, row_sum], [],
            [one_own, one_came, one_last, tokens, whole, middle_grad], micros=3.6, mib=16, name="finish",
        )

        def vector_pack(s, gain_one, shift_one, out_ref, gain_two, shift_two, down_ref, up_ref, up_more, joined, packed, line):
            packed[...] = jnp.zeros(packed.shape, F32)
            line[...] = jnp.zeros(line.shape, F32)
            for k, ref in ((0, gain_one), (1, shift_one), (4, out_ref), (5, gain_two), (6, shift_two), (7, down_ref)):
                line[k : k + 1] = ref[...]

            def of_member(m):
                line[2:3, m * part : (m + 1) * part] = joined[:, :part]
                line[3:4, m * part : (m + 1) * part] = joined[:, 2 * part :]
                for n in range(depth):
                    cols = slice(n * block, (n + 1) * block)
                    packed[n, 8 + m : 9 + m] = up_ref[:, cols] + up_more[:, cols]

            when_each(s[0], GROUP, of_member)
            for n in range(depth):
                packed[n, :8] = line[:, n * part_depth : (n + 1) * part_depth]

        packed_shape = shape_of((depth, 8 + GROUP, part_depth), F32)
        (packed,) = step(
            vector_pack,
            [packed_shape],
            [member],
            [gain_one_sum, shift_one_sum, out_sum, gain_two_sum, shift_two_sum, down_sum, up_sums_near, up_sums_far,
             joined_sums],
            scratch=[pltpu.VMEM((8, width), F32)],
            micros=0.6, mib=8, name="vector_pack",
        )

        def vector_hops(packed):
            def add(s, one, two, out):
                out[...] = one[...] + two[...]

            spans = [1 << k for k in range(depth.bit_length() - 1)]
            hops = ["c", "x", "y", *spans]
            for k, hop in enumerate(hops):
                if isinstance(hop, str):
                    came = swap(packed, hop)
                else:
                    came = send(packed, "z", [(i, i ^ hop) for i in range(depth)])
                yield packed
                (packed,) = step(add, [packed_shape], [], [packed, came], micros=0.5, mib=8, name="vector_add")
            yield packed

        hops = vector_hops(packed)
        next(hops)

        low_type = BF if outer == 1 else F32

        def feed_pieces(s, down_ref, up_ref, out):
            out[0] = sum_of(down_ref).astype(low_type)
            out[1] = sum_of(up_ref).astype(low_type)

        (feed_piece,) = step(
            feed_pieces, [shape_of((2, fold_rows, 2 * outer * each), low_type)], [], [down_parts, up_parts], micros=2.2,
            mib=16, name="feed_pieces",
        )
        if outer > 1:

            def over_outer(value):
                value = value.reshape(2, fold_rows, 2, outer, each)
                value = lax.psum_scatter(value, "o", scatter_dimension=3, tiled=False).astype(BF)
                return value.reshape(2, fold_rows, 2 * each)

            feed_piece = Later(over_outer, feed_piece)
        feed_all = group_gather(feed_piece)
        next(hops)

        next(hops)

        ratio = wide // depth
        fold = GROUP // ratio

        def feed_grads(s, *refs):
            blocks, (down_out, up_out) = refs[:4], refs[4:]

            def of_member(k):
                for m in range(GROUP):
                    at, to = k * (side // GROUP), m * block
                    ref, span = blocks[k ^ m], side // GROUP
                    down_out[to : to + fold_rows] = ref[0, :, at : at + span].astype(F32)
                    down_out[to + fold_rows : to + block] = ref[0, :fold_rest, side + at : side + at + span].astype(F32)
                for f in range(fold):
                    source = k % ratio * fold + f
                    at = k // ratio * block
                    ref, to = blocks[k ^ source], slice(f * block, (f + 1) * block)
                    up_out[:fold_rows, to] = ref[1, :, at : at + block].astype(F32)
                    up_out[fold_rows:, to] = ref[1, :fold_rest, each + at : each + at + block].astype(F32)

            when_each(s[0], GROUP, of_member)

        down_weight_grad, up_weight_grad = step(
            feed_grads,
            [shape_of((hidden_depth, side // GROUP), F32), shape_of((part_depth, fold * block), F32)],
            [member],
            feed_all,
            micros=2.9, mib=12, name="feed_grads",
        )

        def out_split(s, keep, came, *rest_refs):
            *outs, packed = rest_refs
            for q in range(outer):
                total = keep[q].astype(F32) + came[q].astype(F32)
                for n in range(depth):
                    packed[n, q] = total[:, n * part_depth : (n + 1) * part_depth].astype(BF)
            for r, ref in enumerate(outs):
                ref[...] = packed[lax.rem(s[0] + r, depth)]

        out_parts = step(
            out_split, [shape_of((outer, padded, part_depth), BF)] * depth, [z], [out_keep, out_came],
            scratch=[pltpu.VMEM((depth, outer, padded, part_depth), BF)], micros=1, mib=8, name="out_split",
        )
        out_parts = [out_parts[0]] + [depth_shift(out_parts[r], r, depth) for r in others]
        next(hops)

        def qkv_sum(s, parts, out):
            out[...] = sum_of(parts).astype(BF)

        (qkv_piece,) = step(qkv_sum, [shape_of((half, 3 * part), BF)], [], [qkv_parts], micros=1, mib=8, name="qkv_sum")
        qkv_all = group_gather(qkv_piece)
        packed = list(hops)[-1]
        span = 3 * width // wide

        def qkv_columns(s, *refs):
            blocks, (keep, send) = refs[:4], refs[4:]

            def of_member(k):
                for o in range(outer):
                    for side_at in range(2):
                        cut, at = [], ((2 * o + side_at) * GROUP + k) * span
                        stop = at + span
                        while at < stop:
                            to = min(stop, (at // part + 1) * part)
                            p, m = divmod(at // part, GROUP)
                            low = p * part + at % part
                            cut.append(blocks[k ^ m][:, low : low + to - at])
                            at = to
                        found = cut[0] if len(cut) == 1 else jnp.concatenate(cut, axis=1)

                        def put(here, found=found, side_at=side_at, o=o):
                            target = keep if here == side_at else send
                            target[o] = found

                        when_each(s[1], 2, put)

            when_each(s[0], GROUP, of_member)

        span_shape = shape_of((outer, half, span), BF)
        qkv_keep, qkv_send = step(
            qkv_columns, [span_shape, span_shape], [member, y], qkv_all, micros=1, mib=8, name="qkv_columns"
        )
        if outer > 1:
            qkv_keep, qkv_send = (
                Later(lambda v: lax.psum_scatter(v.astype(F32), "o", scatter_dimension=0, tiled=True).astype(BF), v)
                for v in (qkv_keep, qkv_send)
            )
        qkv_came = swap(qkv_send, "y")

        def out_last(s, *refs):
            total = refs[0][...].astype(F32)
            for ref in refs[1:-1]:
                total = total + ref[...].astype(F32)
            refs[-1][...] = total[:, :strip]

        (out_sums,) = step(out_last, [shape_of((outer, strip, part_depth), F32)], [], out_parts, micros=0.7, mib=8, name="out_last")

        def qkv_rows(s, keep, came, out):
            def put(k):
                top, bottom = (keep, came) if k == 0 else (came, keep)
                out[:half] = top[0].astype(F32)
                out[half:] = bottom[0, :rest].astype(F32)

            when_each(s[0], 2, put)

        (qkv_weight_grad,) = step(
            qkv_rows, [shape_of((part_depth, span), F32)], [y], [qkv_keep, qkv_came], micros=0.8, mib=8, name="qkv_rows"
        )
        step.run(PLAN)
        out_sums = out_sums.get()
        out_sums = out_sums[0] if outer == 1 else lax.psum_scatter(out_sums, "o", scatter_dimension=0, tiled=False)
        out_weight_grad = out_sums.T
        packed = lax.dynamic_index_in_dim(packed.get(), z[0], 0, keepdims=False)
        if outer > 1:
            packed = lax.psum(packed, "o")
        found = (
            block_out, input_grad, packed[0], packed[1], qkv_weight_grad, packed[2], packed[3], out_weight_grad,
            packed[4], packed[5], packed[6], up_weight_grad, packed[8:].reshape(hidden_depth), down_weight_grad, packed[7],
        )
        return tuple(now(v) for v in found)

    return shards


def solution(mesh):
    wide, depth = mesh.shape["wide"], mesh.shape["narrow"]
    outer = wide // 8
    fine = Mesh(mesh.devices.reshape(outer, 2, 2, 2, depth), AXES)
    rows, vec, mat = P(AXES, None), P("z"), P("z", None)
    placed = (
        rows, P(AXES), vec, vec, mat, vec, vec, mat, vec, vec, vec, mat, vec, mat, vec, rows,
    )
    grad = P("z", WIDE)
    return jax.shard_map(
        build(outer, depth),
        mesh=fine,
        in_specs=placed,
        out_specs=(rows, rows, vec, vec, grad, vec, vec, grad, vec, vec, vec, grad, vec, grad, vec),
        check_vma=False,
    )
```

```python
import functools

import jax
import jax.numpy as jnp
from jax import lax
from jax.experimental import pallas as pl
from jax.experimental.pallas import tpu as pltpu
from jax.sharding import Mesh, PartitionSpec as P

HEADS = 20
EPSILON = 1e-05
FILL = -1000000000.0
BF = jnp.bfloat16
F32 = jnp.float32
AXES = ("o", "y", "x", "c", "z")
WIDE = ("o", "y", "x", "c")
SWAP = [(0, 1), (1, 0)]
GROUP = 4
MIB = 1024 * 1024
PER_MICRO = 5e8
PLAN = (
    (1, 2, 0),
    (0, 1.6, 0),
    (2, 0.037, 0),
    (4, 1.5, 0),
    (3, 0.15, 0),
    (5, 0.315, 1),
    (6, 0.315, 0),
    (7, 0.36, 4),
    (8, 0.1, 1),
    (9, 0.45, 0),
    (10, 2.7, 0),
    (11, 4.5, 1),
    (12, 3, 0),
    (14, 0.1, 0),
    (15, 5.4, 0),
    (13, 4, 1),
    (16, 25, 0),
    (17, 32, 0),
    (20, 32, 0),
    (19, 0.525, 0),
    (18, 8, 0),
    (26, 4, 0),
    (21, 2, 0),
    (22, 0.25, 0),
    (23, 18, 0),
    (25, 0.3, 1),
    (24, 1, 0),
    (27, 9, 0),
    (29, 2, 0),
    (31, 0.02, 0),
    (30, 0.75, 0),
    (28, 2.52, 0),
    (32, 14.4, 0),
    (33, 7.2, 0),
    (34, 0.08, 0),
    (35, 32, 0),
    (36, 3.6, 0),
    (37, 0.6, 0),
    (39, 1, 0),
    (38, 2.2, 0),
    (40, 16, 0),
    (41, 11.6, 0),
    (42, 2, 0),
    (43, 0.35, 0),
    (44, 2.8, 0),
    (48, 32, 0),
    (47, 0.175, 0),
    (45, 0.35, 0),
    (46, 0.063, 0),
    (49, 10.08, 0),
)


class Later:
    def __init__(self, function, *values):
        self.function, self.values, self.found = function, values, None

    def get(self):
        if self.found is None:
            self.found = self.function(*(now(v) for v in self.values))
        return self.found

    def __getitem__(self, key):
        return Later(lambda v: v[key], self)


def now(value):
    return value.get() if isinstance(value, Later) else value


def send(value, axis, pairs):
    return Later(lambda v: lax.ppermute(v, axis, pairs), value)


def swap(value, axis):
    return send(value, axis, SWAP)


def dot(first, second):
    return jnp.dot(first, second, preferred_element_type=F32)


def dot_left(first, second):
    return lax.dot_general(first, second, (((0,), (0,)), ((), ())), preferred_element_type=F32)


def dot_right(first, second):
    return lax.dot_general(first, second, (((1,), (1,)), ((), ())), preferred_element_type=F32)


def shape_of(dims, dtype):
    return jax.ShapeDtypeStruct(dims, dtype)


class Order:
    def __init__(self):
        self.steps = []

    def __call__(self, body, outs, scalars, arrays, after=(), pins=-1, scratch=(), mib=18, micros=1.0, name=None):
        given = {}
        self.steps.append((body, outs, scalars, arrays, list(after), scratch, mib, micros, name, given, pins))
        return [Later(lambda k=k: given[k]) for k in range(len(outs))]

    def run(self, plan):
        if len(plan) != len(self.steps):
            plan = [(k, entry[7], entry[10]) for k, entry in enumerate(self.steps)]
        token = []
        for k, micros, pins in plan:
            body, outs, scalars, arrays, after, scratch, mib, _, name, given, _ = self.steps[k]
            after = [v for bit, v in enumerate(after) if pins >> bit & 1]
            *found, last = call_step(body, outs, scalars, arrays, after + token, scratch, mib, micros, name)
            token = [last]
            given.update(enumerate(found))


def call_step(body, outs, scalars, arrays, after, scratch, mib, micros, name):
    n_scalar, n_array, n_out = len(scalars), len(arrays), len(outs)

    def run(*refs):
        token = refs[n_scalar + n_array + len(after) + n_out]
        values = tuple(ref[0] for ref in refs[:n_scalar])
        rest = refs[n_scalar + n_array + len(after) :]
        token[...] = jnp.zeros(token.shape, F32)
        body(values, *refs[n_scalar : n_scalar + n_array], *rest[:n_out], *rest[n_out + 1 :])

    return pl.pallas_call(
        run,
        out_shape=(*outs, shape_of((8, 128), F32)),
        in_specs=[pl.BlockSpec(memory_space=pltpu.SMEM)] * n_scalar
        + [pl.BlockSpec(memory_space=pltpu.VMEM)] * n_array
        + [pl.BlockSpec(memory_space=pl.ANY)] * len(after),
        out_specs=(pl.BlockSpec(memory_space=pltpu.VMEM),) * (n_out + 1),
        scratch_shapes=list(scratch),
        compiler_params=pltpu.CompilerParams(vmem_limit_bytes=mib * MIB),
        cost_estimate=pl.CostEstimate(flops=int(micros * PER_MICRO), bytes_accessed=1024, transcendentals=0),
        name=name,
    )(*(now(v) for v in (*scalars, *arrays, *after)))


def group_gather(value):
    over_x = swap(value, "x")
    over_core = swap(value, "c")
    return [value, over_core, over_x, swap(over_x, "c")]


def depth_shift(value, shift, count):
    return send(value, "z", [(i, (i + shift) % count) for i in range(count)])


def depth_line(value, count):
    up, down = [], []
    for s in range(count - 1):
        up.append(send(up[-1] if s else value, "z", [(i, i + 1) for i in range(s, count - 1)]))
        down.append(send(down[-1] if s else value, "z", [(i, i - 1) for i in range(1, count - s)]))
    return up, down


def next_block(z, step, count):
    return z + 1 + step if step < count - 1 - z else count - 2 - step


def line_ref(z, other, up, down):
    return up[z - 1 - other] if other < z else down[other - z - 1]


def depth_exchange(parts):
    return Later(lambda v: lax.all_to_all(v, "z", 0, 0), parts)


def sum_of(refs):
    total = refs[0].astype(F32)
    for k in range(1, refs.shape[0]):
        total = total + refs[k].astype(F32)
    return total


def normal(values):
    center = values - jnp.mean(values, axis=-1, keepdims=True)
    spread = jnp.mean(center * center, axis=-1, keepdims=True)
    inverse = lax.rsqrt(spread + EPSILON)
    return center * inverse, inverse


def normal_back(grad, unit, inverse):
    return (
        grad
        - jnp.mean(grad, axis=-1, keepdims=True)
        - unit * jnp.mean(grad * unit, axis=-1, keepdims=True)
    ) * inverse


def when_each(index, count, step):
    for k in range(count):
        pl.when(index == k)(functools.partial(step, k))


def allowed_of(rows, length):
    query = lax.broadcasted_iota(jnp.int32, (rows, rows), 0)
    key = lax.broadcasted_iota(jnp.int32, (rows, rows), 1)
    return (key <= query) & (key < length)


def length_of(payload, rows):
    high = payload[rows : rows + 1, 0:1].astype(F32)
    low = payload[rows : rows + 1, 128:129].astype(F32)
    return (high * 16.0 + low).astype(jnp.int32)


def head_probs(query, key, allowed, scale):
    scores = jnp.where(allowed, dot_right(query, key) * scale, FILL)
    weights = jnp.exp(scores - jnp.max(scores, axis=1, keepdims=True))
    return weights * (1.0 / jnp.sum(weights, axis=1, keepdims=True))


def attend(heads, tokens, full, vectors, query_shift, value_shift, normed, joined, contexts):
    rows, part = normed.shape[1], full.shape[1] // 3
    head = part // heads
    scale = head ** (-0.5)
    for n, x in enumerate(tokens):
        normed[n] = (normal(x[:rows].astype(F32))[0] * vectors[0:1] + vectors[1:2]).astype(BF)
        sums = dot(normed[n], full[...])
        query = (sums[:, :part] + query_shift[...]).astype(BF)
        key = sums[:, part : 2 * part].astype(BF)
        value = (sums[:, 2 * part :] + value_shift[...]).astype(BF)
        joined[n, :, :part] = query
        joined[n, :, part : 2 * part] = key
        joined[n, :, 2 * part :] = value
        allowed = allowed_of(rows, length_of(x, rows))
        out = []
        for h in range(heads):
            cut = slice(h * head, (h + 1) * head)
            probs = head_probs(query[:, cut], key[:, cut], allowed, scale).astype(BF)
            out.append(dot(probs, value[:, cut]))
        contexts[n][...] = jnp.concatenate(out, axis=1).astype(BF)


def attend_back(chosen, head, length, joined, above, out):
    rows, part = above.shape
    scale = head ** (-0.5)
    allowed = allowed_of(rows, length)
    found = ([], [], [])
    for h in chosen:
        q, k, v = (joined[:, p * part + h * head : p * part + (h + 1) * head] for p in range(3))
        g = above[:, h * head : (h + 1) * head]
        probs = head_probs(q, k, allowed, scale)
        probs_grad = dot_right(g, v)
        found[2].append(dot_left(probs.astype(BF), g))
        score = probs * (probs_grad - jnp.sum(probs * probs_grad, axis=1, keepdims=True))
        score = score.astype(BF)
        found[0].append(dot(score, k) * scale)
        found[1].append(dot_left(score, q) * scale)
    out[...] = jnp.concatenate(found[0] + found[1] + found[2], axis=1).astype(BF)


def gelu_both(values):
    root = (2.0 / jnp.pi) ** 0.5
    square = values * values
    bend = jnp.tanh(root * (values + 0.044715 * (square * values)))
    half = 0.5 * (1.0 + bend)
    slope = half + 0.5 * values * (1.0 - bend * bend) * (root * (1.0 + 3.0 * 0.044715 * square))
    return values * half, slope


def column_sum(values):
    return jnp.sum(values, axis=0, keepdims=True)


def build(outer, depth):
    def shards(
        tokens, lengths, norm1_gain, norm1_bias, qkv_weight, query_bias, value_bias, out_weight,
        out_bias, norm2_gain, norm2_bias, up_weight, up_bias, down_weight, down_bias, cotangent,
    ):
        rows, width = tokens.shape
        heads = HEADS // GROUP
        part = width // GROUP
        part_depth = width // depth
        hidden_depth = up_weight.shape[1] // depth
        block = hidden_depth // GROUP
        mine = depth * block
        wide = outer * 2 * GROUP
        sides = outer * 2
        y, x, c, z = (lax.axis_index(name).astype(jnp.int32).reshape(1) for name in ("y", "x", "c", "z"))
        member = 2 * x + c
        others = range(1, depth)
        step = Order()

        row_low, row_full = shape_of((rows, width), BF), shape_of((rows, width), F32)
        row_pair = shape_of((2, rows, width), BF)
        row_sum = shape_of((1, width), F32)
        cell, pair = shape_of((rows, part), BF), shape_of((2, rows, part), BF)

        def take_rows(s, values, out):
            out[:rows] = values[...]
            lane = lax.broadcasted_iota(jnp.int32, (16, width), 1)
            out[rows:] = jnp.where(lane < 128, s[0] // 16, s[0] % 16).astype(F32).astype(BF)

        (tokens_low,) = step(
            take_rows, [shape_of((rows + 16, width), BF)], [lengths], [tokens], micros=0.8, mib=10, name="take_rows"
        )
        tokens_all = group_gather(tokens_low)

        half = (part_depth // 2 + 15) // 16 * 16
        rest = part_depth - half
        quad_shape, half_shape = shape_of((part_depth, 4 * part), BF), shape_of((half, 4 * part), BF)
        biases = (norm1_gain, norm1_bias, query_bias, value_bias, out_bias, norm2_gain, norm2_bias, down_bias, up_bias)

        def take_quad(s, qkv, out, own, send):
            def columns(k):
                for p in range(3):
                    at = (p * GROUP + k) * part
                    own[:, p * part : (p + 1) * part] = qkv[:, at : at + part]
                own[:, 3 * part :] = out[:, k * part : (k + 1) * part]

            when_each(s[0], GROUP, columns)

            @pl.when(s[1] == 0)
            def _():
                send[...] = own[:half]

            @pl.when(s[1] == 1)
            def _():
                send[:rest] = own[half:]
                send[rest:] = jnp.zeros((half - rest, 4 * part), BF)

        quad_own, quad_half = step(
            take_quad, [quad_shape, half_shape], [member, y], [qkv_weight, out_weight], micros=0.5, mib=12, name="take_quad"
        )
        quad_up, quad_down = depth_line(quad_half, depth)

        def take_vectors(s, *refs):
            found = [ref[...].astype(F32).reshape(1, part_depth) for ref in refs[:8]]
            more = [refs[8][k * block : (k + 1) * block].astype(F32).reshape(1, block) for k in range(GROUP)]
            refs[9][...] = jnp.zeros(refs[9].shape, F32)
            refs[9][:8, :part_depth] = jnp.concatenate(found, axis=0)
            refs[9][:GROUP, part_depth : 2 * part_depth] = jnp.concatenate(more, axis=0)

        (lines_own,) = step(
            take_vectors, [shape_of((8, 2 * part_depth), F32)], [], biases, micros=0.5, mib=8, name="take_vectors"
        )
        lines_all = [lines_own] + [depth_shift(lines_own, r, depth) for r in others]

        def live(s, values, low, sums):
            keep = (lax.broadcasted_iota(jnp.int32, (rows, 1), 0) < s[0]).astype(F32)
            kept = values[...].astype(F32) * keep
            low[...] = kept.astype(BF)
            sums[...] = column_sum(kept)

        grad_low, down_sum = step(live, [row_low, row_sum], [lengths], [cotangent], micros=0.5, mib=10, name="live")
        grad_all = group_gather(grad_low)

        def hand_on(up, down, like, after=False):
            came = []
            for s_at in others:

                def choose_block(s, *refs, at=s_at - 1):
                    ups, downs, out = refs[: at + 1], refs[at + 1 : -1], refs[-1]

                    def copy(k):
                        out[...] = line_ref(k, next_block(k, at, depth), ups, downs)[...]

                    when_each(s[0], depth, copy)

                (block_now,) = step(
                    choose_block, [like], [z], [*up[:s_at], *down[:s_at]], after=came[-1:], pins=int(after), micros=1.5, mib=8, name="hand_on"
                )
                came.append(swap(block_now, "y"))
                yield came

        quad_far = list(hand_on(quad_up, quad_down, half_shape))[-1]

        turn_shape = shape_of((part_depth, mine), BF)

        def take_mlp(s, up, down, up_own, turn):
            def part_of(k):
                for n in range(depth):
                    at = n * hidden_depth + k * block
                    up_own[:, n * block : (n + 1) * block] = up[:, at : at + block]

                @pl.when(s[1] == 1)
                def _():
                    turn[...] = down[k * block : (k + 1) * block]

            when_each(s[0], GROUP, part_of)

            @pl.when(s[1] == 0)
            def _():
                turn[...] = up_own[...]

        up_own, turn = step(
            take_mlp, [turn_shape, turn_shape], [member, y], [up_weight, down_weight], after=[quad_up[-1], quad_down[-1], *quad_far], pins=3, micros=1.2, mib=20,
            name="take_mlp",
        )
        mlp_up, mlp_down = depth_line(turn, depth)
        mlp_far_steps = hand_on(mlp_up, mlp_down, turn_shape, True)

        lines = depth - 1

        def assemble(s, own, *refs):
            blocks, refs = refs[:depth], refs[depth:]
            ups, downs, handed = refs[:lines], refs[lines : 2 * lines], refs[2 * lines : 3 * lines]
            full, out_cols, whole, query_shift, value_shift, up_shift = refs[3 * lines :]

            def put_vectors(at, values):
                whole[:, at * part_depth : (at + 1) * part_depth] = values[:, :part_depth]

                def of_member(m):
                    up_shift[:, at * block : (at + 1) * block] = values[m : m + 1, part_depth : 2 * part_depth]

                when_each(s[2], GROUP, of_member)

            def put(k):
                full[k * part_depth : (k + 1) * part_depth] = own[:, : 3 * part]
                out_cols[:, k * part : (k + 1) * part] = own[:, 3 * part :]
                for r in range(depth):
                    put_vectors((k - r) % depth, blocks[r][...])
                for at in range(lines):
                    other = next_block(k, at, depth)
                    low, cols = other * part_depth, slice(other * part, (other + 1) * part)

                    def both(side, at=at, low=low, cols=cols, other=other):
                        ours = line_ref(k, other, ups, downs)
                        top, bottom = (ours, handed[at]) if side == 0 else (handed[at], ours)
                        full[low : low + half] = top[:, : 3 * part]
                        full[low + half : low + part_depth] = bottom[:rest, : 3 * part]
                        out_cols[:half, cols] = top[:, 3 * part :]
                        out_cols[half:, cols] = bottom[:rest, 3 * part :]

                    when_each(s[1], 2, both)

            when_each(s[0], depth, put)

            def of_member(m):
                query_shift[...] = whole[2:3, m * part : (m + 1) * part]
                value_shift[...] = whole[3:4, m * part : (m + 1) * part]

            when_each(s[2], GROUP, of_member)

        shift_shape = shape_of((1, part), F32)
        qkv_full, out_part, whole, query_shift, value_shift, up_shift = step(
            assemble,
            [shape_of((width, 3 * part), BF), shape_of((part_depth, depth * part), BF), shape_of((8, width), F32), shift_shape,
             shift_shape, shape_of((1, mine), F32)],
            [z, y, member],
            [quad_own, *lines_all, *quad_up, *quad_down, *quad_far],
            after=[grad_all[2], grad_all[3], grad_all[1]],
            pins=1,
            micros=1.3, mib=16, name="assemble",
        )
        out_all = group_gather(out_part)
        next(mlp_far_steps)


        def attend_far(s, full, vector, first, second, shift_q, shift_v, normed, joined, context):
            attend(heads, (first, second), full, vector, shift_q, shift_v, normed, joined,
                   (context.at[0], context.at[1]))

        joined_shape = shape_of((2, rows, 3 * part), BF)
        normed_far, joined_far, context_far = step(
            attend_far,
            [row_pair, joined_shape, pair],
            [],
            [qkv_full, whole, tokens_all[2], tokens_all[3], query_shift, value_shift],
            micros=9, mib=20, name="attend_far",
        )
        came_far = swap(context_far, "x")
        next(mlp_far_steps)

        def attend_near(s, full, vector, first, second, shift_q, shift_v, normed, joined, ours, theirs):
            attend(heads, (first, second), full, vector, shift_q, shift_v, normed, joined,
                   (ours, theirs))

        normed_near, joined_near, context_own, context_core = step(
            attend_near,
            [row_pair, joined_shape, cell, cell],
            [],
            [qkv_full, whole, tokens_all[0], tokens_all[1], query_shift, value_shift],
            micros=9, mib=20, name="attend_near",
        )
        came_core = swap(context_core, "c")
        came_last = swap(came_far[1], "c")

        mlp_far = list(mlp_far_steps)[-1]

        def out_whole(s, *refs):
            blocks, full = refs[:-1], refs[-1]

            def put(k):
                for other in range(GROUP):
                    at = (k ^ other) * part
                    for n in range(depth):
                        rows_of = slice(n * part_depth, (n + 1) * part_depth)
                        full[rows_of, at : at + part] = blocks[other][:, n * part : (n + 1) * part]

            when_each(s[0], GROUP, put)

        (out_full,) = step(out_whole, [shape_of((width, width), BF)], [member], out_all, micros=1, mib=12, name="out_whole")

        def project(s, own, core, far_pair, last, full, values, vector, context, middle, normed):
            def put(k):
                for other, ref in enumerate((own, core, None, last)):
                    at = (k ^ other) * part
                    context[:, at : at + part] = far_pair[0] if ref is None else ref[...]

            when_each(s[0], GROUP, put)
            total = values[...].astype(F32) + (dot(context[...], full[...]) + vector[4:5])
            middle[...] = total
            normed[...] = (normal(total)[0] * vector[5:6] + vector[6:7]).astype(BF)

        context, middle, normed_two = step(
            project,
            [row_low, row_full, row_low],
            [member],
            [context_own, came_core, came_far, came_last, out_full, tokens, whole],
            micros=3.6, mib=20, name="project",
        )
        normed_two_all = group_gather(normed_two)

        def feed_cells(cells, normed, grads, up_full, down_full, shift, active, before, sums, two_low, two):
            total = jnp.zeros((1, mine), F32)
            for k in cells:
                at = slice(k * rows, (k + 1) * rows)
                value, slope = gelu_both(dot(normed[k][...], up_full[...]) + shift[...])
                active[at] = value.astype(BF)
                grad = (dot_right(grads[k][...], down_full[...]) * slope).astype(BF)
                before[at] = grad
                total = total + column_sum(grad.astype(F32))
                found = dot_right(grad, up_full[...])
                if k == 0:
                    two[...] = found
                else:
                    two_low[...] = found.astype(BF)
            sums[...] = total

        def feed_near(s, up_ref, down_ref, *refs):
            ups, downs, handed = refs[:lines], refs[lines : 2 * lines], refs[2 * lines : 3 * lines]
            refs = refs[3 * lines :]
            normed, grads, shift, (up_full, down_full, *outs) = refs[:2], refs[2:4], refs[4], refs[5:]

            def put(k):
                up_full[k * part_depth : (k + 1) * part_depth] = up_ref[...]

                def of_member(m):
                    down_full[k * block : (k + 1) * block] = down_ref[m * block : (m + 1) * block]

                when_each(s[2], GROUP, of_member)
                for at in range(lines):
                    other = next_block(k, at, depth)

                    def both(side, at=at, other=other):
                        ours = line_ref(k, other, ups, downs)
                        up_from, down_from = (ours, handed[at]) if side == 0 else (handed[at], ours)
                        up_full[other * part_depth : (other + 1) * part_depth] = up_from[...]
                        down_full[other * block : (other + 1) * block] = down_from[...]

                    when_each(s[1], 2, both)

            when_each(s[0], depth, put)
            feed_cells((1, 0), normed, grads, up_full, down_full, shift, *outs)

        hidden_rows, hidden_sum = shape_of((2 * rows, mine), BF), shape_of((1, mine), F32)
        up_full, down_full, active_near, before_near, up_sums_near, two_core, two_own = step(
            feed_near,
            [shape_of((width, mine), BF), shape_of((mine, width), BF), hidden_rows, hidden_rows, hidden_sum, row_low, row_full],
            [z, y, member],
            [up_own, down_weight, *mlp_up, *mlp_down, *mlp_far, *normed_two_all[:2], *grad_all[:2], up_shift],
            mib=34,
            micros=12.5, name="feed_near",
        )
        two_came = swap(two_core, "c")

        def feed_far(s, up_full, down_full, *refs):
            feed_cells((1, 0), refs[:2], refs[2:4], up_full, down_full, *refs[4:])

        active_far, before_far, up_sums_far, two_next, two_far = step(
            feed_far,
            [hidden_rows, hidden_rows, hidden_sum, row_low, row_full],
            [],
            [up_full, down_full, *normed_two_all[2:], *grad_all[2:], up_shift],
            mib=28,
            micros=10.5, name="feed_far",
        )
        next_came = swap(two_next, "c")
        active, before = [active_near, active_far], [before_near, before_far]

        each, side = mine // sides, width // sides

        def columns_for(value, count, index):
            cut = [value[:, (2 * o + index) * count : (2 * o + index + 1) * count] for o in range(outer)]
            return cut[0] if outer == 1 else jnp.concatenate(cut, axis=1)

        tall = max(block, part_depth)
        fold_rows = (tall // 2 + 15) // 16 * 16
        fold_rest = tall - fold_rows
        pack_shape = shape_of((depth, fold_rows, 2 * outer * each), BF)
        feed_scratch = [pltpu.VMEM((GROUP * rows, width), BF), pltpu.VMEM((GROUP * rows, outer * each), BF)]

        def store_rows(total, came, out):
            cut = total.shape[1]
            for n in range(depth):
                top = total[n * tall : n * tall + fold_rows]
                low = total[n * tall + fold_rows : (n + 1) * tall]
                if came is not None:
                    top = top + came[n, :, :cut].astype(F32)
                    low = low + came[n, :fold_rest, cut:].astype(F32)
                out[n, :, :cut] = top.astype(BF)
                out[n, :fold_rest, cut:] = low.astype(BF)
                out[n, fold_rest:, cut:] = jnp.zeros((fold_rows - fold_rest, cut), BF)

        def down_product(grads, right_all, index):
            for k, ref in enumerate(grads):
                right_all[k * rows : (k + 1) * rows] = columns_for(ref[...], side, index)

        def up_product(befores, right_all, index):
            for k, ref in enumerate(befores):
                right_all[2 * k * rows : 2 * (k + 1) * rows] = columns_for(ref[...], each, index)

        def feed_part(product, arrays, scratch, came, name, after=()):
            n_array, n_came = len(arrays), len(came)

            def body(s, *refs):
                inputs, came_refs, (out, *left_refs, right_all) = (
                    refs[:n_array], refs[n_array : n_array + n_came], refs[n_array + n_came :]
                )
                when_each(s[0], 2, lambda k: product(inputs, right_all, k if n_came else 1 - k))
                if left_refs:
                    for k in range(GROUP):
                        left_refs[0][k * rows : (k + 1) * rows] = inputs[2 + k][...]
                    total = dot_left(left_refs[0][...], right_all[...])
                else:
                    total = dot_left(inputs[0][...], right_all[: 2 * rows]) + dot_left(inputs[1][...], right_all[2 * rows :])
                store_rows(total, came_refs[0] if n_came else None, out)

            return step(
                body, [pack_shape], [y], [*arrays, *came], after=after, scratch=scratch, mib=26, micros=4, name=name
            )[0]

        def down_part(came, name, after=()):
            return feed_part(
                lambda refs, right, k: down_product(refs[2:], right, k),
                [*active, *grad_all], feed_scratch[1:], came, name, after,
            )

        def up_part(came, name, after=()):
            return feed_part(
                lambda refs, right, k: up_product(refs[:2], right, k),
                [*before, *normed_two_all], feed_scratch, came, name, after,
            )

        down_came = swap(down_part([], "down_send"), "y")

        def add_far(s, far, came, out):
            out[...] = (far[...] + came[1].astype(F32)).astype(BF)

        def add_two(s, far, came, out):
            out[...] = (far[...] + came[...].astype(F32)).astype(BF)

        (two_sent,) = step(add_two, [row_low], [], [two_far, next_came], micros=0.7, mib=10, name="add_two")
        two_last = swap(two_sent, "x")

        def feed_out(s, near_ref, far_ref, full, own, core, far_out):
            for k in range(GROUP):
                value = dot((near_ref, far_ref)[k // 2][k % 2 * rows : (k % 2 + 1) * rows], full[...])
                if k == 0:
                    own[...] = value
                elif k == 2:
                    far_out[...] = value
                else:
                    core[k // 2] = value.astype(BF)

        mlp_own, mlp_core, mlp_away = step(
            feed_out, [row_full, row_pair, row_full], [], [*active, down_full], micros=4.5, mib=24, name="feed_out",
        )
        mlp_came = swap(mlp_core, "c")

        def turn_back(
            s, own, came, last, values, grads, vector, full,
            middle_grad, low, ours, core, far_pair, gain_sum, shift_sum, out_sum,
        ):
            two = own[...] + came[...].astype(F32) + last[...].astype(F32)
            unit, inverse = normal(values[...])
            gain_sum[...] = column_sum(two * unit)
            shift_sum[...] = column_sum(two)
            total = grads[...].astype(F32) + normal_back(two * vector[5:6], unit, inverse)
            middle_grad[...] = total
            low[...] = total.astype(BF)
            out_sum[...] = column_sum(total.astype(BF).astype(F32))
            grad = dot_right(low[...], full[...]).astype(BF)

            def split(k):
                for other in range(GROUP):
                    at = (k ^ other) * part
                    piece = grad[:, at : at + part]
                    if other == 0:
                        ours[...] = piece
                    elif other == 1:
                        core[...] = piece
                    else:
                        far_pair[other - 2] = piece

            when_each(s[0], GROUP, split)

        middle_grad, middle_low, grad_own, grad_core, grad_far, gain_two_sum, shift_two_sum, out_sum = step(
            turn_back,
            [row_full, row_low, cell, cell, pair, row_sum, row_sum, row_sum],
            [member],
            [two_own, two_came, two_last, middle, grad_low, whole, out_full],
            micros=3.2, mib=24, name="turn_back",
        )
        back_far = swap(grad_far, "x")
        back_core = swap(grad_core, "c")
        back_last = swap(back_far[1], "c")

        strip = width // wide
        padded = (strip + 15) // 16 * 16

        def out_grad(s, low, values, send, keep):
            total = dot_left(low[...], values[...])

            def split(k):
                for q in range(wide // 2):
                    for core in range(2):
                        target = keep if core == k else send
                        at = (2 * q + core) * strip
                        target[q, :strip] = total[at : at + strip].astype(BF)
                        target[q, strip:] = jnp.zeros((padded - strip, width), BF)

            when_each(s[0], 2, split)

        out_shape = shape_of((wide // 2, padded, width), BF)
        out_send, out_keep = step(
            out_grad, [out_shape, out_shape], [c], [middle_low, context], micros=2, mib=20, name="out_grad"
        )
        out_came = swap(out_send, "c")

        def out_fold(flag, keep, came, count):
            span = 1

            def body(s, kept, arrived, send, keep_out):
                def split(k):
                    for q in range(count):
                        at = q // span * 2 * span + q % span
                        for bit in range(2):
                            target = keep_out if bit == k else send
                            source = at + bit * span
                            target[q] = (kept[source].astype(F32) + arrived[source].astype(F32)).astype(BF)

                when_each(s[0], 2, split)

            out = shape_of((count, padded, width), BF)
            return step(body, [out, out], [flag], [keep, came], micros=1.4, mib=16, name="out_fold")

        head = part // heads

        def attend_back_pair(joined, first, second, lows, name):
            def body(s, source, one, two, low_one, low_two, out):
                for k, (above, low) in enumerate(((one.at[0] if len(one.shape) == 3 else one, low_one), (two, low_two))):
                    attend_back(range(heads), head, length_of(low, rows), source.at[k], above, out.at[k])

            return step(
                body, [joined_shape], [], [joined, first, second, *lows], micros=3.6 * heads / 2, name=name
            )[0]

        joined_grad_near = attend_back_pair(joined_near, grad_own, back_core, tokens_all[:2], "attend_back_near")
        (mlp_sent,) = step(add_far, [row_low], [], [mlp_away, mlp_came], micros=1, mib=10, name="add_mlp")
        mlp_last = swap(mlp_sent, "x")
        down_parts = depth_exchange(down_part([down_came], "down_keep", [back_far]))
        up_came = swap(up_part([], "up_send"), "y")
        joined_grad_far = attend_back_pair(joined_far, back_far, back_last, tokens_all[2:], "attend_back_far")
        out_send, out_keep = out_fold(x, out_keep, out_came, wide // 4)
        out_came = swap(out_send, "x")

        def qkv_grad(s, near_ref, far_ref, grad_near, grad_far, send, keep, sums):
            tall = 2 * rows
            grads = [ref[...].reshape(tall, 3 * part) for ref in (grad_near, grad_far)]
            sums[...] = column_sum(grads[0].astype(F32)) + column_sum(grads[1].astype(F32))
            total = dot_left(near_ref[...].reshape(tall, width), grads[0])
            total = total + dot_left(far_ref[...].reshape(tall, width), grads[1])

            def split(k):
                first_half, second_half = (keep, send) if k == 0 else (send, keep)
                for n in range(depth):
                    at = n * part_depth
                    first_half[n] = total[at : at + half].astype(BF)
                    second_half[n, :rest] = total[at + half : at + part_depth].astype(BF)
                    second_half[n, rest:] = jnp.zeros((half - rest, 3 * part), BF)

            when_each(s[0], 2, split)

        halves = shape_of((depth, half, 3 * part), BF)
        qkv_send, qkv_keep, joined_sums = step(
            qkv_grad,
            [halves, halves, shape_of((1, 3 * part), F32)],
            [y],
            [normed_near, normed_far, joined_grad_near, joined_grad_far],
            mib=26,
            micros=4.5,
            name="qkv_grad",
        )
        qkv_came = swap(qkv_send, "y")

        def one_back(s, near_ref, far_ref, full, own, core, far_out):
            for k in range(GROUP):
                value = dot_right((near_ref, far_ref)[k // 2][k % 2], full[...])
                if k == 0:
                    own[...] = value
                elif k == 2:
                    far_out[...] = value
                else:
                    core[k // 2] = value.astype(BF)

        one_own, one_core, one_far = step(
            one_back, [row_full, row_pair, row_full], [], [joined_grad_near, joined_grad_far, qkv_full], micros=4.7, mib=24, name="one_back",
        )
        one_came = swap(one_core, "c")
        def leave(s, own, came, last, values, vector, out):
            keep = (lax.broadcasted_iota(jnp.int32, (rows, 1), 0) < s[0]).astype(F32)
            fed = own[...] + came[0].astype(F32) + last[...].astype(F32) + vector[7:8]
            out[...] = (keep * (values[...] + fed)).astype(BF)

        (block_out,) = step(
            leave, [row_low], [lengths], [mlp_own, mlp_came, mlp_last, middle, whole], micros=2.5, mib=14, name="leave"
        )

        up_parts = depth_exchange(up_part([up_came], "up_keep"))
        (one_sent,) = step(add_far, [row_low], [], [one_far, one_came], micros=0.7, mib=10, name="add_one")
        one_last = swap(one_sent, "x")

        out_send, out_keep = out_fold(y, out_keep, out_came, wide // 8)
        out_came = swap(out_send, "y")

        def qkv_fold(s, keep, came, out):
            for n in range(depth):
                out[n] = (keep[n].astype(F32) + came[n].astype(F32)).astype(BF)

        (qkv_parts,) = step(qkv_fold, [halves], [], [qkv_keep, qkv_came], micros=1.2, mib=12, name="qkv_fold")
        qkv_parts = depth_exchange(qkv_parts)

        def finish(s, own, came, last, values, vector, middle_ref, out, gain_sum, shift_sum):
            one = own[...] + came[0].astype(F32) + last[...].astype(F32)
            unit, inverse = normal(values[...].astype(F32))
            gain_sum[...] = column_sum(one * unit)
            shift_sum[...] = column_sum(one)
            out[...] = middle_ref[...] + normal_back(one * vector[0:1], unit, inverse)

        input_grad, gain_one_sum, shift_one_sum = step(
            finish, [row_full, row_sum, row_sum], [],
            [one_own, one_came, one_last, tokens, whole, middle_grad], micros=3.6, mib=16, name="finish",
        )

        def vector_pack(s, gain_one, shift_one, out_ref, gain_two, shift_two, down_ref, up_ref, up_more, joined, packed, line):
            packed[...] = jnp.zeros(packed.shape, F32)
            line[...] = jnp.zeros(line.shape, F32)
            for k, ref in ((0, gain_one), (1, shift_one), (4, out_ref), (5, gain_two), (6, shift_two), (7, down_ref)):
                line[k : k + 1] = ref[...]

            def of_member(m):
                line[2:3, m * part : (m + 1) * part] = joined[:, :part]
                line[3:4, m * part : (m + 1) * part] = joined[:, 2 * part :]
                for n in range(depth):
                    cols = slice(n * block, (n + 1) * block)
                    packed[n, 8 + m : 9 + m] = up_ref[:, cols] + up_more[:, cols]

            when_each(s[0], GROUP, of_member)
            for n in range(depth):
                packed[n, :8] = line[:, n * part_depth : (n + 1) * part_depth]

        packed_shape = shape_of((depth, 8 + GROUP, part_depth), F32)
        (packed,) = step(
            vector_pack,
            [packed_shape],
            [member],
            [gain_one_sum, shift_one_sum, out_sum, gain_two_sum, shift_two_sum, down_sum, up_sums_near, up_sums_far,
             joined_sums],
            scratch=[pltpu.VMEM((8, width), F32)],
            micros=0.6, mib=8, name="vector_pack",
        )

        def vector_hops(packed):
            def add(s, one, two, out):
                out[...] = one[...] + two[...]

            spans = [1 << k for k in range(depth.bit_length() - 1)]
            hops = ["c", "x", "y", *spans]
            for k, hop in enumerate(hops):
                if isinstance(hop, str):
                    came = swap(packed, hop)
                else:
                    came = send(packed, "z", [(i, i ^ hop) for i in range(depth)])
                yield packed
                (packed,) = step(add, [packed_shape], [], [packed, came], micros=0.5, mib=8, name="vector_add")
            yield packed

        hops = vector_hops(packed)
        next(hops)

        low_type = BF if outer == 1 else F32

        def feed_pieces(s, down_ref, up_ref, out):
            out[0] = sum_of(down_ref).astype(low_type)
            out[1] = sum_of(up_ref).astype(low_type)

        (feed_piece,) = step(
            feed_pieces, [shape_of((2, fold_rows, 2 * outer * each), low_type)], [], [down_parts, up_parts], micros=2.2,
            mib=16, name="feed_pieces",
        )
        if outer > 1:

            def over_outer(value):
                value = value.reshape(2, fold_rows, 2, outer, each)
                value = lax.psum_scatter(value, "o", scatter_dimension=3, tiled=False).astype(BF)
                return value.reshape(2, fold_rows, 2 * each)

            feed_piece = Later(over_outer, feed_piece)
        feed_all = group_gather(feed_piece)
        next(hops)

        next(hops)

        ratio = wide // depth
        fold = GROUP // ratio

        def feed_grads(s, *refs):
            blocks, (down_out, up_out) = refs[:4], refs[4:]

            def of_member(k):
                for m in range(GROUP):
                    at, to = k * (side // GROUP), m * block
                    ref, span = blocks[k ^ m], side // GROUP
                    down_out[to : to + fold_rows] = ref[0, :, at : at + span].astype(F32)
                    down_out[to + fold_rows : to + block] = ref[0, :fold_rest, side + at : side + at + span].astype(F32)
                for f in range(fold):
                    source = k % ratio * fold + f
                    at = k // ratio * block
                    ref, to = blocks[k ^ source], slice(f * block, (f + 1) * block)
                    up_out[:fold_rows, to] = ref[1, :, at : at + block].astype(F32)
                    up_out[fold_rows:, to] = ref[1, :fold_rest, each + at : each + at + block].astype(F32)

            when_each(s[0], GROUP, of_member)

        down_weight_grad, up_weight_grad = step(
            feed_grads,
            [shape_of((hidden_depth, side // GROUP), F32), shape_of((part_depth, fold * block), F32)],
            [member],
            feed_all,
            micros=2.9, mib=12, name="feed_grads",
        )

        def out_split(s, keep, came, *rest_refs):
            *outs, packed = rest_refs
            for q in range(outer):
                total = keep[q].astype(F32) + came[q].astype(F32)
                for n in range(depth):
                    packed[n, q] = total[:, n * part_depth : (n + 1) * part_depth].astype(BF)
            for r, ref in enumerate(outs):
                ref[...] = packed[lax.rem(s[0] + r, depth)]

        out_parts = step(
            out_split, [shape_of((outer, padded, part_depth), BF)] * depth, [z], [out_keep, out_came],
            scratch=[pltpu.VMEM((depth, outer, padded, part_depth), BF)], micros=1, mib=8, name="out_split",
        )
        out_parts = [out_parts[0]] + [depth_shift(out_parts[r], r, depth) for r in others]
        next(hops)

        def qkv_sum(s, parts, out):
            out[...] = sum_of(parts).astype(BF)

        (qkv_piece,) = step(qkv_sum, [shape_of((half, 3 * part), BF)], [], [qkv_parts], micros=1, mib=8, name="qkv_sum")
        qkv_all = group_gather(qkv_piece)
        packed = list(hops)[-1]
        span = 3 * width // wide

        def qkv_columns(s, *refs):
            blocks, (keep, send) = refs[:4], refs[4:]

            def of_member(k):
                for o in range(outer):
                    for side_at in range(2):
                        cut, at = [], ((2 * o + side_at) * GROUP + k) * span
                        stop = at + span
                        while at < stop:
                            to = min(stop, (at // part + 1) * part)
                            p, m = divmod(at // part, GROUP)
                            low = p * part + at % part
                            cut.append(blocks[k ^ m][:, low : low + to - at])
                            at = to
                        found = cut[0] if len(cut) == 1 else jnp.concatenate(cut, axis=1)

                        def put(here, found=found, side_at=side_at, o=o):
                            target = keep if here == side_at else send
                            target[o] = found

                        when_each(s[1], 2, put)

            when_each(s[0], GROUP, of_member)

        span_shape = shape_of((outer, half, span), BF)
        qkv_keep, qkv_send = step(
            qkv_columns, [span_shape, span_shape], [member, y], qkv_all, micros=1, mib=8, name="qkv_columns"
        )
        if outer > 1:
            qkv_keep, qkv_send = (
                Later(lambda v: lax.psum_scatter(v.astype(F32), "o", scatter_dimension=0, tiled=True).astype(BF), v)
                for v in (qkv_keep, qkv_send)
            )
        qkv_came = swap(qkv_send, "y")

        def out_last(s, *refs):
            total = refs[0][...].astype(F32)
            for ref in refs[1:-1]:
                total = total + ref[...].astype(F32)
            refs[-1][...] = total[:, :strip]

        (out_sums,) = step(out_last, [shape_of((outer, strip, part_depth), F32)], [], out_parts, micros=0.7, mib=8, name="out_last")

        def qkv_rows(s, keep, came, out):
            def put(k):
                top, bottom = (keep, came) if k == 0 else (came, keep)
                out[:half] = top[0].astype(F32)
                out[half:] = bottom[0, :rest].astype(F32)

            when_each(s[0], 2, put)

        (qkv_weight_grad,) = step(
            qkv_rows, [shape_of((part_depth, span), F32)], [y], [qkv_keep, qkv_came], micros=0.8, mib=8, name="qkv_rows"
        )
        step.run(PLAN)
        out_sums = out_sums.get()
        out_sums = out_sums[0] if outer == 1 else lax.psum_scatter(out_sums, "o", scatter_dimension=0, tiled=False)
        out_weight_grad = out_sums.T
        packed = lax.dynamic_index_in_dim(packed.get(), z[0], 0, keepdims=False)
        if outer > 1:
            packed = lax.psum(packed, "o")
        found = (
            block_out, input_grad, packed[0], packed[1], qkv_weight_grad, packed[2], packed[3], out_weight_grad,
            packed[4], packed[5], packed[6], up_weight_grad, packed[8:].reshape(hidden_depth), down_weight_grad, packed[7],
        )
        return tuple(now(v) for v in found)

    return shards


def solution(mesh):
    wide, depth = mesh.shape["wide"], mesh.shape["narrow"]
    outer = wide // 8
    fine = Mesh(mesh.devices.reshape(outer, 2, 2, 2, depth), AXES)
    rows, vec, mat = P(AXES, None), P("z"), P("z", None)
    placed = (
        rows, P(AXES), vec, vec, mat, vec, vec, mat, vec, vec, vec, mat, vec, mat, vec, rows,
    )
    grad = P("z", WIDE)
    return jax.shard_map(
        build(outer, depth),
        mesh=fine,
        in_specs=placed,
        out_specs=(rows, rows, vec, vec, grad, vec, vec, grad, vec, vec, vec, grad, vec, grad, vec),
        check_vma=False,
    )
```
